32 devices in a mesh: shard: 4 (over y, x), rep: 8 (over z, core).
Axes of the slice: x: 2, y: 2, z: 4, core: 2. Of those that a mesh axis runs over, the one named last changes fastest.
Arguments:
- tokens: bfloat16 [16384, 1024], P(('shard', 'rep')), may hold values from -6 to 6
- token_order: int32 [16384], P(('shard', 'rep')), may hold values from 0 to 16383, as said below
- lengths: int32 [128], P(('shard', 'rep')), may hold values from 0 to 512, as said below
- cotangent: bfloat16 [16384, 1024], P(('shard', 'rep')), may hold values from -6 to 6
- norm_gain: bfloat16 [2, 1024], P(None, 'shard'), may hold values from 0.5 to 1.5
- norm_shift: bfloat16 [2, 1024], P(None, 'shard'), may hold values from -3 to 3
- qkv_weight: bfloat16 [2, 1024, 3072], P(None, 'shard'), may hold values from -0.1875 to 0.1875
- qkv_bias: bfloat16 [2, 3072], P(None, 'shard'), may hold values from -3 to 3
- out_weight: bfloat16 [2, 1024, 1024], P(None, 'shard'), may hold values from -0.75 to 0.75
- out_bias: bfloat16 [2, 1024], P(None, 'shard'), may hold values from -3 to 3
- up_weight: bfloat16 [2, 1024, 4096], P(None, 'shard'), may hold values from -0.1875 to 0.1875
- up_bias: bfloat16 [2, 4096], P(None, 'shard'), may hold values from -3 to 3
- down_weight: bfloat16 [2, 4096, 1024], P(None, 'shard'), may hold values from -0.1875 to 0.1875
- down_bias: bfloat16 [2, 1024], P(None, 'shard'), may hold values from -3 to 3
Outputs:
- block_output: bfloat16 [16384, 1024], P(('shard', 'rep'))
- input_grad: bfloat16 [16384, 1024], P(('shard', 'rep'))
- norm_gain_grad: float32 [2, 1024], P(None, 'shard')
- norm_shift_grad: float32 [2, 1024], P(None, 'shard')
- qkv_weight_grad: float32 [2, 1024, 3072], P(None, 'shard')
- qkv_bias_grad: float32 [2, 3072], P(None, 'shard')
- out_weight_grad: float32 [2, 1024, 1024], P(None, 'shard')
- out_bias_grad: float32 [2, 1024], P(None, 'shard')
- up_weight_grad: float32 [2, 1024, 4096], P(None, 'shard')
- up_bias_grad: float32 [2, 4096], P(None, 'shard')
- down_weight_grad: float32 [2, 4096, 1024], P(None, 'shard')
- down_bias_grad: float32 [2, 1024], P(None, 'shard')
The draws below stay inside these ranges and needn't reach their ends.
Inputs may be any that keep to these rules, and one draw needn't show every extreme that they name: `token_order`: A permutation of the tokens that moves whole documents, keeps each document's tokens in order, and maps the 4096 tokens of each index of shard onto themselves; the dealt documents of each device are the slots given by lengths. Each device's 4 lengths sum to 512; slots may be empty; in every draw some device of each index of shard holds one document of 512 tokens.
All inputs are finite; a program needn't handle non-finite values.
Results may differ from the reference program's by a relative error of at most 0.018.
Values may be sent and summed in bfloat16 or wider, within the bound.
No kernel may reach another device: no remote copies, remote signals or barrier semaphores. Data moves between devices by JAX's collectives and lax.ppermute only.
A program may use at most 384 MiB of HBM per device.

```python
import math
from functools import partial
import jax
import jax.numpy as jnp
from jax import lax

D = 1024
FF = 4096
HEADS = 16
HEAD = 64
ROT = 16
LAYERS = 2
DOCS_DEV = 4
TOK_DEV = 512
GROUPS = 4
MEMBERS = 8
GROUP_TOK = 4096
DOCS_GROUP = 32
TOKENS = 16384


def shuffle_one(sub_key):
    return jax.random.permutation(sub_key, DOCS_GROUP)


def deal_layout(key):
    cut_key = jax.random.fold_in(key, 101)
    lone_key = jax.random.fold_in(key, 202)
    shuffle_key = jax.random.fold_in(key, 303)
    cut_points = jax.random.randint(cut_key, (GROUPS, MEMBERS, DOCS_DEV - 1), 0, TOK_DEV + 1)
    cut_points = jnp.sort(cut_points, axis=2)
    lone_member = jax.random.randint(lone_key, (GROUPS, 1, 1), 0, MEMBERS)
    member_ids = jnp.arange(MEMBERS, dtype=jnp.int32)[None, :, None]
    cut_points = jnp.where(member_ids == lone_member, TOK_DEV, cut_points)
    cut_edges = jnp.concatenate([jnp.zeros((GROUPS, MEMBERS, 1), jnp.int32), cut_points, jnp.full((GROUPS, MEMBERS, 1), TOK_DEV, jnp.int32)], axis=2)
    doc_lengths = (cut_edges[:, :, 1:] - cut_edges[:, :, :-1]).reshape(GROUPS, DOCS_GROUP).astype(jnp.int32)
    doc_ends = jnp.cumsum(doc_lengths, axis=1).astype(jnp.int32)
    doc_starts = doc_ends - doc_lengths
    shuffles = jax.vmap(shuffle_one)(jax.random.split(shuffle_key, GROUPS)).astype(jnp.int32)
    moved_lengths = jnp.take_along_axis(doc_lengths, shuffles, axis=1)
    moved_starts = jnp.cumsum(moved_lengths, axis=1).astype(jnp.int32) - moved_lengths
    group_rows = jnp.arange(GROUPS, dtype=jnp.int32)[:, None]
    home_starts = jnp.zeros((GROUPS, DOCS_GROUP), jnp.int32).at[group_rows, shuffles].set(moved_starts)
    places = jnp.arange(GROUP_TOK, dtype=jnp.int32)
    doc_index = jnp.sum((doc_ends[:, None, :] <= places[None, :, None]).astype(jnp.int32), axis=2)
    own_start = jnp.take_along_axis(doc_starts, doc_index, axis=1)
    home_start = jnp.take_along_axis(home_starts, doc_index, axis=1)
    group_base = group_rows * GROUP_TOK
    dealt_order = group_base + home_start + places[None, :] - own_start
    return (doc_lengths.reshape(-1), dealt_order.reshape(-1).astype(jnp.int32))


def draw_lengths(key, part):
    return deal_layout(key)[0]


def draw_token_order(key, part):
    return deal_layout(key)[1]


def block_scale(stream_key, extent, pieces, smallest, high):
    def one(position, blocks):
        heights = jax.random.uniform(jax.random.fold_in(jax.random.fold_in(stream_key, 6), position), (blocks,), jnp.float32, smallest / len(pieces), high / len(pieces))
        return jnp.repeat(jnp.exp(heights), extent[position] // blocks).reshape((-1,) + (1,) * (len(extent) - position - 1))

    factor_of = one(*pieces[0])
    for cut in pieces[1:]:
        factor_of = factor_of * one(*cut)
    return factor_of


def normal_values(rng, extent, spread, reach, shards=(), kind=jnp.bfloat16):
    array = spread * jax.random.normal(rng, extent, jnp.float32)
    if shards:
        array = array * block_scale(rng, extent, shards, -0.22, 0.18)
    return jnp.clip(array, -reach, reach).astype(kind)


def setup_inputs(seed: int = 0) -> dict:
    arg_keys = jax.random.split(jax.random.key(seed), 15)
    return {
        "tokens": normal_values(arg_keys[0], (TOKENS, D), 1.0, 6.0, ((0, 32),)),
        "token_order": draw_token_order(jax.random.fold_in(arg_keys[14], 71), 0),
        "lengths": draw_lengths(jax.random.fold_in(arg_keys[14], 71), 0),
        "cotangent": normal_values(arg_keys[3], (TOKENS, D), 1.0, 6.0, ((0, 32),)),
        "norm_gain": jnp.clip(1.0 + 0.1 * jax.random.normal(arg_keys[4], (LAYERS, D), jnp.float32), 0.5, 1.5).astype(jnp.bfloat16),
        "norm_shift": normal_values(arg_keys[5], (LAYERS, D), 0.5, 3.0, ((1, 4),)),
        "qkv_weight": normal_values(arg_keys[6], (LAYERS, D, 3 * D), D ** -0.5, 0.1875, ((1, 4),)),
        "qkv_bias": normal_values(arg_keys[7], (LAYERS, 3 * D), 0.5, 3.0, ((1, 4),)),
        "out_weight": normal_values(arg_keys[8], (LAYERS, D, D), (D // 16) ** -0.5, 0.75, ((1, 4),)),
        "out_bias": normal_values(arg_keys[9], (LAYERS, D), 0.5, 3.0, ((1, 4),)),
        "up_weight": normal_values(arg_keys[10], (LAYERS, D, FF), D ** -0.5, 0.1875, ((1, 4),)),
        "up_bias": normal_values(arg_keys[11], (LAYERS, FF), 0.5, 3.0, ((1, 4),)),
        "down_weight": normal_values(arg_keys[12], (LAYERS, FF, D), (FF // 4) ** -0.5, 0.1875, ((1, 4),)),
        "down_bias": normal_values(arg_keys[13], (LAYERS, D), 0.5, 3.0, ((1, 4),)),
    }


PRECISE = lax.Precision.HIGHEST
EPSILON = 1e-05
NEG_FILL = -1e+30

@jax.custom_vjp
def low(v):
    return lax.optimization_barrier(v.astype(jnp.bfloat16)).astype(jnp.float32)

@jax.custom_vjp
def low_back(v):
    return v

def low_keep(v):
    return (low(v), None)

def low_pass(kept, grad):
    return (grad,)

def back_keep(v):
    return (v, None)

def back_low(kept, grad):
    return (low(grad),)
low.defvjp(low_keep, low_pass)
low_back.defvjp(back_keep, back_low)

def doc_layout(lengths, row_count):
    doc_ends = jnp.cumsum(lengths).astype(jnp.int32)
    places = jnp.arange(row_count, dtype=jnp.int32)
    passed = doc_ends[None, :] <= places[:, None]
    segment = lax.optimization_barrier(jnp.sum(passed.astype(jnp.int32), axis=1)).astype(jnp.int32)
    starts = lax.optimization_barrier(jnp.sum(jnp.where(passed, lengths[None, :], 0), axis=1)).astype(jnp.int32)
    return (segment, places - starts)

def rotary_tables(positions):
    half_index = jnp.arange(ROT // 2, dtype=jnp.float32)
    inverse_freq = jnp.exp(half_index * (-2.0 * math.log(10000.0) / ROT))
    angles = positions.astype(jnp.float32)[:, None] * inverse_freq[None, :]
    angles = jnp.concatenate([angles, angles], axis=1)
    return (jnp.cos(angles), jnp.sin(angles))

def rotate_heads(flat, cosine, sine):
    row_count = flat.shape[0]
    heads = flat.reshape(row_count, HEADS, HEAD)
    turning = heads[:, :, :ROT]
    first_half = turning[:, :, :ROT // 2]
    second_half = turning[:, :, ROT // 2:]
    swapped = jnp.concatenate([-second_half, first_half], axis=2)
    turned = turning * cosine[:, None, :] + swapped * sine[:, None, :]
    return jnp.concatenate([turned, heads[:, :, ROT:]], axis=2).reshape(row_count, HEADS * HEAD)

def attend_block(block_data):
    query_rows, key_rows, value_rows, segment = block_data
    places = jnp.arange(query_rows.shape[0])
    allowed = (segment[:, None] == segment[None, :]) & (places[None, :] <= places[:, None])
    scores = low_back(jnp.einsum('qhe,khe->hqk', query_rows, key_rows, precision=PRECISE) * HEAD ** (-0.5))
    scores = jnp.where(allowed[None], scores, NEG_FILL)
    weights = low(jax.nn.softmax(scores, axis=-1))
    return jnp.einsum('hqk,khe->qhe', weights, value_rows, precision=PRECISE)

def layer_forward(stream, params, segment_grid, cosine, sine):
    norm_gain, norm_shift, qkv_weight, qkv_bias, out_weight, out_bias, up_weight, up_bias, down_weight, down_bias = params
    row_count = stream.shape[0]
    average = lax.optimization_barrier(jnp.mean(stream, axis=1, keepdims=True))
    centered = stream - average
    variance = lax.optimization_barrier(jnp.mean(centered * centered, axis=1, keepdims=True))
    unit = centered * lax.rsqrt(variance + EPSILON)
    normed = low(unit * norm_gain + norm_shift)
    packed = low_back(jnp.dot(normed, qkv_weight, precision=PRECISE) + qkv_bias)
    queries = low(rotate_heads(packed[:, :D], cosine, sine))
    key_rows = low(rotate_heads(packed[:, D:2 * D], cosine, sine))
    value_rows = low(packed[:, 2 * D:])
    block_count = row_count // TOK_DEV
    grid_shape = (block_count, TOK_DEV, HEADS, HEAD)
    attended = lax.map(jax.checkpoint(attend_block), (queries.reshape(grid_shape), key_rows.reshape(grid_shape), value_rows.reshape(grid_shape), segment_grid))
    attended = low(low_back(attended.reshape(row_count, D)))
    attention_out = low_back(jnp.dot(attended, out_weight, precision=PRECISE) + out_bias)
    pre_act = low_back(jnp.dot(normed, up_weight, precision=PRECISE) + up_bias)
    activated = low(jax.nn.gelu(pre_act, approximate=False))
    network_out = low_back(jnp.dot(activated, down_weight, precision=PRECISE) + down_bias)
    return stream + attention_out + network_out

def reference(tokens, token_order, lengths, cotangent, norm_gain, norm_shift, qkv_weight, qkv_bias, out_weight, out_bias, up_weight, up_bias, down_weight, down_bias):
    stacked = tuple((member.astype(jnp.float32) for member in (norm_gain, norm_shift, qkv_weight, qkv_bias, out_weight, out_bias, up_weight, up_bias, down_weight, down_bias)))
    dealt = jnp.take(tokens.astype(jnp.float32), token_order, axis=0)
    dealt_cot = jnp.take(cotangent.astype(jnp.float32), token_order, axis=0)
    block_count = TOKENS // TOK_DEV
    segment_grid, position_grid = jax.vmap(partial(doc_layout, row_count=TOK_DEV))(lengths.reshape(block_count, DOCS_DEV))
    cosine, sine = rotary_tables(position_grid.reshape(TOKENS))

    def whole_forward(stream, weights):
        for layer_index in range(LAYERS):
            stream = layer_forward(stream, tuple((member[layer_index] for member in weights)), segment_grid, cosine, sine)
        return stream
    result, pullback = jax.vjp(whole_forward, dealt, stacked)
    stream_grad, weight_grads = pullback(dealt_cot)
    restored = jnp.zeros_like(result).at[token_order].set(result)
    restored_grad = jnp.zeros_like(stream_grad).at[token_order].set(stream_grad)
    return (restored.astype(jnp.bfloat16), restored_grad.astype(jnp.bfloat16), weight_grads[0], weight_grads[1], weight_grads[2], weight_grads[3], weight_grads[4], weight_grads[5], weight_grads[6], weight_grads[7], weight_grads[8], weight_grads[9])
```

```python
import math

import jax
import jax.numpy as jnp
from jax import lax
from jax.experimental import pallas as pl
from jax.experimental.pallas import tpu as pltpu
from jax.sharding import PartitionSpec as P

HEADS = 16
HEAD = 64
ROT = 16
EPSILON = 1e-05
NEG_FILL = -1e30
AXES = ("shard", "rep")
bf16 = jnp.bfloat16
f32 = jnp.float32
VMEM_BYTES = 48 * 1024 * 1024
COLS = 512


def nn(a, b):
    return jnp.dot(a, b, preferred_element_type=f32)


def nt(a, b):
    return lax.dot_general(a, b, (((1,), (1,)), ((), ())), preferred_element_type=f32)


def whole(shape):
    return pl.BlockSpec(shape, lambda *_: (0,) * len(shape))


def row_blocks(rows, width):
    return pl.BlockSpec((rows, width), lambda i, *_: (i, 0))


ANY = pl.BlockSpec(memory_space=pl.ANY)


def call(kernel, scalars, inputs, outputs, grid, scratch=(), aliases={}, flops=0, bytes_=0):
    return pl.pallas_call(
        kernel,
        grid_spec=pltpu.PrefetchScalarGridSpec(
            num_scalar_prefetch=1,
            grid=grid,
            in_specs=[s for _, s in inputs],
            out_specs=[s for _, s in outputs],
            scratch_shapes=list(scratch),
        ),
        out_shape=[o for o, _ in outputs],
        input_output_aliases=aliases,
        compiler_params=pltpu.CompilerParams(vmem_limit_bytes=VMEM_BYTES),
        cost_estimate=pl.CostEstimate(flops=int(flops), bytes_accessed=int(bytes_), transcendentals=0),
    )(scalars, *[a for a, _ in inputs])


class Group:
    def __init__(self, blocks, first_half, extra=0):
        self.blocks = blocks
        self.rows = sum(b[0] for b in blocks) + extra
        self.first_half = first_half

    def cut(self, half):
        return (0, self.first_half) if half == 0 else (self.first_half, self.rows)


def piece_ranges(group, shards):
    ranges = []
    for r in range(shards):
        if bin(r).count("1") > 1:
            ranges += [(r,) + group.cut(0), (r,) + group.cut(1)]
        else:
            ranges.append((r, 0, group.rows))
    return ranges


def assembly(group, shards):
    plan = []
    for a, (r, lo, hi) in enumerate(piece_ranges(group, shards)):
        start = 0
        for rows, key, index in group.blocks:
            first, last = max(lo, start), min(hi, start + rows)
            if first < last:
                plan.append((a, first - lo, last - first, key, index, r, rows, first - start))
            start += rows
    return plan


def assemble_copies(group, shards, own, refs, targets, sems):
    copies = []
    for i, (a, src, rows, key, index, r, per, off) in enumerate(assembly(group, shards)):
        at = pl.multiple_of(lax.bitwise_xor(own, r) * per + off, 16)
        copies.append(
            pltpu.make_async_copy(
                refs[a].at[pl.ds(src, rows), :],
                targets[key].at[index, pl.ds(at, rows), :],
                sems.at[i],
            )
        )
    return copies


def spin(x, c, s1, s2):
    parts = []
    for j in range(x.shape[1] // 128):
        part = x[:, j * 128 : (j + 1) * 128]
        up = pltpu.roll(part, 128 - ROT // 2, 1)
        down = pltpu.roll(part, ROT // 2, 1)
        parts.append(part * c + up * s1 + down * s2)
    return parts


def forward_qkv(own, prev, adds, bias, gain, shift, qkv_b, tables, pieces, group, shards, block=256):
    rows, width = prev.shape
    count = len(pieces)
    n_add = len(adds)
    plan = assembly(group, shards)
    half = COLS

    def kernel(own_ref, *refs):
        prev_ref, *rest = refs
        add_refs, rest = rest[:n_add], rest[n_add:]
        bias_ref, gain_ref, shift_ref, qkvb_ref, c_ref, s1_ref, s2_ref, *rest = rest
        piece_refs, rest = rest[:count], rest[count:]
        stream_ref, unit_ref, inv_ref, normed_ref, q_ref, kv_ref, w_ref, sems = rest

        @pl.when(pl.program_id(0) == 0)
        def _():
            for c in assemble_copies(group, shards, own_ref[0], piece_refs, {"a": w_ref}, sems):
                c.start()

        x = prev_ref[...].astype(f32)
        if n_add:
            for a in add_refs:
                x = x + a[...].astype(f32)
            x = x + bias_ref[...]
        stream_ref[...] = x
        mean = jnp.mean(x, axis=1, keepdims=True)
        centered = x - mean
        inv = lax.rsqrt(jnp.mean(centered * centered, axis=1, keepdims=True) + EPSILON)
        unit = centered * inv
        unit_ref[...] = unit.astype(bf16)
        inv_ref[...] = jnp.broadcast_to(inv, inv_ref.shape)
        normed = (unit * gain_ref[...] + shift_ref[...]).astype(bf16)
        normed_ref[...] = normed

        @pl.when(pl.program_id(0) == 0)
        def _():
            for c in assemble_copies(group, shards, own_ref[0], piece_refs, {"a": w_ref}, sems):
                c.wait()

        c, s1, s2 = c_ref[...], s1_ref[...], s2_ref[...]
        q = nn(normed, w_ref[0]) + qkvb_ref[:, :half]
        for j, part in enumerate(spin(q, c, s1, s2)):
            q_ref[:, j * 128 : (j + 1) * 128] = (part * HEAD ** (-0.5)).astype(bf16)
        k = nn(normed, w_ref[1]) + qkvb_ref[:, half : 2 * half]
        for j, part in enumerate(spin(k, c, s1, s2)):
            kv_ref[:, j * 128 : (j + 1) * 128] = part.astype(bf16)
        v = nn(normed, w_ref[2]) + qkvb_ref[:, 2 * half :]
        kv_ref[:, half:] = v.astype(bf16)

    wide = row_blocks(block, width)
    inputs = (
        [(prev, wide)]
        + [(a, wide) for a in adds]
        + [(v, whole(v.shape)) for v in (bias, gain, shift, qkv_b)]
        + [(t, row_blocks(block, 128)) for t in tables]
        + [(p, ANY) for p in pieces]
    )
    S = jax.ShapeDtypeStruct
    outputs = [
        (S((rows, width), f32), wide),
        (S((rows, width), bf16), wide),
        (S((rows, 128), f32), row_blocks(block, 128)),
        (S((rows, width), bf16), wide),
        (S((rows, half), bf16), row_blocks(block, half)),
        (S((rows, 2 * half), bf16), row_blocks(block, 2 * half)),
    ]
    return call(
        kernel, own, inputs, outputs, (rows // block,),
        [pltpu.VMEM((3, width, half), bf16), pltpu.SemaphoreType.DMA((len(plan),))],
        flops=2 * rows * width * 3 * half, bytes_=rows * width * 12 + 3 * width * half * 2,
    )


def gelu_parts(x):
    z = jnp.abs(x) * math.sqrt(0.5)
    t = 1.0 / (1.0 + 0.3275911 * z)
    poly = t * (
        0.254829592 + t * (-0.284496736 + t * (1.421413741 + t * (-1.453152027 + t * 1.061405429)))
    )
    e = jnp.exp(-0.5 * x * x)
    tail = 0.5 * poly * e
    big = jnp.where(x >= 0, 1.0 - tail, tail)
    return x * big, big + x * e * (1.0 / math.sqrt(2.0 * math.pi))


def forward_up(own, normed, up_b, pieces, group, shards, block=256):
    rows, width = normed.shape
    count = len(pieces)
    plan = assembly(group, shards)
    chunks = len(group.blocks)

    def kernel(own_ref, x_ref, b_ref, *rest):
        piece_refs, rest = rest[:count], rest[count:]
        act_ref, slope_ref, w_ref, sems = rest

        @pl.when(pl.program_id(0) == 0)
        def _():
            copies = assemble_copies(group, shards, own_ref[0], piece_refs, {"u": w_ref}, sems)
            for c in copies:
                c.start()
            for c in copies:
                c.wait()

        for j in range(chunks):
            at = slice(j * COLS, (j + 1) * COLS)
            pre = nn(x_ref[...], w_ref[j]) + b_ref[:, at]
            act, slope = gelu_parts(pre)
            act_ref[:, at] = act.astype(bf16)
            slope_ref[:, at] = slope.astype(bf16)

    S = jax.ShapeDtypeStruct
    ff = chunks * COLS
    out = (S((rows, ff), bf16), row_blocks(block, ff))
    return call(
        kernel, own,
        [(normed, row_blocks(block, width)), (up_b, whole(up_b.shape))] + [(p, ANY) for p in pieces],
        [out, out], (rows // block,),
        [pltpu.VMEM((chunks, width, COLS), bf16), pltpu.SemaphoreType.DMA((len(plan),))],
        flops=4 * rows * width * ff, bytes_=rows * ff * 4 + width * ff * 2 + rows * width * 2,
    )


def forward_out(own, attended, activated, pieces, group, shards, block=256):
    rows, ff = activated.shape
    half = attended.shape[1]
    count = len(pieces)
    plan = assembly(group, shards)
    width = 2 * COLS

    def kernel(own_ref, att_ref, act_ref, *rest):
        piece_refs, rest = rest[:count], rest[count:]
        out_ref, d_ref, o_ref, sems = rest

        @pl.when(pl.program_id(0) == 0)
        def _():
            copies = assemble_copies(
                group, shards, own_ref[0], piece_refs, {"d": d_ref, "o": o_ref}, sems
            )
            for c in copies:
                c.start()
            for c in copies:
                c.wait()

        for j in range(2):
            got = nn(att_ref[...], o_ref[j]) + nn(act_ref[...], d_ref[j])
            out_ref[:, j * COLS : (j + 1) * COLS] = got.astype(bf16)

    S = jax.ShapeDtypeStruct
    return call(
        kernel, own,
        [(attended, row_blocks(block, half)), (activated, row_blocks(block, ff))]
        + [(p, ANY) for p in pieces],
        [(S((rows, width), bf16), row_blocks(block, width))], (rows // block,),
        [
            pltpu.VMEM((2, ff, COLS), bf16),
            pltpu.VMEM((2, half, COLS), bf16),
            pltpu.SemaphoreType.DMA((len(plan),)),
        ],
        flops=2 * rows * width * (ff + half), bytes_=(rows + width) * (ff + half) * 2 + rows * width * 2,
    )[0]


def attend(meta, q, kv, halo, doc_start, block=256):
    rows, width = q.shape
    reach = halo.shape[0]
    heads = width // HEAD

    def kernel(meta_ref, q_ref, kv_ref, halo_ref, ds_ref, out_ref, lse_ref, ext_ref, bias_ref, sems):
        b = pl.program_id(0)

        @pl.when(b == 0)
        def _():
            one = pltpu.make_async_copy(halo_ref, ext_ref.at[pl.ds(0, reach), :], sems.at[0])
            two = pltpu.make_async_copy(kv_ref, ext_ref.at[pl.ds(reach, rows), :], sems.at[1])
            one.start()
            two.start()
            one.wait()
            two.wait()

        def variant(skip):
            count = (reach // block + 1 - skip) * block
            first = pl.multiple_of((b + skip) * block, block)
            key = first - reach + lax.broadcasted_iota(jnp.int32, (block, count), 1)
            query = b * block + lax.broadcasted_iota(jnp.int32, (block, count), 0)
            allowed = (key <= query) & (key >= ds_ref[...])
            bias_ref[:, :count] = jnp.where(allowed, 0.0, NEG_FILL)
            lane = lax.broadcasted_iota(jnp.int32, (block, 128), 1)
            lse = jnp.zeros((block, 128), f32)
            for p in range(width // 128):
                q2 = q_ref[:, p * 128 : (p + 1) * 128]
                k2 = ext_ref[pl.ds(first, count), p * 128 : (p + 1) * 128]
                v2 = ext_ref[pl.ds(first, count), width + p * 128 : width + (p + 1) * 128]
                outs = []
                for side in range(2):
                    mine = (lane < HEAD) if side == 0 else (lane >= HEAD)
                    s = nt(jnp.where(mine, q2, jnp.zeros_like(q2)), k2) + bias_ref[:, :count]
                    top = jnp.max(s, axis=1, keepdims=True)
                    e = jnp.exp(s - top)
                    total = jnp.sum(e, axis=1, keepdims=True)
                    outs.append(nn(e.astype(bf16), v2) / total)
                    lse = jnp.where(lane == 2 * p + side, top + jnp.log(total), lse)
                out_ref[:, p * 128 : (p + 1) * 128] = jnp.where(lane < HEAD, outs[0], outs[1]).astype(bf16)
            lse_ref[...] = jnp.transpose(lse)[:heads]

        for skip in range(reach // block + 1):
            pl.when(meta_ref[b] == skip)(lambda skip=skip: variant(skip))

    S = jax.ShapeDtypeStruct
    return call(
        kernel, meta,
        [
            (q, row_blocks(block, width)), (kv, ANY), (halo, ANY), (doc_start, row_blocks(block, 1)),
        ],
        [
            (S((rows, width), bf16), row_blocks(block, width)),
            (S((heads, rows), f32), pl.BlockSpec((heads, block), lambda i, *_: (0, i))),
        ],
        (rows // block,),
        [
            pltpu.VMEM((rows + reach, 2 * width), bf16),
            pltpu.VMEM((block, reach + block), f32),
            pltpu.SemaphoreType.DMA((2,)),
        ],
        flops=8 * rows * 2 * reach * width, bytes_=(rows + reach) * width * 8,
    )


def attend_back(meta, q, kv, halo, doc_start_row, grad, attended, lse, tables, block=256):
    rows, width = q.shape
    reach = halo.shape[0]
    heads = width // HEAD
    steps = rows // block

    def kernel(meta_ref, q_ref, kv_ref, halo_ref, ds_ref, g_ref, o_ref, lse_ref, c_ref, s1_ref, s2_ref,
               dq_ref, dkv_ref, ext_ref, acc_ref, bias_ref, sems):
        b = pl.program_id(0)

        @pl.when(b == 0)
        def _():
            one = pltpu.make_async_copy(halo_ref, ext_ref.at[pl.ds(0, reach), :], sems.at[0])
            two = pltpu.make_async_copy(kv_ref, ext_ref.at[pl.ds(reach, rows), :], sems.at[1])
            one.start()
            two.start()
            acc_ref[...] = jnp.zeros_like(acc_ref)
            one.wait()
            two.wait()

        def variant(skip):
            count = (reach // block + 1 - skip) * block
            first = pl.multiple_of((b + skip) * block, block)
            key = first - reach + lax.broadcasted_iota(jnp.int32, (count, block), 0)
            query = b * block + lax.broadcasted_iota(jnp.int32, (count, block), 1)
            allowed = (key <= query) & (key >= ds_ref[...])
            bias_ref[:count, :] = jnp.where(allowed, 0.0, NEG_FILL)
            lane = lax.broadcasted_iota(jnp.int32, (block, 128), 1)
            wide_lane = lax.broadcasted_iota(jnp.int32, (count, 128), 1)
            for p in range(width // 128):
                at = slice(p * 128, (p + 1) * 128)
                q2, g2 = q_ref[:, at], g_ref[:, at]
                k2 = ext_ref[pl.ds(first, count), at]
                v2 = ext_ref[pl.ds(first, count), width + p * 128 : width + (p + 1) * 128]
                prod = jnp.transpose(g2.astype(f32) * o_ref[:, at].astype(f32))
                dk = dv = dq = None
                for side in range(2):
                    mine = (lane < HEAD) if side == 0 else (lane >= HEAD)
                    qm = jnp.where(mine, q2, jnp.zeros_like(q2))
                    gm = jnp.where(mine, g2, jnp.zeros_like(g2))
                    km = jnp.where((wide_lane < HEAD) if side == 0 else (wide_lane >= HEAD), k2, jnp.zeros_like(k2))
                    h = 2 * p + side
                    delta = jnp.sum(prod[side * HEAD : (side + 1) * HEAD], axis=0, keepdims=True)
                    prob = jnp.exp(nt(k2, qm) + bias_ref[:count, :] - lse_ref[h : h + 1, :])
                    ds = (prob * (nt(v2, gm) - delta)).astype(bf16)
                    one_dv = nn(prob.astype(bf16), gm)
                    one_dk = nn(ds, qm)
                    one_dq = lax.dot_general(ds, km, (((0,), (0,)), ((), ())), preferred_element_type=f32)
                    dv = one_dv if dv is None else dv + one_dv
                    dk = one_dk if dk is None else dk + one_dk
                    dq = one_dq if dq is None else dq + one_dq
                acc_ref[pl.ds(first, count), at] += dk
                acc_ref[pl.ds(first, count), width + p * 128 : width + (p + 1) * 128] += dv
                turned = spin(dq * HEAD ** (-0.5), c_ref[...], -s1_ref[...], -s2_ref[...])
                dq_ref[:, at] = turned[0].astype(bf16)

        for skip in range(reach // block + 1):
            pl.when(meta_ref[b] == skip)(lambda skip=skip: variant(skip))

        @pl.when(b == steps - 1)
        def _():
            dkv_ref[...] = acc_ref[...].astype(bf16)

    S = jax.ShapeDtypeStruct
    narrow = row_blocks(block, width)
    return call(
        kernel, meta,
        [
            (q, narrow), (kv, ANY), (halo, ANY),
            (doc_start_row, pl.BlockSpec((1, block), lambda i, *_: (0, i))),
            (grad, narrow), (attended, narrow),
            (lse, pl.BlockSpec((heads, block), lambda i, *_: (0, i))),
        ]
        + [(t, row_blocks(block, 128)) for t in tables],
        [
            (S((rows, width), bf16), narrow),
            (S((rows + reach, 2 * width), bf16), whole((rows + reach, 2 * width))),
        ],
        (steps,),
        [
            pltpu.VMEM((rows + reach, 2 * width), bf16),
            pltpu.VMEM((rows + reach, 2 * width), f32),
            pltpu.VMEM((reach + block, block), f32),
            pltpu.SemaphoreType.DMA((2,)),
        ],
        flops=20 * rows * 2 * reach * width, bytes_=(rows + reach) * width * 12,
    )


def backward_branch(own, branch, slope, pieces, group, shards, block=256):
    rows, width = branch.shape
    ff = slope.shape[1]
    half = COLS
    count = len(pieces)
    plan = assembly(group, shards)

    def kernel(own_ref, g_ref, slope_ref, *rest):
        piece_refs, rest = rest[:count], rest[count:]
        pre_ref, att_ref, presum_ref, gsum_ref, d_ref, o_ref, sems = rest
        i = pl.program_id(0)

        @pl.when(i == 0)
        def _():
            copies = assemble_copies(
                group, shards, own_ref[0], piece_refs, {"d": d_ref, "o": o_ref}, sems
            )
            for c in copies:
                c.start()
            presum_ref[...] = jnp.zeros_like(presum_ref)
            gsum_ref[...] = jnp.zeros_like(gsum_ref)
            for c in copies:
                c.wait()

        parts = [g_ref[:, j * COLS : (j + 1) * COLS] for j in range(2)]
        att_ref[...] = (nt(parts[0], o_ref[0]) + nt(parts[1], o_ref[1])).astype(bf16)
        for j in range(ff // COLS):
            at = slice(j * COLS, (j + 1) * COLS)
            got = nt(parts[0], d_ref[0, at, :]) + nt(parts[1], d_ref[1, at, :])
            pre = (got * slope_ref[:, at].astype(f32)).astype(bf16)
            pre_ref[:, at] = pre
            presum_ref[:, at] += jnp.sum(pre.astype(f32), axis=0, keepdims=True)

        core = own_ref[1]
        mine = (i * block // (rows // 2)) == core

        @pl.when(mine)
        def _():
            gsum_ref[...] += jnp.sum(g_ref[...].astype(f32), axis=0, keepdims=True)

    S = jax.ShapeDtypeStruct
    return call(
        kernel, own,
        [(branch, row_blocks(block, width)), (slope, row_blocks(block, ff))] + [(p, ANY) for p in pieces],
        [
            (S((rows, ff), bf16), row_blocks(block, ff)),
            (S((rows, half), bf16), row_blocks(block, half)),
            (S((1, ff), f32), whole((1, ff))),
            (S((1, width), f32), whole((1, width))),
        ],
        (rows // block,),
        [
            pltpu.VMEM((2, ff, COLS), bf16),
            pltpu.VMEM((2, half, COLS), bf16),
            pltpu.SemaphoreType.DMA((len(plan),)),
        ],
        flops=2 * rows * width * (ff + half), bytes_=(2 * rows + width) * (ff + half) * 2 + rows * width * 2,
    )


def backward_normed(own, dq, dkv, halo, pre_grad, unit, tables, a_pieces, u_pieces, a_group, u_group, shards, block=256):
    rows, half = dq.shape
    width, ff = unit.shape[1], pre_grad.shape[1]
    reach = halo.shape[0]
    steps, late = rows // block, (rows - reach) // block
    na, nu = len(a_pieces), len(u_pieces)
    plan_a, plan_u = assembly(a_group, shards), assembly(u_group, shards)

    def kernel(own_ref, dq_ref, dkv_ref, halo_ref, pre_ref, unit_ref, c_ref, s1_ref, s2_ref, *rest):
        a_refs, rest = rest[:na], rest[na:]
        u_refs, rest = rest[:nu], rest[nu:]
        packed_ref, part_ref, bsum_ref, gain_ref, shift_ref, a_ref, u_ref, sem_a, sem_u = rest
        i = pl.program_id(0)

        def copies():
            return assemble_copies(a_group, shards, own_ref[0], a_refs, {"a": a_ref}, sem_a) + assemble_copies(
                u_group, shards, own_ref[0], u_refs, {"u": u_ref}, sem_u
            )

        @pl.when(i == 0)
        def _():
            for c in copies():
                c.start()
            for ref in (bsum_ref, gain_ref, shift_ref):
                ref[...] = jnp.zeros_like(ref)

        dkv_now = dkv_ref[...].astype(f32) + jnp.where(i >= late, halo_ref[...].astype(f32), 0.0)
        packed_ref[:, :half] = dq_ref[...]
        for j, part in enumerate(spin(dkv_now[:, :half], c_ref[...], -s1_ref[...], -s2_ref[...])):
            packed_ref[:, half + j * 128 : half + (j + 1) * 128] = part.astype(bf16)
        packed_ref[:, 2 * half :] = dkv_now[:, half:].astype(bf16)

        @pl.when(i == 0)
        def _():
            for c in copies():
                c.wait()

        bsum_ref[...] += jnp.sum(packed_ref[...].astype(f32), axis=0, keepdims=True)
        for n in range(width // COLS):
            at = slice(n * COLS, (n + 1) * COLS)
            total = None
            for j in range(3):
                got = nt(packed_ref[:, j * COLS : (j + 1) * COLS], a_ref[j, at, :])
                total = got if total is None else total + got
            for j in range(ff // COLS):
                total += nt(pre_ref[:, j * COLS : (j + 1) * COLS], u_ref[j, at, :])
            part_ref[:, at] = total.astype(bf16)
            gain_ref[:, at] += jnp.sum(total * unit_ref[:, at].astype(f32), axis=0, keepdims=True)
            shift_ref[:, at] += jnp.sum(total, axis=0, keepdims=True)

    S = jax.ShapeDtypeStruct
    skip = reach // block
    return call(
        kernel, own,
        [
            (dq, row_blocks(block, half)),
            (dkv, pl.BlockSpec((block, 2 * half), lambda i, *_: (i + skip, 0))),
            (halo, pl.BlockSpec((block, 2 * half), lambda i, *_: (jnp.maximum(i - late, 0), 0))),
            (pre_grad, row_blocks(block, ff)),
            (unit, row_blocks(block, width)),
        ]
        + [(t, row_blocks(block, 128)) for t in tables]
        + [(p, ANY) for p in (*a_pieces, *u_pieces)],
        [
            (S((rows, 3 * half), bf16), row_blocks(block, 3 * half)),
            (S((rows, width), bf16), row_blocks(block, width)),
            (S((1, 3 * half), f32), whole((1, 3 * half))),
            (S((1, width), f32), whole((1, width))),
            (S((1, width), f32), whole((1, width))),
        ],
        (steps,),
        [
            pltpu.VMEM((3, width, COLS), bf16),
            pltpu.VMEM((ff // COLS, width, COLS), bf16),
            pltpu.SemaphoreType.DMA((len(plan_a),)),
            pltpu.SemaphoreType.DMA((len(plan_u),)),
        ],
        flops=2 * rows * width * (ff + 3 * half), bytes_=(rows + width) * (ff + 3 * half) * 2 + rows * width * 4,
    )


def norm_backward(own, grad, parts, unit, inv, gain, block=256):
    rows, width = unit.shape

    def kernel(own_ref, g_ref, p0_ref, p1_ref, unit_ref, inv_ref, gain_ref, new_ref, low_ref):
        u = (p0_ref[...].astype(f32) + p1_ref[...].astype(f32)) * gain_ref[...]
        unit = unit_ref[...].astype(f32)
        new = g_ref[...].astype(f32) + inv_ref[:, :1] * (
            u - jnp.mean(u, axis=1, keepdims=True) - unit * jnp.mean(u * unit, axis=1, keepdims=True)
        )
        new_ref[...] = new
        low_ref[...] = new.astype(bf16)

    S = jax.ShapeDtypeStruct
    wide = row_blocks(block, width)
    return call(
        kernel, own,
        [(grad, wide), (parts[0], wide), (parts[1], wide), (unit, wide), (inv, row_blocks(block, 128)),
         (gain, whole(gain.shape))],
        [(S((rows, width), f32), wide), (S((rows, width), bf16), wide)],
        (rows // block,), bytes_=rows * width * 16, flops=rows * width * 10,
    )


def weight_grads(own, lefts, rights, extra, group, first_half, shards):
    rows = rights.shape[0]
    blocks = rights.shape[1] // COLS
    ks = [l.shape[1] // shards for l in lefts]
    height = sum(ks)
    n_left = len(lefts)
    extra_rows = 0 if extra is None else extra.shape[0] // shards
    total = height * blocks + extra_rows
    ranges = piece_ranges(Group([(total, "", 0)], first_half), shards)

    def kernel(own_ref, *refs):
        left_refs, rest = refs[:n_left], refs[n_left:]
        right_ref, rest = rest[0], rest[1:]
        extra_ref, rest = (None, rest) if extra is None else (rest[0], rest[1:])
        out_refs, flipped = rest[: len(ranges)], rest[len(ranges) :]
        for l, t in zip(left_refs, flipped):
            t[...] = jnp.transpose(l[...])

        def store(r, start, value):
            for (rel, lo, hi), ref in zip(ranges, out_refs):
                first, last = max(lo, start), min(hi, start + value.shape[0])
                if rel == r and first < last:
                    ref[first - lo : last - lo, :] = value[first - start : last - start]

        for r in range(shards):
            s = lax.bitwise_xor(own_ref[0], r)
            for j in range(blocks):
                start = j * height
                right = right_ref[:, j * COLS : (j + 1) * COLS]
                for t, k in zip(flipped, ks):
                    left = t[pl.ds(pl.multiple_of(s * k, k), k), :]
                    store(r, start, nn(left, right).astype(bf16))
                    start += k
            if extra is not None:
                store(r, height * blocks, extra_ref[pl.ds(pl.multiple_of(s * extra_rows, extra_rows), extra_rows), :].astype(bf16))

    S = jax.ShapeDtypeStruct
    extras = [] if extra is None else [extra]
    inputs = [(a, whole(a.shape)) for a in (*lefts, rights, *extras)]
    outputs = [(S((hi - lo, COLS), bf16), whole((hi - lo, COLS))) for _, lo, hi in ranges]
    return call(
        kernel, own, inputs, outputs, (1,),
        [pltpu.VMEM((l.shape[1], rows), bf16) for l in lefts],
        flops=2 * rows * sum(l.shape[1] for l in lefts) * rights.shape[1],
        bytes_=2 * (rows * rights.shape[1] + sum(l.size for l in lefts) + shards * total * COLS),
    )


def pick(core, first, second):
    return jnp.where(core == 0, first, second)


def pack_qkv(own, weight, layer, shards):
    _, rows, columns = weight.shape
    w = columns // (6 * shards)

    def kernel(own_ref, w_ref, out_ref):
        core = own_ref[1]
        for g in range(3):
            for s in range(shards):
                at = (g * shards + s) * 2 * w
                out_ref[g * rows : (g + 1) * rows, s * w : (s + 1) * w] = pick(
                    core, w_ref[0, :, at : at + w], w_ref[0, :, at + w : at + 2 * w]
                )

    shape = (3 * rows, COLS)
    return call(
        kernel, own,
        [(weight, pl.BlockSpec((1, rows, columns), lambda i, *_: (layer, 0, 0)))],
        [(jax.ShapeDtypeStruct(shape, bf16), whole(shape))], (1,), bytes_=rows * columns * 3,
    )[0]


def pack_up(own, weight, layer, shards):
    _, rows, columns = weight.shape
    w = columns // (2 * shards)
    blocks = columns // 2 // COLS

    def kernel(own_ref, w_ref, out_ref):
        core = own_ref[1]
        for s in range(shards):
            j, off = s * w // COLS, s * w % COLS
            at = s * 2 * w
            out_ref[j * rows : (j + 1) * rows, off : off + w] = pick(
                core, w_ref[0, :, at : at + w], w_ref[0, :, at + w : at + 2 * w]
            )

    shape = (blocks * rows, COLS)
    return call(
        kernel, own,
        [(weight, pl.BlockSpec((1, rows, columns), lambda i, *_: (layer, 0, 0)))],
        [(jax.ShapeDtypeStruct(shape, bf16), whole(shape))], (1,), bytes_=rows * columns * 3,
    )[0]


def pack_out(own, down, out, layer):
    dr, orows = down.shape[1] // 2, out.shape[1] // 2
    width = down.shape[2]
    blocks = width // COLS

    def kernel(own_ref, d_ref, o_ref, out_ref):
        for j in range(blocks):
            at = slice(j * COLS, (j + 1) * COLS)
            base = j * (dr + orows)
            out_ref[base : base + dr, :] = d_ref[0, :, at]
            out_ref[base + dr : base + dr + orows, :] = o_ref[0, :, at]

    shape = (blocks * (dr + orows), COLS)
    spec = lambda r: pl.BlockSpec((1, r, width), lambda i, own_ref: (layer, own_ref[1], 0))
    return call(
        kernel, own, [(down, spec(dr)), (out, spec(orows))],
        [(jax.ShapeDtypeStruct(shape, bf16), whole(shape))], (1,), bytes_=(dr + orows) * width * 4,
    )[0]


def unpack_columns(own, mine, theirs, before, layer, layers, rows, kinds, w, shards):
    columns = kinds * shards * 2 * w
    blocks = kinds * shards * w // COLS

    def kernel(own_ref, a_ref, b_ref, *rest):
        out_ref = rest[-1]
        core = own_ref[1]
        for g in range(kinds):
            for s in range(shards):
                c = (g * shards + s) * w
                j, off = c // COLS, c % COLS
                a = a_ref[j * rows : (j + 1) * rows, off : off + w].astype(f32)
                b = b_ref[j * rows : (j + 1) * rows, off : off + w].astype(f32)
                out_ref[0, :, 2 * c : 2 * c + w] = pick(core, a, b)
                out_ref[0, :, 2 * c + w : 2 * c + 2 * w] = pick(core, b, a)

    extra = [] if before is None else [(before, ANY)]
    shape = (blocks * rows, COLS)
    return call(
        kernel, own, [(mine, whole(shape)), (theirs, whole(shape))] + extra,
        [(jax.ShapeDtypeStruct((layers, rows, columns), f32),
          pl.BlockSpec((1, rows, columns), lambda i, *_: (layer, 0, 0)))],
        (1,), aliases={} if before is None else {3: 0}, bytes_=rows * columns * 6,
    )[0]


def unpack_rows(own, mine, theirs, befores, layer, layers, heights, width):
    blocks = width // COLS
    total = sum(heights)

    def kernel(own_ref, a_ref, b_ref, *rest):
        out_refs = rest[-len(heights) :]
        core = own_ref[1]
        for j in range(blocks):
            start = j * total
            for h, ref in zip(heights, out_refs):
                a = a_ref[start : start + h, :].astype(f32)
                b = b_ref[start : start + h, :].astype(f32)
                ref[0, :h, j * COLS : (j + 1) * COLS] = pick(core, a, b)
                ref[0, h:, j * COLS : (j + 1) * COLS] = pick(core, b, a)
                start += h

    extra = [] if befores is None else [(b, ANY) for b in befores]
    shape = (blocks * total, COLS)
    return call(
        kernel, own, [(mine, whole(shape)), (theirs, whole(shape))] + extra,
        [(jax.ShapeDtypeStruct((layers, 2 * h, width), f32),
          pl.BlockSpec((1, 2 * h, width), lambda i, *_: (layer, 0, 0))) for h in heights],
        (1,), aliases={} if befores is None else {3 + i: i for i in range(len(heights))},
        bytes_=total * width * 12,
    )


class Net:
    def __init__(self, shards, reps):
        self.shards, self.reps = shards, reps
        self.bits = [1 << b for b in range(shards.bit_length() - 1)]
        self.chips = reps // 2
        self.shard = lax.axis_index("shard")
        self.rep = lax.axis_index("rep")
        self.core = self.rep % 2
        self.chip = self.rep // 2

    def send(self, value, where):
        pairs = []
        for s in range(self.shards):
            for r in range(self.reps):
                to = where(s, r)
                if to is not None:
                    pairs.append((s * self.reps + r, to[0] * self.reps + to[1]))
        return lax.ppermute(value, AXES, pairs)

    def other_core(self, value):
        return self.send(value, lambda s, r: (s, r ^ 1))

    def flip(self, value, bit):
        return self.send(value, lambda s, r: (s ^ bit, r))

    def next_chip(self, value):
        return self.send(value, lambda s, r: (s, r + 2) if r + 2 < self.reps else None)

    def last_chip(self, value):
        return self.send(value, lambda s, r: (s, r - 2) if r >= 2 else None)

    def last_bit(self, relative, half):
        order = self.bits if half == 0 else self.bits[::-1]
        return [b for b in order if relative & b][-1]

    def gather(self, own, group, after=None):
        if after is not None:
            own, _ = lax.optimization_barrier((own, after))
        pieces = {0: own}
        for bit in self.bits:
            pieces[bit] = self.flip(own, bit)
        near = [pieces[bit] for bit in self.bits]
        got = []
        for r, lo, hi in piece_ranges(group, self.shards):
            if bin(r).count("1") <= 1:
                got.append(pieces[r])
                continue
            half = 0 if lo == 0 else 1
            bit = self.last_bit(r, half)
            source = pieces[r ^ bit]
            part = source[half] if isinstance(source, list) else source[lo:hi]
            pieces.setdefault(r, []).append(self.flip(part, bit))
            got.append(pieces[r][-1])
        return got, near

    def scatter_sum(self, arrays, group):
        ranges = piece_ranges(group, self.shards)
        acc = {}
        for (r, lo, hi), a in zip(ranges, arrays):
            acc.setdefault(r, []).append((lo, hi, a))
        for r in sorted(range(1, self.shards), key=lambda r: (-bin(r).count("1"), r)):
            for lo, hi, a in acc[r]:
                half = 0 if lo == 0 else 1
                bit = self.last_bit(r, half)
                came = self.flip(a, bit)
                target = acc[r ^ bit]
                for i, (tlo, thi, t) in enumerate(target):
                    first, last = max(lo, tlo), min(hi, thi)
                    if first >= last:
                        continue
                    part = came[first - lo : last - lo]
                    if (first, last) == (tlo, thi):
                        new = t.astype(f32) + part.astype(f32)
                    else:
                        new = t.astype(f32) + jnp.pad(
                            part.astype(f32), ((first - tlo, thi - last), (0, 0))
                        )
                    target[i] = (tlo, thi, new.astype(bf16))
        return acc[0][0][2]

    def sum_chips(self, value):
        chips = self.chips
        line = 4 if chips % 4 == 0 else 1
        if line == 4:
            at = self.chip % 4

            def inward(s, r):
                z = (r // 2) % 4
                return (s, r + 2) if z == 0 else (s, r - 2) if z == 3 else None

            def across(s, r):
                z = (r // 2) % 4
                return (s, r + 2) if z == 1 else (s, r - 2) if z == 2 else None

            def outward(s, r):
                z = (r // 2) % 4
                return (s, r - 2) if z == 1 else (s, r + 2) if z == 2 else None

            value = (value.astype(f32) + self.send(value, inward).astype(f32)).astype(bf16)
            value = (value.astype(f32) + self.send(value, across).astype(f32)).astype(bf16)
            back = self.send(value, outward)
            value = jnp.where((at == 0) | (at == 3), back, value)
        step = line
        while step < chips:
            came = self.send(value, lambda s, r, step=step: (s, r ^ (2 * step)))
            value = (value.astype(f32) + came.astype(f32)).astype(bf16)
            step *= 2
        return value


def core_columns(core, rows, kinds, shards):
    cut = rows.reshape(rows.shape[0], kinds * shards, 2, -1)
    return pick(core, cut[:, :, 0], cut[:, :, 1]).reshape(rows.shape[0], -1)


def body(
    tokens,
    token_order,
    lengths,
    cotangent,
    norm_gain,
    norm_shift,
    qkv_weight,
    qkv_bias,
    out_weight,
    out_bias,
    up_weight,
    up_bias,
    down_weight,
    down_bias,
):
    net = Net(lax.axis_size("shard"), lax.axis_size("rep"))
    shards, core = net.shards, net.core
    layers = norm_gain.shape[0]
    row_count, width = tokens.shape
    rows = 2 * row_count
    reach = row_count
    block = 256
    piece = width // shards
    ff = up_weight.shape[2] // 2
    group_first = net.shard * row_count * net.reps
    chip_first = net.chip * rows
    own = jnp.stack([net.shard, core]).astype(jnp.int32)

    ff_piece, head_piece = ff // shards, width // 2 // shards
    group_a = Group([(piece, "a", j) for j in range(3)], 3 * piece // 2)
    group_u = Group([(piece, "u", j) for j in range(ff // COLS)], piece * (ff // COLS) // 2)
    group_o = Group(
        [b for j in range(2) for b in ((ff_piece, "d", j), (head_piece, "o", j))], ff_piece + head_piece
    )
    grads_a = Group([(3 * piece + 16, "", 0)], 3 * piece // 2)

    after = None
    gathered = []
    for l in range(layers):
        layer = []
        for group, packed in (
            (group_a, lambda: pack_qkv(own, qkv_weight, l, shards)),
            (group_u, lambda: pack_up(own, up_weight, l, shards)),
            (group_o, lambda: pack_out(own, down_weight, out_weight, l)),
        ):
            got, after = net.gather(packed(), group, after)
            layer.append(got)
        gathered.append(layer)

    names = (norm_gain, norm_shift, qkv_bias, out_bias, up_bias, down_bias)
    small = lax.all_gather(jnp.concatenate([v.reshape(-1) for v in names]), "shard", axis=0)
    vectors, offset = [], 0
    for v in names:
        part = small[:, offset : offset + v.size].reshape((shards,) + v.shape)
        vectors.append(jnp.moveaxis(part, 0, 1).reshape(layers, -1).astype(f32))
        offset += v.size
    gains, shifts, qkv_b, out_b, up_b, down_b = vectors
    qkv_b = core_columns(core, qkv_b, 3, shards)
    up_b = core_columns(core, up_b, 1, shards)
    branch_b = out_b + down_b

    slots = lengths.shape[0]
    before = jnp.arange(slots)[None, :] < jnp.arange(slots)[:, None]
    dealt_start = jnp.sum(jnp.where(before, lengths[None, :], 0), axis=1)
    hit = dealt_start[:, None] == jnp.arange(row_count)[None, :]
    home = jnp.sum(jnp.where(hit, token_order[None, :], 0), axis=1) - group_first
    docs = lax.all_gather(jnp.stack([home, lengths]), "rep", axis=0)
    home, length = docs[:, 0].reshape(-1), docs[:, 1].reshape(-1)
    place = chip_first + jnp.arange(rows, dtype=jnp.int32)
    inside = (home[None, :] <= place[:, None]) & (place[:, None] < (home + length)[None, :])
    doc_start = jnp.sum(jnp.where(inside, home[None, :], 0), axis=1) - chip_first
    earliest = jnp.min(doc_start.reshape(rows // block, block), axis=1)
    meta = jnp.clip((earliest + reach) // block - jnp.arange(rows // block), 0, reach // block)
    meta = meta.astype(jnp.int32)
    start_column, start_row = doc_start[:, None], doc_start[None, :]

    lane = jnp.arange(128) % HEAD
    positions = (jnp.arange(rows, dtype=jnp.int32) - doc_start).astype(f32)
    inverse_freq = jnp.exp((lane % (ROT // 2)).astype(f32) * (-2.0 * math.log(10000.0) / ROT))
    angles = positions[:, None] * inverse_freq[None, :]
    sine = jnp.sin(angles)
    tables = (
        jnp.where(lane < ROT, jnp.cos(angles), 1.0),
        jnp.where(lane < ROT // 2, -sine, 0.0),
        jnp.where((lane >= ROT // 2) & (lane < ROT), sine, 0.0),
    )

    def pair_rows(x):
        other = net.other_core(x)
        return jnp.concatenate([pick(core, x, other), pick(core, other, x)])

    def own_rows(x):
        return lax.dynamic_slice_in_dim(x, core * row_count, row_count)

    stream, adds = pair_rows(tokens), []
    saved = []
    bias = jnp.zeros((1, width), f32)
    for l in range(layers):
        a_pieces, u_pieces, o_pieces = gathered[l]
        stream, unit, inv, normed, q, kv = forward_qkv(
            own, stream, adds, bias, gains[l : l + 1], shifts[l : l + 1], qkv_b[l : l + 1], tables,
            a_pieces, group_a, shards,
        )
        halo = net.next_chip(kv[rows - reach :])
        activated, slope = forward_up(own, normed, up_b[l : l + 1], u_pieces, group_u, shards)
        attended, lse = attend(meta, q, kv, halo, start_column)
        partial = forward_out(own, attended, activated, o_pieces, group_o, shards)
        adds = [partial, net.other_core(partial)]
        bias = branch_b[l : l + 1]
        saved.append((unit, inv, normed, q, kv, halo, activated, slope, attended, lse))
    block_output = (
        own_rows(stream) + own_rows(adds[0]).astype(f32) + own_rows(adds[1]).astype(f32) + bias
    ).astype(bf16)

    branch = pair_rows(cotangent)
    grad = branch
    reduced = [None] * layers
    for l in reversed(range(layers)):
        a_pieces, u_pieces, o_pieces = gathered[l]
        unit, inv, normed, q, kv, halo, activated, slope, attended, lse = saved[l]
        o_sum = net.scatter_sum(
            weight_grads(own, [activated, attended], branch, None, None, group_o.first_half, shards), group_o
        )
        pre_grad, attended_grad, up_sum, branch_sum = backward_branch(
            own, branch, slope, o_pieces, group_o, shards
        )
        dq, dkv = attend_back(meta, q, kv, halo, start_row, attended_grad, attended, lse, tables)
        halo_grad = net.last_chip(dkv[:reach])
        u_sum = net.scatter_sum(
            weight_grads(own, [normed], pre_grad, None, None, group_u.first_half, shards), group_u
        )
        packed_grad, part, qkv_sum, gain_sum, shift_sum = backward_normed(
            own, dq, dkv, halo_grad, pre_grad, unit, tables, a_pieces, u_pieces, group_a, group_u, shards
        )
        came = net.other_core(part)

        def line(v, width):
            v = v.reshape(shards, -1)
            return jnp.pad(v, ((0, 0), (0, width - v.shape[1])))

        qkv_sum = qkv_sum.reshape(3 * shards, 1, -1)
        nothing = jnp.zeros_like(qkv_sum)
        qkv_sum = jnp.concatenate(
            [pick(core, qkv_sum, nothing), pick(core, nothing, qkv_sum)], axis=1
        )
        extra = jnp.concatenate(
            [
                line(gain_sum, COLS // 2),
                line(shift_sum, COLS // 2),
                line(branch_sum, COLS),
                line(up_sum, COLS),
                line(qkv_sum, 13 * COLS),
            ],
            axis=1,
        ).reshape(shards * 16, COLS)
        a_sum = net.scatter_sum(
            weight_grads(own, [normed], packed_grad, extra, None, group_a.first_half, shards), grads_a
        )
        reduced[l] = (a_sum, u_sum, o_sum)
        grad, branch = norm_backward(own, grad, [part, came], unit, inv, gains[l : l + 1])
    input_grad = own_rows(branch)

    qkv_g = up_g = out_g = down_g = None
    smalls = [None] * layers
    for l in reversed(range(layers)):
        final = [net.sum_chips(v) for v in reduced[l]]
        theirs = [net.other_core(v) for v in final]
        o_before = None if down_g is None else [down_g, out_g]
        down_g, out_g = unpack_rows(
            own, final[2], theirs[2], o_before, l, layers, (ff_piece, head_piece), width
        )
        up_g = unpack_columns(
            own, final[1], theirs[1], up_g, l, layers, piece, 1, ff_piece, shards
        )
        qkv_g = unpack_columns(
            own, final[0], theirs[0], qkv_g, l, layers, piece, 3, head_piece, shards
        )
        smalls[l] = (final[0][3 * piece :], theirs[0][3 * piece :])
    mine, theirs = (jnp.stack([s[i] for s in smalls]).astype(f32) for i in range(2))
    low, high = pick(core, mine, theirs), pick(core, theirs, mine)
    both = low + high
    branch_g = both[:, 1, :piece]
    return (
        block_output,
        input_grad,
        both[:, 0, :piece],
        both[:, 0, COLS // 2 : COLS // 2 + piece],
        qkv_g,
        both[:, 3:5].reshape(layers, -1)[:, : 3 * piece],
        out_g,
        branch_g,
        up_g,
        jnp.concatenate([low[:, 2, :ff_piece], high[:, 2, :ff_piece]], axis=1),
        down_g,
        branch_g,
    )


def solution(mesh):
    rows = P(("shard", "rep"), None)
    vector, matrix = P(None, "shard"), P(None, "shard", None)
    line = P(("shard", "rep"))
    return jax.shard_map(
        body,
        mesh=mesh,
        in_specs=(
            rows, line, line, rows, vector, vector, matrix, vector, matrix, vector,
            matrix, vector, matrix, vector,
        ),
        out_specs=(
            rows, rows, vector, vector, matrix, vector, matrix, vector, matrix, vector,
            matrix, vector,
        ),
        check_vma=False,
    )
```

```python
import math

import jax
import jax.numpy as jnp
from jax import lax
from jax.experimental import pallas as pl
from jax.experimental.pallas import tpu as pltpu
from jax.sharding import PartitionSpec as P

HEADS = 16
HEAD = 64
ROT = 16
EPSILON = 1e-05
NEG_FILL = -1e30
AXES = ("shard", "rep")
bf16 = jnp.bfloat16
f32 = jnp.float32
VMEM_BYTES = 48 * 1024 * 1024
COLS = 512


def nn(a, b):
    return jnp.dot(a, b, preferred_element_type=f32)


def nt(a, b):
    return lax.dot_general(a, b, (((1,), (1,)), ((), ())), preferred_element_type=f32)


def whole(shape):
    return pl.BlockSpec(shape, lambda *_: (0,) * len(shape))


def row_blocks(rows, width):
    return pl.BlockSpec((rows, width), lambda i, *_: (i, 0))


ANY = pl.BlockSpec(memory_space=pl.ANY)


def call(kernel, scalars, inputs, outputs, grid, scratch=(), aliases={}, flops=0, bytes_=0):
    return pl.pallas_call(
        kernel,
        grid_spec=pltpu.PrefetchScalarGridSpec(
            num_scalar_prefetch=1,
            grid=grid,
            in_specs=[s for _, s in inputs],
            out_specs=[s for _, s in outputs],
            scratch_shapes=list(scratch),
        ),
        out_shape=[o for o, _ in outputs],
        input_output_aliases=aliases,
        compiler_params=pltpu.CompilerParams(vmem_limit_bytes=VMEM_BYTES),
        cost_estimate=pl.CostEstimate(flops=1, bytes_accessed=1, transcendentals=0),
    )(scalars, *[a for a, _ in inputs])


class Group:
    def __init__(self, blocks, first_half, extra=0):
        self.blocks = blocks
        self.rows = sum(b[0] for b in blocks) + extra
        self.first_half = first_half

    def cut(self, half):
        return (0, self.first_half) if half == 0 else (self.first_half, self.rows)


def piece_ranges(group, shards):
    ranges = []
    for r in range(shards):
        if bin(r).count("1") > 1:
            ranges += [(r,) + group.cut(0), (r,) + group.cut(1)]
        else:
            ranges.append((r, 0, group.rows))
    return ranges


def hop_bits(shards, half):
    bits = [1 << b for b in range(shards.bit_length() - 1)]
    return bits if half == 0 else bits[::-1]


def last_bit(shards, relative, half):
    return [b for b in hop_bits(shards, half) if relative & b][-1]


def sum_rounds(shards):
    keys = [(r, h) for r in range(1, shards) for h in range(2)]
    goes = {(r, h): (r ^ last_bit(shards, r, h), h) for r, h in keys}
    depth = {}
    for key in sorted(keys, key=lambda k: -bin(k[0]).count("1")):
        before = [depth[k] for k, to in goes.items() if to == key]
        depth[key] = 1 + max(before) if before else 0
    rounds = {}
    for key in sorted(keys, key=lambda k: (depth[k], -bin(k[0]).count("1"), k)):
        rounds.setdefault((depth[key], last_bit(shards, *key)), []).append(key)
    return rounds, goes


def store_rows(refs, halves, start, value):
    for (lo, hi), ref in zip(halves, refs):
        first, last = max(lo, start), min(hi, start + value.shape[0])
        if first < last:
            ref[first - lo : last - lo, :] = value[first - start : last - start]


def assembly(group, shards):
    plan = []
    for a, (r, lo, hi) in enumerate(piece_ranges(group, shards)):
        start = 0
        for rows, key, index in group.blocks:
            first, last = max(lo, start), min(hi, start + rows)
            if first < last:
                plan.append((a, first - lo, last - first, key, index, r, rows, first - start))
            start += rows
    return plan


def assemble_copies(group, shards, own, refs, targets, sems):
    copies = []
    for i, (a, src, rows, key, index, r, per, off) in enumerate(assembly(group, shards)):
        at = pl.multiple_of(lax.bitwise_xor(own, r) * per + off, 16)
        copies.append(
            pltpu.make_async_copy(
                refs[a].at[pl.ds(src, rows), :],
                targets[key].at[index, pl.ds(at, rows), :],
                sems.at[i],
            )
        )
    return copies


def spin(x, c, s1, s2):
    parts = []
    for j in range(x.shape[1] // 128):
        part = x[:, j * 128 : (j + 1) * 128]
        up = pltpu.roll(part, 128 - ROT // 2, 1)
        down = pltpu.roll(part, ROT // 2, 1)
        parts.append(part * c + up * s1 + down * s2)
    return parts


def forward_qkv(own, layer, prev, adds, biases, gain, shift, qkv_b, tables, pieces, group, shards, block=256):
    rows, width = prev.shape
    count = len(pieces)
    n_add = len(adds)
    plan = assembly(group, shards)
    half = COLS

    def kernel(own_ref, *refs):
        prev_ref, *rest = refs
        add_refs, rest = rest[:n_add], rest[n_add:]
        bias_refs, rest = rest[: len(biases)], rest[len(biases) :]
        gain_ref, shift_ref, qkvb_ref, c_ref, s1_ref, s2_ref, *rest = rest
        now = slice(layer, layer + 1)
        piece_refs, rest = rest[:count], rest[count:]
        stream_ref, unit_ref, inv_ref, normed_ref, q_ref, kv_ref, w_ref, sems = rest

        @pl.when(pl.program_id(0) == 0)
        def _():
            for c in assemble_copies(group, shards, own_ref[0], piece_refs, {"a": w_ref}, sems):
                c.start()

        x = prev_ref[...].astype(f32)
        if n_add:
            for a in add_refs:
                x = x + a[...].astype(f32)
            for b in bias_refs:
                x = x + b[layer - 1 : layer, :]
        stream_ref[...] = x
        mean = jnp.mean(x, axis=1, keepdims=True)
        centered = x - mean
        inv = lax.rsqrt(jnp.mean(centered * centered, axis=1, keepdims=True) + EPSILON)
        unit = centered * inv
        unit_ref[...] = unit.astype(bf16)
        inv_ref[...] = jnp.broadcast_to(inv, inv_ref.shape)
        normed = (unit * gain_ref[now, :] + shift_ref[now, :]).astype(bf16)
        normed_ref[...] = normed

        @pl.when(pl.program_id(0) == 0)
        def _():
            for c in assemble_copies(group, shards, own_ref[0], piece_refs, {"a": w_ref}, sems):
                c.wait()

        c, s1, s2 = c_ref[...], s1_ref[...], s2_ref[...]
        q = nn(normed, w_ref[0]) + qkvb_ref[now, :half]
        for j, part in enumerate(spin(q, c, s1, s2)):
            q_ref[:, j * 128 : (j + 1) * 128] = (part * HEAD ** (-0.5)).astype(bf16)
        k = nn(normed, w_ref[1]) + qkvb_ref[now, half : 2 * half]
        for j, part in enumerate(spin(k, c, s1, s2)):
            kv_ref[:, j * 128 : (j + 1) * 128] = part.astype(bf16)
        v = nn(normed, w_ref[2]) + qkvb_ref[now, 2 * half :]
        kv_ref[:, half:] = v.astype(bf16)

    wide = row_blocks(block, width)
    inputs = (
        [(prev, wide)]
        + [(a, wide) for a in adds]
        + [(v, whole(v.shape)) for v in (*biases, gain, shift, qkv_b)]
        + [(t, row_blocks(block, 128)) for t in tables]
        + [(p, ANY) for p in pieces]
    )
    S = jax.ShapeDtypeStruct
    outputs = [
        (S((rows, width), f32), wide),
        (S((rows, width), bf16), wide),
        (S((rows, 128), f32), row_blocks(block, 128)),
        (S((rows, width), bf16), wide),
        (S((rows, half), bf16), row_blocks(block, half)),
        (S((rows, 2 * half), bf16), row_blocks(block, 2 * half)),
    ]
    return call(
        kernel, own, inputs, outputs, (rows // block,),
        [pltpu.VMEM((3, width, half), bf16), pltpu.SemaphoreType.DMA((len(plan),))],
        flops=2 * rows * width * 3 * half, bytes_=rows * width * 12 + 3 * width * half * 2,
    )


def gelu_parts(x):
    z = jnp.abs(x) * math.sqrt(0.5)
    t = 1.0 / (1.0 + 0.3275911 * z)
    poly = t * (
        0.254829592 + t * (-0.284496736 + t * (1.421413741 + t * (-1.453152027 + t * 1.061405429)))
    )
    e = jnp.exp(-0.5 * x * x)
    tail = 0.5 * poly * e
    big = jnp.where(x >= 0, 1.0 - tail, tail)
    return x * big, big + x * e * (1.0 / math.sqrt(2.0 * math.pi))


def forward_up(own, layer, normed, up_b, pieces, group, shards, block=256):
    rows, width = normed.shape
    count = len(pieces)
    plan = assembly(group, shards)
    chunks = len(group.blocks)

    def kernel(own_ref, x_ref, b_ref, *rest):
        piece_refs, rest = rest[:count], rest[count:]
        act_ref, slope_ref, w_ref, sems = rest

        @pl.when(pl.program_id(0) == 0)
        def _():
            copies = assemble_copies(group, shards, own_ref[0], piece_refs, {"u": w_ref}, sems)
            for c in copies:
                c.start()
            for c in copies:
                c.wait()

        for j in range(chunks):
            at = slice(j * COLS, (j + 1) * COLS)
            pre = nn(x_ref[...], w_ref[j]) + b_ref[layer : layer + 1, at]
            act, slope = gelu_parts(pre)
            act_ref[:, at] = act.astype(bf16)
            slope_ref[:, at] = slope.astype(bf16)

    S = jax.ShapeDtypeStruct
    ff = chunks * COLS
    out = (S((rows, ff), bf16), row_blocks(block, ff))
    return call(
        kernel, own,
        [(normed, row_blocks(block, width)), (up_b, whole(up_b.shape))] + [(p, ANY) for p in pieces],
        [out, out], (rows // block,),
        [pltpu.VMEM((chunks, width, COLS), bf16), pltpu.SemaphoreType.DMA((len(plan),))],
        flops=4 * rows * width * ff, bytes_=rows * ff * 4 + width * ff * 2 + rows * width * 2,
    )


def forward_out(own, attended, activated, pieces, group, shards, block=256):
    rows, ff = activated.shape
    half = attended.shape[1]
    count = len(pieces)
    plan = assembly(group, shards)
    width = 2 * COLS

    def kernel(own_ref, att_ref, act_ref, *rest):
        piece_refs, rest = rest[:count], rest[count:]
        out_ref, d_ref, o_ref, sems = rest

        @pl.when(pl.program_id(0) == 0)
        def _():
            copies = assemble_copies(
                group, shards, own_ref[0], piece_refs, {"d": d_ref, "o": o_ref}, sems
            )
            for c in copies:
                c.start()
            for c in copies:
                c.wait()

        for j in range(2):
            got = nn(att_ref[...], o_ref[j]) + nn(act_ref[...], d_ref[j])
            out_ref[:, j * COLS : (j + 1) * COLS] = got.astype(bf16)

    S = jax.ShapeDtypeStruct
    return call(
        kernel, own,
        [(attended, row_blocks(block, half)), (activated, row_blocks(block, ff))]
        + [(p, ANY) for p in pieces],
        [(S((rows, width), bf16), row_blocks(block, width))], (rows // block,),
        [
            pltpu.VMEM((2, ff, COLS), bf16),
            pltpu.VMEM((2, half, COLS), bf16),
            pltpu.SemaphoreType.DMA((len(plan),)),
        ],
        flops=2 * rows * width * (ff + half), bytes_=(rows + width) * (ff + half) * 2 + rows * width * 2,
    )[0]


def attend(meta, q, kv, halo, doc_start, block=256):
    rows, width = q.shape
    reach = halo.shape[0]
    heads = width // HEAD

    def kernel(meta_ref, q_ref, kv_ref, halo_ref, ds_ref, out_ref, lse_ref, ext_ref, bias_ref, sems):
        b = pl.program_id(0)

        @pl.when(b == 0)
        def _():
            one = pltpu.make_async_copy(halo_ref, ext_ref.at[pl.ds(0, reach), :], sems.at[0])
            two = pltpu.make_async_copy(kv_ref, ext_ref.at[pl.ds(reach, rows), :], sems.at[1])
            one.start()
            two.start()
            one.wait()
            two.wait()

        def variant(skip):
            count = (reach // block + 1 - skip) * block
            first = pl.multiple_of((b + skip) * block, block)
            key = first - reach + lax.broadcasted_iota(jnp.int32, (block, count), 1)
            query = b * block + lax.broadcasted_iota(jnp.int32, (block, count), 0)
            allowed = (key <= query) & (key >= ds_ref[...])
            bias_ref[:, :count] = jnp.where(allowed, 0.0, NEG_FILL)
            lane = lax.broadcasted_iota(jnp.int32, (block, 128), 1)
            lse = jnp.zeros((block, 128), f32)
            for p in range(width // 128):
                q2 = q_ref[:, p * 128 : (p + 1) * 128]
                k2 = ext_ref[pl.ds(first, count), p * 128 : (p + 1) * 128]
                v2 = ext_ref[pl.ds(first, count), width + p * 128 : width + (p + 1) * 128]
                outs = []
                for side in range(2):
                    mine = (lane < HEAD) if side == 0 else (lane >= HEAD)
                    s = nt(jnp.where(mine, q2, jnp.zeros_like(q2)), k2) + bias_ref[:, :count]
                    top = jnp.max(s, axis=1, keepdims=True)
                    e = jnp.exp(s - top)
                    total = jnp.sum(e, axis=1, keepdims=True)
                    outs.append(nn(e.astype(bf16), v2) / total)
                    lse = jnp.where(lane == 2 * p + side, top + jnp.log(total), lse)
                out_ref[:, p * 128 : (p + 1) * 128] = jnp.where(lane < HEAD, outs[0], outs[1]).astype(bf16)
            lse_ref[...] = jnp.transpose(lse)[:heads]

        for skip in range(reach // block + 1):
            pl.when(meta_ref[b] == skip)(lambda skip=skip: variant(skip))

    S = jax.ShapeDtypeStruct
    return call(
        kernel, meta,
        [
            (q, row_blocks(block, width)), (kv, ANY), (halo, ANY), (doc_start, row_blocks(block, 1)),
        ],
        [
            (S((rows, width), bf16), row_blocks(block, width)),
            (S((heads, rows), f32), pl.BlockSpec((heads, block), lambda i, *_: (0, i))),
        ],
        (rows // block,),
        [
            pltpu.VMEM((rows + reach, 2 * width), bf16),
            pltpu.VMEM((block, reach + block), f32),
            pltpu.SemaphoreType.DMA((2,)),
        ],
        flops=8 * rows * 2 * reach * width, bytes_=(rows + reach) * width * 8,
    )


def attend_back(meta, q, kv, halo, doc_start_row, grad, attended, lse, tables, block=256):
    rows, width = q.shape
    reach = halo.shape[0]
    heads = width // HEAD
    steps = rows // block

    def kernel(meta_ref, q_ref, kv_ref, halo_ref, ds_ref, g_ref, o_ref, lse_ref, c_ref, s1_ref, s2_ref,
               dq_ref, dkv_ref, ext_ref, acc_ref, bias_ref, sems):
        b = pl.program_id(0)

        @pl.when(b == 0)
        def _():
            one = pltpu.make_async_copy(halo_ref, ext_ref.at[pl.ds(0, reach), :], sems.at[0])
            two = pltpu.make_async_copy(kv_ref, ext_ref.at[pl.ds(reach, rows), :], sems.at[1])
            one.start()
            two.start()
            acc_ref[...] = jnp.zeros_like(acc_ref)
            one.wait()
            two.wait()

        def variant(skip):
            count = (reach // block + 1 - skip) * block
            first = pl.multiple_of((b + skip) * block, block)
            key = first - reach + lax.broadcasted_iota(jnp.int32, (count, block), 0)
            query = b * block + lax.broadcasted_iota(jnp.int32, (count, block), 1)
            allowed = (key <= query) & (key >= ds_ref[...])
            bias_ref[:count, :] = jnp.where(allowed, 0.0, NEG_FILL)
            lane = lax.broadcasted_iota(jnp.int32, (block, 128), 1)
            wide_lane = lax.broadcasted_iota(jnp.int32, (count, 128), 1)
            for p in range(width // 128):
                at = slice(p * 128, (p + 1) * 128)
                q2, g2 = q_ref[:, at], g_ref[:, at]
                k2 = ext_ref[pl.ds(first, count), at]
                v2 = ext_ref[pl.ds(first, count), width + p * 128 : width + (p + 1) * 128]
                prod = jnp.transpose(g2.astype(f32) * o_ref[:, at].astype(f32))
                dk = dv = dq = None
                for side in range(2):
                    mine = (lane < HEAD) if side == 0 else (lane >= HEAD)
                    qm = jnp.where(mine, q2, jnp.zeros_like(q2))
                    gm = jnp.where(mine, g2, jnp.zeros_like(g2))
                    km = jnp.where((wide_lane < HEAD) if side == 0 else (wide_lane >= HEAD), k2, jnp.zeros_like(k2))
                    h = 2 * p + side
                    delta = jnp.sum(prod[side * HEAD : (side + 1) * HEAD], axis=0, keepdims=True)
                    prob = jnp.exp(nt(k2, qm) + bias_ref[:count, :] - lse_ref[h : h + 1, :])
                    ds = (prob * (nt(v2, gm) - delta)).astype(bf16)
                    one_dv = nn(prob.astype(bf16), gm)
                    one_dk = nn(ds, qm)
                    one_dq = lax.dot_general(ds, km, (((0,), (0,)), ((), ())), preferred_element_type=f32)
                    dv = one_dv if dv is None else dv + one_dv
                    dk = one_dk if dk is None else dk + one_dk
                    dq = one_dq if dq is None else dq + one_dq
                acc_ref[pl.ds(first, count), at] += dk
                acc_ref[pl.ds(first, count), width + p * 128 : width + (p + 1) * 128] += dv
                turned = spin(dq * HEAD ** (-0.5), c_ref[...], -s1_ref[...], -s2_ref[...])
                dq_ref[:, at] = turned[0].astype(bf16)

        for skip in range(reach // block + 1):
            pl.when(meta_ref[b] == skip)(lambda skip=skip: variant(skip))

        @pl.when(b == steps - 1)
        def _():
            dkv_ref[...] = acc_ref[...].astype(bf16)

    S = jax.ShapeDtypeStruct
    narrow = row_blocks(block, width)
    return call(
        kernel, meta,
        [
            (q, narrow), (kv, ANY), (halo, ANY),
            (doc_start_row, pl.BlockSpec((1, block), lambda i, *_: (0, i))),
            (grad, narrow), (attended, narrow),
            (lse, pl.BlockSpec((heads, block), lambda i, *_: (0, i))),
        ]
        + [(t, row_blocks(block, 128)) for t in tables],
        [
            (S((rows, width), bf16), narrow),
            (S((rows + reach, 2 * width), bf16), whole((rows + reach, 2 * width))),
        ],
        (steps,),
        [
            pltpu.VMEM((rows + reach, 2 * width), bf16),
            pltpu.VMEM((rows + reach, 2 * width), f32),
            pltpu.VMEM((reach + block, block), f32),
            pltpu.SemaphoreType.DMA((2,)),
        ],
        flops=20 * rows * 2 * reach * width, bytes_=(rows + reach) * width * 12,
    )


def backward_branch(own, branch, slope, pieces, group, shards, block=256):
    rows, width = branch.shape
    ff = slope.shape[1]
    half = COLS
    count = len(pieces)
    plan = assembly(group, shards)

    def kernel(own_ref, g_ref, slope_ref, *rest):
        piece_refs, rest = rest[:count], rest[count:]
        pre_ref, att_ref, presum_ref, gsum_ref, d_ref, o_ref, sems = rest
        i = pl.program_id(0)

        @pl.when(i == 0)
        def _():
            copies = assemble_copies(
                group, shards, own_ref[0], piece_refs, {"d": d_ref, "o": o_ref}, sems
            )
            for c in copies:
                c.start()
            presum_ref[...] = jnp.zeros_like(presum_ref)
            gsum_ref[...] = jnp.zeros_like(gsum_ref)
            for c in copies:
                c.wait()

        parts = [g_ref[:, j * COLS : (j + 1) * COLS] for j in range(2)]
        att_ref[...] = (nt(parts[0], o_ref[0]) + nt(parts[1], o_ref[1])).astype(bf16)
        for j in range(ff // COLS):
            at = slice(j * COLS, (j + 1) * COLS)
            got = nt(parts[0], d_ref[0, at, :]) + nt(parts[1], d_ref[1, at, :])
            pre = (got * slope_ref[:, at].astype(f32)).astype(bf16)
            pre_ref[:, at] = pre
            presum_ref[:, at] += jnp.sum(pre.astype(f32), axis=0, keepdims=True)

        core = own_ref[1]
        mine = (i * block // (rows // 2)) == core

        @pl.when(mine)
        def _():
            gsum_ref[...] += jnp.sum(g_ref[...].astype(f32), axis=0, keepdims=True)

    S = jax.ShapeDtypeStruct
    return call(
        kernel, own,
        [(branch, row_blocks(block, width)), (slope, row_blocks(block, ff))] + [(p, ANY) for p in pieces],
        [
            (S((rows, ff), bf16), row_blocks(block, ff)),
            (S((rows, half), bf16), row_blocks(block, half)),
            (S((1, ff), f32), whole((1, ff))),
            (S((1, width), f32), whole((1, width))),
        ],
        (rows // block,),
        [
            pltpu.VMEM((2, ff, COLS), bf16),
            pltpu.VMEM((2, half, COLS), bf16),
            pltpu.SemaphoreType.DMA((len(plan),)),
        ],
        flops=2 * rows * width * (ff + half), bytes_=(2 * rows + width) * (ff + half) * 2 + rows * width * 2,
    )


def backward_normed(own, dq, dkv, halo, pre_grad, unit, tables, a_pieces, u_pieces, a_group, u_group, shards, block=256):
    rows, half = dq.shape
    width, ff = unit.shape[1], pre_grad.shape[1]
    reach = halo.shape[0]
    steps, late = rows // block, (rows - reach) // block
    na, nu = len(a_pieces), len(u_pieces)
    plan_a, plan_u = assembly(a_group, shards), assembly(u_group, shards)

    def kernel(own_ref, dq_ref, dkv_ref, halo_ref, pre_ref, unit_ref, c_ref, s1_ref, s2_ref, *rest):
        a_refs, rest = rest[:na], rest[na:]
        u_refs, rest = rest[:nu], rest[nu:]
        packed_ref, part_ref, bsum_ref, gain_ref, shift_ref, a_ref, u_ref, sem_a, sem_u = rest
        i = pl.program_id(0)

        def copies():
            return assemble_copies(a_group, shards, own_ref[0], a_refs, {"a": a_ref}, sem_a) + assemble_copies(
                u_group, shards, own_ref[0], u_refs, {"u": u_ref}, sem_u
            )

        @pl.when(i == 0)
        def _():
            for c in copies():
                c.start()
            for ref in (bsum_ref, gain_ref, shift_ref):
                ref[...] = jnp.zeros_like(ref)

        dkv_now = dkv_ref[...].astype(f32) + jnp.where(i >= late, halo_ref[...].astype(f32), 0.0)
        packed_ref[:, :half] = dq_ref[...]
        for j, part in enumerate(spin(dkv_now[:, :half], c_ref[...], -s1_ref[...], -s2_ref[...])):
            packed_ref[:, half + j * 128 : half + (j + 1) * 128] = part.astype(bf16)
        packed_ref[:, 2 * half :] = dkv_now[:, half:].astype(bf16)

        @pl.when(i == 0)
        def _():
            for c in copies():
                c.wait()

        bsum_ref[...] += jnp.sum(packed_ref[...].astype(f32), axis=0, keepdims=True)
        for n in range(width // COLS):
            at = slice(n * COLS, (n + 1) * COLS)
            total = None
            for j in range(3):
                got = nt(packed_ref[:, j * COLS : (j + 1) * COLS], a_ref[j, at, :])
                total = got if total is None else total + got
            for j in range(ff // COLS):
                total += nt(pre_ref[:, j * COLS : (j + 1) * COLS], u_ref[j, at, :])
            part_ref[:, at] = total.astype(bf16)
            gain_ref[:, at] += jnp.sum(total * unit_ref[:, at].astype(f32), axis=0, keepdims=True)
            shift_ref[:, at] += jnp.sum(total, axis=0, keepdims=True)

    S = jax.ShapeDtypeStruct
    skip = reach // block
    return call(
        kernel, own,
        [
            (dq, row_blocks(block, half)),
            (dkv, pl.BlockSpec((block, 2 * half), lambda i, *_: (i + skip, 0))),
            (halo, pl.BlockSpec((block, 2 * half), lambda i, *_: (jnp.maximum(i - late, 0), 0))),
            (pre_grad, row_blocks(block, ff)),
            (unit, row_blocks(block, width)),
        ]
        + [(t, row_blocks(block, 128)) for t in tables]
        + [(p, ANY) for p in (*a_pieces, *u_pieces)],
        [
            (S((rows, 3 * half), bf16), row_blocks(block, 3 * half)),
            (S((rows, width), bf16), row_blocks(block, width)),
            (S((1, 3 * half), f32), whole((1, 3 * half))),
            (S((1, width), f32), whole((1, width))),
            (S((1, width), f32), whole((1, width))),
        ],
        (steps,),
        [
            pltpu.VMEM((3, width, COLS), bf16),
            pltpu.VMEM((ff // COLS, width, COLS), bf16),
            pltpu.SemaphoreType.DMA((len(plan_a),)),
            pltpu.SemaphoreType.DMA((len(plan_u),)),
        ],
        flops=2 * rows * width * (ff + 3 * half), bytes_=(rows + width) * (ff + 3 * half) * 2 + rows * width * 4,
    )


def norm_backward(own, layer, grad, parts, unit, inv, gain, block=256):
    rows, width = unit.shape

    def kernel(own_ref, g_ref, p0_ref, p1_ref, unit_ref, inv_ref, gain_ref, new_ref, low_ref):
        u = (p0_ref[...].astype(f32) + p1_ref[...].astype(f32)) * gain_ref[layer : layer + 1, :]
        unit = unit_ref[...].astype(f32)
        new = g_ref[...].astype(f32) + inv_ref[:, :1] * (
            u - jnp.mean(u, axis=1, keepdims=True) - unit * jnp.mean(u * unit, axis=1, keepdims=True)
        )
        new_ref[...] = new
        low_ref[...] = new.astype(bf16)

    S = jax.ShapeDtypeStruct
    wide = row_blocks(block, width)
    return call(
        kernel, own,
        [(grad, wide), (parts[0], wide), (parts[1], wide), (unit, wide), (inv, row_blocks(block, 128)),
         (gain, whole(gain.shape))],
        [(S((rows, width), f32), wide), (S((rows, width), bf16), wide)],
        (rows // block,), bytes_=rows * width * 16, flops=rows * width * 10,
    )


def weight_grads(own, lefts, rights, extra, group, shards):
    rows = rights.shape[0]
    blocks = rights.shape[1] // COLS
    ks = [l.shape[1] // shards for l in lefts]
    height = sum(ks)
    n_left = len(lefts)
    extra_rows = 0 if extra is None else extra.shape[0] // shards
    rounds, _ = sum_rounds(shards)
    size = [hi - lo for lo, hi in (group.cut(0), group.cut(1))]
    parts = {}
    shapes = [(group.rows, COLS)]
    parts[0] = [(0, 0, 0, group.rows)]
    for i, keys in enumerate(rounds.values()):
        at = 0
        for r, h in keys:
            parts.setdefault(r, []).append((i + 1, at) + group.cut(h))
            at += size[h]
        shapes.append((at, COLS))

    def kernel(own_ref, *refs):
        left_refs, rest = refs[:n_left], refs[n_left:]
        right_ref, rest = rest[0], rest[1:]
        extra_ref, rest = (None, rest) if extra is None else (rest[0], rest[1:])
        out_refs, flipped = rest[: len(shapes)], rest[len(shapes) :]
        for l, t in zip(left_refs, flipped):
            t[...] = jnp.transpose(l[...])

        def store(r, start, value):
            for i, at, lo, hi in parts[r]:
                first, last = max(lo, start), min(hi, start + value.shape[0])
                if first < last:
                    out_refs[i][at + first - lo : at + last - lo, :] = value[first - start : last - start]

        for r in range(shards):
            s = lax.bitwise_xor(own_ref[0], r)
            for j in range(blocks):
                start = j * height
                right = right_ref[:, j * COLS : (j + 1) * COLS]
                for t, k in zip(flipped, ks):
                    left = t[pl.ds(pl.multiple_of(s * k, k), k), :]
                    store(r, start, nn(left, right).astype(bf16))
                    start += k
            if extra is not None:
                store(r, height * blocks, extra_ref[pl.ds(pl.multiple_of(s * extra_rows, extra_rows), extra_rows), :].astype(bf16))

    S = jax.ShapeDtypeStruct
    extras = [] if extra is None else [extra]
    inputs = [(a, whole(a.shape)) for a in (*lefts, rights, *extras)]
    return call(
        kernel, own, inputs, [(S(s, bf16), whole(s)) for s in shapes], (1,),
        [pltpu.VMEM((l.shape[1], rows), bf16) for l in lefts],
    )


def pick(core, first, second):
    return jnp.where(core == 0, first, second)


def vector_places(widths):
    places, row, column = {}, 0, 0
    for name, (layers, width) in widths.items():
        places[name] = []
        for _ in range(layers):
            parts, done = [], 0
            while done < width:
                take = min(COLS - column, width - done)
                parts.append((row, column, take, done))
                done += take
                column += take
                if column == COLS:
                    row, column = row + 1, 0
            places[name].append(parts)
    return places


def pack_qkv(own, weight, layer, group, shards, vectors=None):
    _, rows, columns = weight.shape
    w = columns // (6 * shards)
    halves = [(0, group.rows)]
    names = [] if vectors is None else list(vectors)
    places = vector_places({n: vectors[n].shape for n in names})

    def kernel(own_ref, w_ref, *rest):
        vec_refs, rest = rest[: len(names)], rest[len(names) :]
        out_refs = rest[:1]
        core = own_ref[1]
        if names:
            tmp = rest[1]
            tmp[...] = jnp.zeros_like(tmp)
            for n, ref in zip(names, vec_refs):
                for l, parts in enumerate(places[n]):
                    for row, column, take, first in parts:
                        tmp[row : row + 1, column : column + take] = ref[l : l + 1, first : first + take].astype(f32)
            store_rows(out_refs, halves, 3 * rows, tmp[...].astype(bf16))
        for g in range(3):
            parts = []
            for s in range(shards):
                at = (g * shards + s) * 2 * w
                parts.append(pick(core, w_ref[0, :, at : at + w], w_ref[0, :, at + w : at + 2 * w]))
            store_rows(out_refs, halves, g * rows, jnp.concatenate(parts, axis=1))

    return call(
        kernel, own,
        [(weight, pl.BlockSpec((1, rows, columns), lambda i, *_: (layer, 0, 0)))]
        + [(vectors[n], whole(vectors[n].shape)) for n in names],
        piece_output(group), (1,),
        [pltpu.VMEM((16, COLS), f32)] if names else [], bytes_=rows * columns * 3,
    )


def whole_vectors(own, pieces, group, first, widths, shards, kinds):
    ranges = piece_ranges(group, shards)
    takes = [(a, r, first - lo) for a, (r, lo, hi) in enumerate(ranges) if lo <= first and first + 16 <= hi]
    names = list(widths)
    places = vector_places(widths)

    def kernel(own_ref, *refs):
        piece_refs, rest = refs[: len(takes)], refs[len(takes) :]
        out_refs, (all_ref, sems) = rest[: len(names)], rest[len(names) :]
        core = own_ref[1]
        copies = []
        for i, ((_, r, at), ref) in enumerate(zip(takes, piece_refs)):
            copies.append(
                pltpu.make_async_copy(
                    ref.at[pl.ds(at, 16), :], all_ref.at[lax.bitwise_xor(own_ref[0], r)], sems.at[i]
                )
            )
        for c in copies:
            c.start()
        for c in copies:
            c.wait()
        rows = [all_ref[s].astype(f32) for s in range(shards)]

        def piece_of(name, l, lo, hi):
            width = widths[name][1]
            s = lo // width
            lo, hi = lo - s * width, hi - s * width
            got = []
            for row, column, take, start in places[name][l]:
                a, b = max(lo, start), min(hi, start + take)
                if a < b:
                    got.append(rows[s][row : row + 1, column + a - start : column + b - start])
            return got[0] if len(got) == 1 else jnp.concatenate(got, axis=1)

        for name, ref in zip(names, out_refs):
            layers, width = widths[name]
            for l in range(layers):
                if not kinds[name]:
                    for s in range(shards):
                        ref[l : l + 1, s * width : (s + 1) * width] = piece_of(name, l, s * width, (s + 1) * width)
                    continue
                blocks = kinds[name] * shards
                w = width * shards // (2 * blocks)
                for b in range(blocks):
                    ref[l : l + 1, b * w : (b + 1) * w] = pick(
                        core, piece_of(name, l, 2 * b * w, (2 * b + 1) * w),
                        piece_of(name, l, (2 * b + 1) * w, (2 * b + 2) * w),
                    )

    outs = []
    for n in names:
        shape = (8, widths[n][1] * shards // (2 if kinds[n] else 1))
        outs.append((jax.ShapeDtypeStruct(shape, f32), whole(shape)))
    return call(
        kernel, own, [(pieces[a], ANY) for a, _, _ in takes], outs, (1,),
        [pltpu.VMEM((shards, 16, COLS), bf16), pltpu.SemaphoreType.DMA((len(takes),))], bytes_=shards * 16 * COLS * 2,
    )


def piece_output(group):
    shape = (group.rows, COLS)
    return [(jax.ShapeDtypeStruct(shape, bf16), whole(shape))]


def pack_up(own, weight, layer, group, shards):
    _, rows, columns = weight.shape
    w = columns // (2 * shards)
    halves = [(0, group.rows)]

    def kernel(own_ref, w_ref, *out_refs):
        core = own_ref[1]
        for j in range(columns // 2 // COLS):
            parts = []
            for s in range(j * COLS // w, (j + 1) * COLS // w):
                at = s * 2 * w
                parts.append(pick(core, w_ref[0, :, at : at + w], w_ref[0, :, at + w : at + 2 * w]))
            value = parts[0] if len(parts) == 1 else jnp.concatenate(parts, axis=1)
            store_rows(out_refs, halves, j * rows, value)

    return call(
        kernel, own,
        [(weight, pl.BlockSpec((1, rows, columns), lambda i, *_: (layer, 0, 0)))],
        piece_output(group), (1,), bytes_=rows * columns * 3,
    )


def pack_out(own, down, out, layer, group):
    halves = [(0, group.rows)]
    dr, orows = down.shape[1] // 2, out.shape[1] // 2
    width = down.shape[2]
    blocks = width // COLS

    def kernel(own_ref, d_ref, o_ref, *out_refs):
        for j in range(blocks):
            at = slice(j * COLS, (j + 1) * COLS)
            base = j * (dr + orows)
            store_rows(out_refs, halves, base, d_ref[0, :, at])
            store_rows(out_refs, halves, base + dr, o_ref[0, :, at])

    spec = lambda r: pl.BlockSpec((1, r, width), lambda i, own_ref: (layer, own_ref[1], 0))
    return call(
        kernel, own, [(down, spec(dr)), (out, spec(orows))],
        piece_output(group), (1,), bytes_=(dr + orows) * width * 4,
    )


def read_rows(refs, lo, hi):
    got, start = [], 0
    for ref in refs:
        first, last = max(lo, start), min(hi, start + ref.shape[0])
        if first < last:
            got.append(ref[first - start : last - start, :])
        start += ref.shape[0]
    return got[0] if len(got) == 1 else jnp.concatenate(got)


def unpack_columns(own, mine, theirs, before, layer, layers, rows, kinds, w, shards):
    columns = kinds * shards * 2 * w

    n = len(mine)

    def kernel(own_ref, *refs):
        a_refs, b_refs, out_ref = refs[:n], refs[n : 2 * n], refs[-1]
        core = own_ref[1]
        for j in range(kinds * shards * w // COLS):
            a_block = read_rows(a_refs, j * rows, (j + 1) * rows)
            b_block = read_rows(b_refs, j * rows, (j + 1) * rows)
            for c in range(j * COLS, (j + 1) * COLS, w):
                off = c % COLS
                a = a_block[:, off : off + w].astype(f32)
                b = b_block[:, off : off + w].astype(f32)
                out_ref[0, :, 2 * c : 2 * c + w] = pick(core, a, b)
                out_ref[0, :, 2 * c + w : 2 * c + 2 * w] = pick(core, b, a)

    extra = [] if before is None else [(before, ANY)]
    return call(
        kernel, own, [(v, whole(v.shape)) for v in (*mine, *theirs)] + extra,
        [(jax.ShapeDtypeStruct((layers, rows, columns), f32),
          pl.BlockSpec((1, rows, columns), lambda i, *_: (layer, 0, 0)))],
        (1,), aliases={} if before is None else {1 + 2 * n: 0}, bytes_=rows * columns * 6,
    )[0]


def unpack_rows(own, mine, theirs, befores, layer, layers, heights, width):
    blocks = width // COLS
    total = sum(heights)

    n = len(mine)

    def kernel(own_ref, *refs):
        a_refs, b_refs, out_refs = refs[:n], refs[n : 2 * n], refs[-len(heights) :]
        core = own_ref[1]
        for j in range(blocks):
            start = j * total
            for h, ref in zip(heights, out_refs):
                a = read_rows(a_refs, start, start + h).astype(f32)
                b = read_rows(b_refs, start, start + h).astype(f32)
                ref[0, :h, j * COLS : (j + 1) * COLS] = pick(core, a, b)
                ref[0, h:, j * COLS : (j + 1) * COLS] = pick(core, b, a)
                start += h

    extra = [] if befores is None else [(b, ANY) for b in befores]
    return call(
        kernel, own, [(v, whole(v.shape)) for v in (*mine, *theirs)] + extra,
        [(jax.ShapeDtypeStruct((layers, 2 * h, width), f32),
          pl.BlockSpec((1, 2 * h, width), lambda i, *_: (layer, 0, 0))) for h in heights],
        (1,), aliases={} if befores is None else {1 + 2 * n + i: i for i in range(len(heights))},
        bytes_=total * width * 12,
    )


class Net:
    def __init__(self, shards, reps):
        self.shards, self.reps = shards, reps
        self.bits = [1 << b for b in range(shards.bit_length() - 1)]
        self.chips = reps // 2
        self.shard = lax.axis_index("shard")
        self.rep = lax.axis_index("rep")
        self.core = self.rep % 2
        self.chip = self.rep // 2

    def send(self, value, where):
        pairs = []
        for s in range(self.shards):
            for r in range(self.reps):
                to = where(s, r)
                if to is not None:
                    pairs.append((s * self.reps + r, to[0] * self.reps + to[1]))
        return lax.ppermute(value, AXES, pairs)

    def other_core(self, value):
        return self.send(value, lambda s, r: (s, r ^ 1))

    def flip(self, value, bit):
        return self.send(value, lambda s, r: (s ^ bit, r))

    def next_chip(self, value):
        return self.send(value, lambda s, r: (s, r + 2) if r + 2 < self.reps else None)

    def last_chip(self, value):
        return self.send(value, lambda s, r: (s, r - 2) if r >= 2 else None)

    def chip_steps(self):
        chips = self.chips
        line = 4 if chips % 4 == 0 else 1
        steps = []
        if line == 4:
            at = self.chip % 4

            def inward(s, r):
                z = (r // 2) % 4
                return (s, r + 2) if z == 0 else (s, r - 2) if z == 3 else None

            def across(s, r):
                z = (r // 2) % 4
                return (s, r + 2) if z == 1 else (s, r - 2) if z == 2 else None

            def outward(s, r):
                z = (r // 2) % 4
                return (s, r - 2) if z == 1 else (s, r + 2) if z == 2 else None

            steps += [(inward, None), (across, None), (outward, (at == 0) | (at == 3))]
        step = line
        while step < chips:
            steps.append((lambda s, r, step=step: (s, r ^ (2 * step)), None))
            step *= 2
        return steps


class Clock:
    def __init__(self):
        self.last = None

    def tie(self, value):
        if self.last is None:
            return value
        return lax.optimization_barrier((value, self.last))[0]

    def mark(self, value):
        self.last = value


class Gather:
    def __init__(self, net, group, own):
        self.net, self.group, self.own = net, group, own[0]

    def near(self, clock):
        own = clock.tie(self.own)
        clock.mark(own)
        self.pieces = {0: [own]}
        for bit in self.net.bits:
            self.pieces[bit] = [self.net.flip(own, bit)]

    def far(self, clock):
        net, bits = self.net, self.net.bits
        for bit, came in zip(bits, clock.tie(tuple(self.pieces[bit][0] for bit in bits))):
            self.pieces[bit] = [came]
        got, parts = [], []
        for r, lo, hi in piece_ranges(self.group, net.shards):
            if bin(r).count("1") <= 1:
                got.append(self.pieces[r][0])
                continue
            half = 0 if lo == 0 else 1
            bit = last_bit(net.shards, r, half)
            source = self.pieces[r ^ bit]
            part = source[half] if len(source) == 2 else source[0][lo:hi]
            parts.append(part)
            self.pieces.setdefault(r, []).append(net.flip(part, bit))
            got.append(self.pieces[r][-1])
        clock.mark(tuple(parts))
        self.arrays = got

    def arrived(self, clock):
        self.arrays = list(clock.tie(tuple(self.arrays)))
        clock.mark(tuple(self.arrays[-2:]))


def sum_low(values):
    total = values[0].astype(f32)
    for v in values[1:]:
        total = total + v.astype(f32)
    return total.astype(bf16)


class Reduce:
    def __init__(self, net, clock, group, arrays, apart):
        self.at = None
        self.steps = self.run(net, clock, group, arrays, apart)

    def step(self, name):
        while self.at != name:
            self.at = next(self.steps)

    def run(self, net, clock, group, arrays, apart):
        rounds, goes = sum_rounds(net.shards)
        last = max(d for d, _ in rounds)
        cuts = [group.cut(h) for h in range(2)]
        size = [hi - lo for lo, hi in cuts]
        own = arrays[0]
        held = dict(zip(rounds, arrays[1:]))
        came = {}
        for now in range(last + 1):
            sent = {}
            for (d, bit), keys in rounds.items():
                if d != now:
                    continue
                value = held[d, bit]
                if any(k in came for k in keys):
                    parts, at = [], 0
                    for r, h in keys:
                        mine = value if len(keys) == 1 else value[at : at + size[h]]
                        parts.append(sum_low([mine] + came.get((r, h), [])))
                        at += size[h]
                    value = parts[0] if len(parts) == 1 else jnp.concatenate(parts)
                    clock.mark(value)
                sent[d, bit] = net.flip(value, bit)
            yield "r0" if now == 0 else "r1" if now == last else None
            sent = clock.tie(sent)
            for key, value in sent.items():
                at = 0
                for r, h in rounds[key]:
                    part = value if len(rounds[key]) == 1 else value[at : at + size[h]]
                    came.setdefault(goes[r, h], []).append(part)
                    at += size[h]
        halves = [sum_low([own[lo:hi]] + came[0, h]) for h, (lo, hi) in enumerate(cuts)]
        self.chains = {}
        for name, value in zip("ab", halves) if apart else [("", jnp.concatenate(halves))]:
            clock.mark(value)
            self.chains[name] = ChipSum(net, clock, value)
        yield "r2"


class ChipSum:
    def __init__(self, net, clock, value):
        self.steps = self.run(net, clock, value)
        self.at = next(self.steps)

    def step(self, name):
        while self.at != name:
            self.at = next(self.steps)

    def run(self, net, clock, value):
        for i, (where, replaced) in enumerate(net.chip_steps()):
            came = net.send(value, where)
            yield f"r{2 + i}" if i < 3 else None
            came = clock.tie(came)
            value = sum_low([value, came]) if replaced is None else jnp.where(replaced, came, value)
            clock.mark(value)
        theirs = net.other_core(value)
        yield "r5"
        self.mine, self.theirs = value, clock.tie(theirs)
        clock.mark(self.theirs)
        yield "r6"


ORDER = """
g0a0 docs g1a0 g2a0 g0u0 f10 g1u0 h0 g2u0 g0o0 f20 f30 g1o0 g2o0 g0a1 f40 g1a1 g2a1
g0u1 f11 g1u1 h1 g2u1 g0o1 f21 f31 g1o1 wo1 f41 g2o1 r0o1 bb1 ab1 p1 r1o1 out
wu1 r0u1 r2o1 bn1 wa1 r1u1 nb1 r0a1 r3o1 r2u1 wo0 r1a1 bb0 r3u1 r4o1 r2a1 r0o0 ab0
r4u1 r3a1 r5o1 r1o0 r6o1 p0 wu0 r5u1 r2o0 r6u1 r0u0 r4a1 bn0 r1u0 r3o0 nb0 r2u0 wa0
r0a0 r4o0 r3u0 r1a0 r5a1 r2a0 r4u0 r3a0a r3a0b r4a0a r5o0 r6a1 r4a0b r5a0a r5u0 r6o0 r5a0b r6u0
r6a0
""".split()


def body(
    tokens,
    token_order,
    lengths,
    cotangent,
    norm_gain,
    norm_shift,
    qkv_weight,
    qkv_bias,
    out_weight,
    out_bias,
    up_weight,
    up_bias,
    down_weight,
    down_bias,
):
    net = Net(lax.axis_size("shard"), lax.axis_size("rep"))
    shards, core = net.shards, net.core
    layers = norm_gain.shape[0]
    row_count, width = tokens.shape
    rows = 2 * row_count
    reach = row_count
    block = 256
    piece = width // shards
    ff = up_weight.shape[2] // 2
    group_first = net.shard * row_count * net.reps
    chip_first = net.chip * rows
    own = jnp.stack([net.shard, core]).astype(jnp.int32)
    clock = Clock()

    ff_piece, head_piece = ff // shards, width // 2 // shards
    a_blocks = [(piece, "a", j) for j in range(3)]
    group_a0 = Group(a_blocks, 3 * piece // 2, 16)
    group_a = Group(a_blocks, 3 * piece // 2)
    group_u = Group([(piece, "u", j) for j in range(ff // COLS)], piece * (ff // COLS) // 2)
    group_o = Group(
        [b for j in range(2) for b in ((ff_piece, "d", j), (head_piece, "o", j))], ff_piece + head_piece
    )
    grads_a = Group([(3 * piece + 16, "", 0)], 3 * piece // 2)

    def pair_rows(x):
        other = net.other_core(x)
        return jnp.concatenate([pick(core, x, other), pick(core, other, x)])

    def own_rows(x):
        return lax.dynamic_slice_in_dim(x, core * row_count, row_count)

    small = {
        "gain": norm_gain, "shift": norm_shift, "qkv": qkv_bias, "out": out_bias, "up": up_bias, "down": down_bias
    }
    gathers = []
    for l in range(layers):
        gathers += [
            Gather(net, group_a0 if l == 0 else group_a, pack_qkv(own, qkv_weight, l, group_a if l else group_a0, shards, None if l else small)),
            Gather(net, group_u, pack_up(own, up_weight, l, group_u, shards)),
            Gather(net, group_o, pack_out(own, down_weight, out_weight, l, group_o)),
        ]
    slots = lengths.shape[0]
    before = jnp.arange(slots)[None, :] < jnp.arange(slots)[:, None]
    dealt_start = jnp.sum(jnp.where(before, lengths[None, :], 0), axis=1)
    hit = dealt_start[:, None] == jnp.arange(row_count)[None, :]
    home = jnp.sum(jnp.where(hit, token_order[None, :], 0), axis=1) - group_first
    docs = lax.all_gather(jnp.stack([home, lengths]), "rep", axis=0)
    home, length = docs[:, 0].reshape(-1), docs[:, 1].reshape(-1)
    place = chip_first + jnp.arange(rows, dtype=jnp.int32)
    inside = (home[None, :] <= place[:, None]) & (place[:, None] < (home + length)[None, :])
    doc_start = jnp.sum(jnp.where(inside, home[None, :], 0), axis=1) - chip_first
    earliest = jnp.min(doc_start.reshape(rows // block, block), axis=1)
    meta = jnp.clip((earliest + reach) // block - jnp.arange(rows // block), 0, reach // block)
    meta = meta.astype(jnp.int32)
    start_column, start_row = doc_start[:, None], doc_start[None, :]

    lane = jnp.arange(128) % HEAD
    positions = (jnp.arange(rows, dtype=jnp.int32) - doc_start).astype(f32)
    inverse_freq = jnp.exp((lane % (ROT // 2)).astype(f32) * (-2.0 * math.log(10000.0) / ROT))
    angles = positions[:, None] * inverse_freq[None, :]
    sine = jnp.sin(angles)
    tables = (
        jnp.where(lane < ROT, jnp.cos(angles), 1.0),
        jnp.where(lane < ROT // 2, -sine, 0.0),
        jnp.where((lane >= ROT // 2) & (lane < ROT), sine, 0.0),
    )

    stream0 = pair_rows(tokens)
    branch_top = pair_rows(cotangent)
    top = layers - 1
    at = [dict() for _ in range(layers)]
    sums = {}
    common = {}

    def forward_first(l):
        a = gathers[3 * l]
        if l == 0:
            common["vectors"] = whole_vectors(
                own, a.arrays, group_a0, 3 * piece, {n: v.shape for n, v in small.items()}, shards,
                {"gain": 0, "shift": 0, "qkv": 3, "out": 0, "up": 1, "down": 0},
            )
            before, adds, biases = stream0, [], []
        else:
            before, adds = at[l - 1]["stream"], at[l - 1]["adds"]
            biases = [common["vectors"][3], common["vectors"][5]]
        gains, shifts, qkv_b, _, _, _ = common["vectors"]
        stream, unit, inv, normed, q, kv = forward_qkv(
            own, l, clock.tie(before), adds, biases, gains, shifts, qkv_b, tables, a.arrays, a.group, shards
        )
        clock.mark(q)
        at[l].update(stream=stream, unit=unit, inv=inv, normed=normed, q=q, kv=kv)

    def send_halo(l):
        part = clock.tie(at[l]["kv"])[rows - reach :]
        clock.mark(part)
        at[l]["halo"] = net.next_chip(part)

    def forward_second(l):
        at[l]["activated"], at[l]["slope"] = forward_up(
            own, l, clock.tie(at[l]["normed"]), common["vectors"][4], gathers[3 * l + 1].arrays, group_u, shards
        )
        clock.mark(at[l]["slope"])

    def forward_third(l):
        at[l]["attended"], at[l]["lse"] = attend(
            meta, clock.tie(at[l]["q"]), at[l]["kv"], at[l]["halo"], start_column
        )
        clock.mark(at[l]["lse"])

    def forward_fourth(l):
        partial = forward_out(
            own, clock.tie(at[l]["attended"]), at[l]["activated"], gathers[3 * l + 2].arrays, group_o, shards
        )
        clock.mark(partial)
        at[l]["adds"] = [partial, net.other_core(partial)]

    def branch_of(l):
        return branch_top if l == top else at[l + 1]["branch"]

    def output():
        adds = at[top]["adds"]
        value = own_rows(clock.tie(at[top]["stream"])) + own_rows(adds[0]).astype(f32) + own_rows(adds[1]).astype(f32)
        out_b, down_b = common["vectors"][3], common["vectors"][5]
        common["output"] = (value + out_b[top : top + 1] + down_b[top : top + 1]).astype(bf16)
        clock.mark(common["output"])

    def reduce(name, l, group, lefts, rights, extra=None):
        got = weight_grads(own, [clock.tie(lefts[0])] + lefts[1:], rights, extra, group, shards)
        clock.mark(got[0])
        sums[name, l] = Reduce(net, clock, group, got, name == "a" and l == 0)

    def grads_out(l):
        reduce("o", l, group_o, [at[l]["activated"], at[l]["attended"]], branch_of(l))

    def grads_up(l):
        reduce("u", l, group_u, [at[l]["normed"]], at[l]["pre_grad"])

    def grads_qkv(l):
        qkv_sum = at[l]["qkv_sum"].reshape(3 * shards, 1, -1)
        nothing = jnp.zeros_like(qkv_sum)
        qkv_sum = jnp.concatenate([pick(core, qkv_sum, nothing), pick(core, nothing, qkv_sum)], axis=1)

        def line(v, width):
            v = v.reshape(shards, -1)
            return jnp.pad(v, ((0, 0), (0, width - v.shape[1])))

        extra = jnp.concatenate(
            [
                line(at[l]["gain_sum"], COLS // 2),
                line(at[l]["shift_sum"], COLS // 2),
                line(at[l]["branch_sum"], COLS),
                line(at[l]["up_sum"], COLS),
                line(qkv_sum, 13 * COLS),
            ],
            axis=1,
        ).reshape(shards * 16, COLS)
        reduce("a", l, grads_a, [at[l]["normed"]], at[l]["packed_grad"], extra)

    def backward_first(l):
        pre_grad, attended_grad, up_sum, branch_sum = backward_branch(
            own, clock.tie(branch_of(l)), at[l]["slope"], gathers[3 * l + 2].arrays, group_o, shards
        )
        clock.mark(attended_grad)
        at[l].update(pre_grad=pre_grad, attended_grad=attended_grad, up_sum=up_sum, branch_sum=branch_sum)

    def backward_attention(l):
        d = at[l]
        d["dq"], d["dkv"] = attend_back(
            meta, clock.tie(d["q"]), d["kv"], d["halo"], start_row, d["attended_grad"], d["attended"], d["lse"], tables
        )
        clock.mark(d["dq"])

    def send_halo_back(l):
        part = clock.tie(at[l]["dkv"])[:reach]
        clock.mark(part)
        at[l]["halo_grad"] = net.last_chip(part)

    def backward_norm_in(l):
        d = at[l]
        a = gathers[3 * l]
        d["packed_grad"], part, d["qkv_sum"], d["gain_sum"], d["shift_sum"] = backward_normed(
            own, clock.tie(d["dq"]), d["dkv"], d["halo_grad"], d["pre_grad"], d["unit"], tables,
            a.arrays, gathers[3 * l + 1].arrays, a.group, group_u, shards,
        )
        clock.mark(part)
        d["parts"] = [part, net.other_core(part)]

    def backward_norm(l):
        d = at[l]
        grad = branch_top if l == top else at[l + 1]["grad"]
        d["grad"], d["branch"] = norm_backward(
            own, l, clock.tie(grad), d["parts"], d["unit"], d["inv"], common["vectors"][0]
        )
        clock.mark(d["branch"])

    def finish(name, l):
        chains = [c for _, c in sorted(sums[name, l].chains.items())]
        for c in chains:
            c.step("r6")
        mine, theirs = [c.mine for c in chains], [c.theirs for c in chains]
        if name == "o":
            got = unpack_rows(own, mine, theirs, common.get(name), l, layers, (ff_piece, head_piece), width)
        else:
            kinds, w = (3, head_piece) if name == "a" else (1, ff_piece)
            got = unpack_columns(own, mine, theirs, common.get(name), l, layers, piece, kinds, w, shards)
        common[name] = got
        clock.mark(got)
        if name == "a":
            common["small", l] = mine[-1][-16:], theirs[-1][-16:]

    kernels = {
        "f1": forward_first, "f2": forward_second, "f3": forward_third, "f4": forward_fourth, "h": send_halo,
        "wo": grads_out, "wu": grads_up, "wa": grads_qkv, "bb": backward_first, "ab": backward_attention,
        "p": send_halo_back, "bn": backward_norm_in, "nb": backward_norm,
    }
    others = {"docs": lambda: clock.mark(docs), "out": output}
    for token in ORDER:
        if token in others:
            others[token]()
        elif token[:-1] in kernels:
            kernels[token[:-1]](int(token[-1]))
        else:
            stage, name, l = token[:2], token[2], int(token[3])
            weights = gathers[3 * l + "auo".index(name)]
            if stage == "g0":
                weights.near(clock)
            elif stage == "g1":
                weights.far(clock)
            elif stage == "g2":
                weights.arrived(clock)
            elif stage == "r6":
                finish(name, l)
            elif stage in ("r0", "r1", "r2"):
                sums[name, l].step(stage)
            else:
                sums[name, l].chains[token[4:]].step(stage)
    block_output, input_grad = common["output"], own_rows(at[0]["branch"])
    (down_g, out_g), up_g, qkv_g = common["o"], common["u"], common["a"]
    mine, theirs = (
        jnp.stack([common["small", l][i] for l in range(layers)]).astype(f32) for i in range(2)
    )
    low, high = pick(core, mine, theirs), pick(core, theirs, mine)
    both = low + high
    branch_g = both[:, 1, :piece]
    return (
        block_output,
        input_grad,
        both[:, 0, :piece],
        both[:, 0, COLS // 2 : COLS // 2 + piece],
        qkv_g,
        both[:, 3:5].reshape(layers, -1)[:, : 3 * piece],
        out_g,
        branch_g,
        up_g,
        jnp.concatenate([low[:, 2, :ff_piece], high[:, 2, :ff_piece]], axis=1),
        down_g,
        branch_g,
    )


def solution(mesh):
    rows = P(("shard", "rep"), None)
    vector, matrix = P(None, "shard"), P(None, "shard", None)
    line = P(("shard", "rep"))
    return jax.shard_map(
        body,
        mesh=mesh,
        in_specs=(
            rows, line, line, rows, vector, vector, matrix, vector, matrix, vector,
            matrix, vector, matrix, vector,
        ),
        out_specs=(
            rows, rows, vector, vector, matrix, vector, matrix, vector, matrix, vector,
            matrix, vector,
        ),
        check_vma=False,
    )
```

```python
import math

import jax
import jax.numpy as jnp
from jax import lax
from jax.experimental import pallas as pl
from jax.experimental.pallas import tpu as pltpu
from jax.sharding import PartitionSpec as P

HEADS = 16
HEAD = 64
ROT = 16
EPSILON = 1e-05
NEG_FILL = -1e30
AXES = ("shard", "rep")
bf16 = jnp.bfloat16
f32 = jnp.float32
VMEM_BYTES = 48 * 1024 * 1024
COLS = 512


def nn(a, b):
    return jnp.dot(a, b, preferred_element_type=f32)


def nt(a, b):
    return lax.dot_general(a, b, (((1,), (1,)), ((), ())), preferred_element_type=f32)


def whole(shape):
    return pl.BlockSpec(shape, lambda *_: (0,) * len(shape))


def row_blocks(rows, width):
    return pl.BlockSpec((rows, width), lambda i, *_: (i, 0))


ANY = pl.BlockSpec(memory_space=pl.ANY)


def call(kernel, scalars, inputs, outputs, grid, scratch=(), aliases={}, flops=0, bytes_=0):
    return pl.pallas_call(
        kernel,
        grid_spec=pltpu.PrefetchScalarGridSpec(
            num_scalar_prefetch=1,
            grid=grid,
            in_specs=[s for _, s in inputs],
            out_specs=[s for _, s in outputs],
            scratch_shapes=list(scratch),
        ),
        out_shape=[o for o, _ in outputs],
        input_output_aliases=aliases,
        compiler_params=pltpu.CompilerParams(vmem_limit_bytes=VMEM_BYTES),
        cost_estimate=pl.CostEstimate(flops=1, bytes_accessed=1, transcendentals=0),
    )(scalars, *[a for a, _ in inputs])


class Group:
    def __init__(self, blocks, first_half, extra=0):
        self.blocks = blocks
        self.rows = sum(b[0] for b in blocks) + extra
        self.first_half = first_half

    def cut(self, half):
        return (0, self.first_half) if half == 0 else (self.first_half, self.rows)


def piece_ranges(group, shards):
    ranges = []
    for r in range(shards):
        if bin(r).count("1") > 1:
            ranges += [(r,) + group.cut(0), (r,) + group.cut(1)]
        else:
            ranges.append((r, 0, group.rows))
    return ranges


def hop_bits(shards, half):
    bits = [1 << b for b in range(shards.bit_length() - 1)]
    return bits if half == 0 else bits[::-1]


def last_bit(shards, relative, half):
    return [b for b in hop_bits(shards, half) if relative & b][-1]


def sum_rounds(shards):
    keys = [(r, h) for r in range(1, shards) for h in range(2)]
    goes = {(r, h): (r ^ last_bit(shards, r, h), h) for r, h in keys}
    depth = {}
    for key in sorted(keys, key=lambda k: -bin(k[0]).count("1")):
        before = [depth[k] for k, to in goes.items() if to == key]
        depth[key] = 1 + max(before) if before else 0
    rounds = {}
    for key in sorted(keys, key=lambda k: (depth[k], -bin(k[0]).count("1"), k)):
        rounds.setdefault((depth[key], last_bit(shards, *key)), []).append(key)
    return rounds, goes


def store_rows(refs, halves, start, value):
    for (lo, hi), ref in zip(halves, refs):
        first, last = max(lo, start), min(hi, start + value.shape[0])
        if first < last:
            ref[first - lo : last - lo, :] = value[first - start : last - start]


def assembly(group, shards):
    plan = []
    for a, (r, lo, hi) in enumerate(piece_ranges(group, shards)):
        start = 0
        for rows, key, index in group.blocks:
            first, last = max(lo, start), min(hi, start + rows)
            if first < last:
                plan.append((a, first - lo, last - first, key, index, r, rows, first - start))
            start += rows
    return plan


def assemble_copies(group, shards, own, refs, targets, sems):
    copies = []
    for i, (a, src, rows, key, index, r, per, off) in enumerate(assembly(group, shards)):
        at = pl.multiple_of(lax.bitwise_xor(own, r) * per + off, 16)
        copies.append(
            pltpu.make_async_copy(
                refs[a].at[pl.ds(src, rows), :],
                targets[key].at[index, pl.ds(at, rows), :],
                sems.at[i],
            )
        )
    return copies


def spin(x, c, s1, s2):
    parts = []
    for j in range(x.shape[1] // 128):
        part = x[:, j * 128 : (j + 1) * 128]
        up = pltpu.roll(part, 128 - ROT // 2, 1)
        down = pltpu.roll(part, ROT // 2, 1)
        parts.append(part * c + up * s1 + down * s2)
    return parts


def forward_qkv(own, layer, prev, adds, biases, gain, shift, qkv_b, tables, pieces, group, shards, tail, block=256):
    rows, width = prev.shape
    late = (rows - tail) // block
    count = len(pieces)
    n_add = len(adds)
    plan = assembly(group, shards)
    half = COLS

    def kernel(own_ref, *refs):
        prev_ref, *rest = refs
        add_refs, rest = rest[:n_add], rest[n_add:]
        bias_refs, rest = rest[: len(biases)], rest[len(biases) :]
        gain_ref, shift_ref, qkvb_ref, c_ref, s1_ref, s2_ref, *rest = rest
        now = slice(layer, layer + 1)
        piece_refs, rest = rest[:count], rest[count:]
        stream_ref, unit_ref, inv_ref, normed_ref, q_ref, kv_ref, tail_ref, w_ref, sems = rest

        @pl.when(pl.program_id(0) == 0)
        def _():
            for c in assemble_copies(group, shards, own_ref[0], piece_refs, {"a": w_ref}, sems):
                c.start()

        x = prev_ref[...].astype(f32)
        if n_add:
            for a in add_refs:
                x = x + a[...].astype(f32)
            for b in bias_refs:
                x = x + b[layer - 1 : layer, :]
        stream_ref[...] = x
        mean = jnp.mean(x, axis=1, keepdims=True)
        centered = x - mean
        inv = lax.rsqrt(jnp.mean(centered * centered, axis=1, keepdims=True) + EPSILON)
        unit = centered * inv
        unit_ref[...] = unit.astype(bf16)
        inv_ref[...] = jnp.broadcast_to(inv, inv_ref.shape)
        normed = (unit * gain_ref[now, :] + shift_ref[now, :]).astype(bf16)
        normed_ref[...] = normed

        @pl.when(pl.program_id(0) == 0)
        def _():
            for c in assemble_copies(group, shards, own_ref[0], piece_refs, {"a": w_ref}, sems):
                c.wait()

        c, s1, s2 = c_ref[...], s1_ref[...], s2_ref[...]
        q = nn(normed, w_ref[0]) + qkvb_ref[now, :half]
        for j, part in enumerate(spin(q, c, s1, s2)):
            q_ref[:, j * 128 : (j + 1) * 128] = (part * HEAD ** (-0.5)).astype(bf16)
        k = nn(normed, w_ref[1]) + qkvb_ref[now, half : 2 * half]
        for j, part in enumerate(spin(k, c, s1, s2)):
            kv_ref[:, j * 128 : (j + 1) * 128] = part.astype(bf16)
        v = nn(normed, w_ref[2]) + qkvb_ref[now, 2 * half :]
        kv_ref[:, half:] = v.astype(bf16)

        @pl.when(pl.program_id(0) >= late)
        def _():
            tail_ref[...] = kv_ref[...]

    wide = row_blocks(block, width)
    inputs = (
        [(prev, wide)]
        + [(a, wide) for a in adds]
        + [(v, whole(v.shape)) for v in (*biases, gain, shift, qkv_b)]
        + [(t, row_blocks(block, 128)) for t in tables]
        + [(p, ANY) for p in pieces]
    )
    S = jax.ShapeDtypeStruct
    outputs = [
        (S((rows, width), f32), wide),
        (S((rows, width), bf16), wide),
        (S((rows, 128), f32), row_blocks(block, 128)),
        (S((rows, width), bf16), wide),
        (S((rows, half), bf16), row_blocks(block, half)),
        (S((rows, 2 * half), bf16), row_blocks(block, 2 * half)),
        (S((tail, 2 * half), bf16), pl.BlockSpec((block, 2 * half), lambda i, *_: (jnp.maximum(i - late, 0), 0))),
    ]
    return call(
        kernel, own, inputs, outputs, (rows // block,),
        [pltpu.VMEM((3, width, half), bf16), pltpu.SemaphoreType.DMA((len(plan),))],
        flops=2 * rows * width * 3 * half, bytes_=rows * width * 12 + 3 * width * half * 2,
    )


def gelu_parts(x):
    z = jnp.abs(x) * math.sqrt(0.5)
    t = 1.0 / (1.0 + 0.3275911 * z)
    poly = t * (
        0.254829592 + t * (-0.284496736 + t * (1.421413741 + t * (-1.453152027 + t * 1.061405429)))
    )
    e = jnp.exp(-0.5 * x * x)
    tail = 0.5 * poly * e
    big = jnp.where(x >= 0, 1.0 - tail, tail)
    return x * big, big + x * e * (1.0 / math.sqrt(2.0 * math.pi))


def forward_up(own, layer, normed, up_b, pieces, group, shards, block=256):
    rows, width = normed.shape
    count = len(pieces)
    plan = assembly(group, shards)
    chunks = len(group.blocks)

    def kernel(own_ref, x_ref, b_ref, *rest):
        piece_refs, rest = rest[:count], rest[count:]
        act_ref, slope_ref, w_ref, sems = rest

        @pl.when(pl.program_id(0) == 0)
        def _():
            copies = assemble_copies(group, shards, own_ref[0], piece_refs, {"u": w_ref}, sems)
            for c in copies:
                c.start()
            for c in copies:
                c.wait()

        for j in range(chunks):
            at = slice(j * COLS, (j + 1) * COLS)
            pre = nn(x_ref[...], w_ref[j]) + b_ref[layer : layer + 1, at]
            act, slope = gelu_parts(pre)
            act_ref[:, at] = act.astype(bf16)
            slope_ref[:, at] = slope.astype(bf16)

    S = jax.ShapeDtypeStruct
    ff = chunks * COLS
    out = (S((rows, ff), bf16), row_blocks(block, ff))
    return call(
        kernel, own,
        [(normed, row_blocks(block, width)), (up_b, whole(up_b.shape))] + [(p, ANY) for p in pieces],
        [out, out], (rows // block,),
        [pltpu.VMEM((chunks, width, COLS), bf16), pltpu.SemaphoreType.DMA((len(plan),))],
        flops=4 * rows * width * ff, bytes_=rows * ff * 4 + width * ff * 2 + rows * width * 2,
    )


def forward_out(own, attended, activated, pieces, group, shards, block=256):
    rows, ff = activated.shape
    half = attended.shape[1]
    count = len(pieces)
    plan = assembly(group, shards)
    width = 2 * COLS

    def kernel(own_ref, att_ref, act_ref, *rest):
        piece_refs, rest = rest[:count], rest[count:]
        out_ref, d_ref, o_ref, sems = rest

        @pl.when(pl.program_id(0) == 0)
        def _():
            copies = assemble_copies(
                group, shards, own_ref[0], piece_refs, {"d": d_ref, "o": o_ref}, sems
            )
            for c in copies:
                c.start()
            for c in copies:
                c.wait()

        for j in range(2):
            got = nn(att_ref[...], o_ref[j]) + nn(act_ref[...], d_ref[j])
            out_ref[:, j * COLS : (j + 1) * COLS] = got.astype(bf16)

    S = jax.ShapeDtypeStruct
    return call(
        kernel, own,
        [(attended, row_blocks(block, half)), (activated, row_blocks(block, ff))]
        + [(p, ANY) for p in pieces],
        [(S((rows, width), bf16), row_blocks(block, width))], (rows // block,),
        [
            pltpu.VMEM((2, ff, COLS), bf16),
            pltpu.VMEM((2, half, COLS), bf16),
            pltpu.SemaphoreType.DMA((len(plan),)),
        ],
        flops=2 * rows * width * (ff + half), bytes_=(rows + width) * (ff + half) * 2 + rows * width * 2,
    )[0]


def attend(meta, q, kv, halo, doc_start, block=256):
    rows, width = q.shape
    reach = halo.shape[0]
    heads = width // HEAD

    def kernel(meta_ref, q_ref, kv_ref, halo_ref, ds_ref, out_ref, lse_ref, ext_ref, bias_ref, sems):
        b = pl.program_id(0)

        @pl.when(b == 0)
        def _():
            one = pltpu.make_async_copy(halo_ref, ext_ref.at[pl.ds(0, reach), :], sems.at[0])
            two = pltpu.make_async_copy(kv_ref, ext_ref.at[pl.ds(reach, rows), :], sems.at[1])
            one.start()
            two.start()
            one.wait()
            two.wait()

        def variant(skip):
            count = (reach // block + 1 - skip) * block
            first = pl.multiple_of((b + skip) * block, block)
            key = first - reach + lax.broadcasted_iota(jnp.int32, (block, count), 1)
            query = b * block + lax.broadcasted_iota(jnp.int32, (block, count), 0)
            allowed = (key <= query) & (key >= ds_ref[...])
            bias_ref[:, :count] = jnp.where(allowed, 0.0, NEG_FILL)
            lane = lax.broadcasted_iota(jnp.int32, (block, 128), 1)
            lse = jnp.zeros((block, 128), f32)
            for p in range(width // 128):
                q2 = q_ref[:, p * 128 : (p + 1) * 128]
                k2 = ext_ref[pl.ds(first, count), p * 128 : (p + 1) * 128]
                v2 = ext_ref[pl.ds(first, count), width + p * 128 : width + (p + 1) * 128]
                outs = []
                for side in range(2):
                    mine = (lane < HEAD) if side == 0 else (lane >= HEAD)
                    s = nt(jnp.where(mine, q2, jnp.zeros_like(q2)), k2) + bias_ref[:, :count]
                    top = jnp.max(s, axis=1, keepdims=True)
                    e = jnp.exp(s - top)
                    total = jnp.sum(e, axis=1, keepdims=True)
                    outs.append(nn(e.astype(bf16), v2) / total)
                    lse = jnp.where(lane == 2 * p + side, top + jnp.log(total), lse)
                out_ref[:, p * 128 : (p + 1) * 128] = jnp.where(lane < HEAD, outs[0], outs[1]).astype(bf16)
            lse_ref[...] = jnp.transpose(lse)[:heads]

        for skip in range(reach // block + 1):
            pl.when(meta_ref[b] == skip)(lambda skip=skip: variant(skip))

    S = jax.ShapeDtypeStruct
    return call(
        kernel, meta,
        [
            (q, row_blocks(block, width)), (kv, ANY), (halo, ANY), (doc_start, row_blocks(block, 1)),
        ],
        [
            (S((rows, width), bf16), row_blocks(block, width)),
            (S((heads, rows), f32), pl.BlockSpec((heads, block), lambda i, *_: (0, i))),
        ],
        (rows // block,),
        [
            pltpu.VMEM((rows + reach, 2 * width), bf16),
            pltpu.VMEM((block, reach + block), f32),
            pltpu.SemaphoreType.DMA((2,)),
        ],
        flops=8 * rows * 2 * reach * width, bytes_=(rows + reach) * width * 8,
    )


def attend_back(meta, q, kv, halo, doc_start_row, grad, attended, lse, tables, block=256):
    rows, width = q.shape
    reach = halo.shape[0]
    heads = width // HEAD
    steps = rows // block

    def kernel(meta_ref, q_ref, kv_ref, halo_ref, ds_ref, g_ref, o_ref, lse_ref, c_ref, s1_ref, s2_ref,
               dq_ref, dkv_ref, far_ref, ext_ref, acc_ref, bias_ref, sems):
        b = pl.program_id(0)

        @pl.when(b == 0)
        def _():
            one = pltpu.make_async_copy(halo_ref, ext_ref.at[pl.ds(0, reach), :], sems.at[0])
            two = pltpu.make_async_copy(kv_ref, ext_ref.at[pl.ds(reach, rows), :], sems.at[1])
            one.start()
            two.start()
            acc_ref[...] = jnp.zeros_like(acc_ref)
            one.wait()
            two.wait()

        def variant(skip):
            count = (reach // block + 1 - skip) * block
            first = pl.multiple_of((b + skip) * block, block)
            key = first - reach + lax.broadcasted_iota(jnp.int32, (count, block), 0)
            query = b * block + lax.broadcasted_iota(jnp.int32, (count, block), 1)
            allowed = (key <= query) & (key >= ds_ref[...])
            bias_ref[:count, :] = jnp.where(allowed, 0.0, NEG_FILL)
            lane = lax.broadcasted_iota(jnp.int32, (block, 128), 1)
            wide_lane = lax.broadcasted_iota(jnp.int32, (count, 128), 1)
            for p in range(width // 128):
                at = slice(p * 128, (p + 1) * 128)
                q2, g2 = q_ref[:, at], g_ref[:, at]
                k2 = ext_ref[pl.ds(first, count), at]
                v2 = ext_ref[pl.ds(first, count), width + p * 128 : width + (p + 1) * 128]
                prod = jnp.transpose(g2.astype(f32) * o_ref[:, at].astype(f32))
                dk = dv = dq = None
                for side in range(2):
                    mine = (lane < HEAD) if side == 0 else (lane >= HEAD)
                    qm = jnp.where(mine, q2, jnp.zeros_like(q2))
                    gm = jnp.where(mine, g2, jnp.zeros_like(g2))
                    km = jnp.where((wide_lane < HEAD) if side == 0 else (wide_lane >= HEAD), k2, jnp.zeros_like(k2))
                    h = 2 * p + side
                    delta = jnp.sum(prod[side * HEAD : (side + 1) * HEAD], axis=0, keepdims=True)
                    prob = jnp.exp(nt(k2, qm) + bias_ref[:count, :] - lse_ref[h : h + 1, :])
                    ds = (prob * (nt(v2, gm) - delta)).astype(bf16)
                    one_dv = nn(prob.astype(bf16), gm)
                    one_dk = nn(ds, qm)
                    one_dq = lax.dot_general(ds, km, (((0,), (0,)), ((), ())), preferred_element_type=f32)
                    dv = one_dv if dv is None else dv + one_dv
                    dk = one_dk if dk is None else dk + one_dk
                    dq = one_dq if dq is None else dq + one_dq
                acc_ref[pl.ds(first, count), at] += dk
                acc_ref[pl.ds(first, count), width + p * 128 : width + (p + 1) * 128] += dv
                turned = spin(dq * HEAD ** (-0.5), c_ref[...], -s1_ref[...], -s2_ref[...])
                dq_ref[:, at] = turned[0].astype(bf16)

        for skip in range(reach // block + 1):
            pl.when(meta_ref[b] == skip)(lambda skip=skip: variant(skip))

        @pl.when(b == steps - 1)
        def _():
            far_ref[...] = acc_ref[:reach, :].astype(bf16)
            dkv_ref[...] = acc_ref[reach:, :].astype(bf16)

    S = jax.ShapeDtypeStruct
    narrow = row_blocks(block, width)
    return call(
        kernel, meta,
        [
            (q, narrow), (kv, ANY), (halo, ANY),
            (doc_start_row, pl.BlockSpec((1, block), lambda i, *_: (0, i))),
            (grad, narrow), (attended, narrow),
            (lse, pl.BlockSpec((heads, block), lambda i, *_: (0, i))),
        ]
        + [(t, row_blocks(block, 128)) for t in tables],
        [
            (S((rows, width), bf16), narrow),
            (S((rows, 2 * width), bf16), whole((rows, 2 * width))),
            (S((reach, 2 * width), bf16), whole((reach, 2 * width))),
        ],
        (steps,),
        [
            pltpu.VMEM((rows + reach, 2 * width), bf16),
            pltpu.VMEM((rows + reach, 2 * width), f32),
            pltpu.VMEM((reach + block, block), f32),
            pltpu.SemaphoreType.DMA((2,)),
        ],
        flops=20 * rows * 2 * reach * width, bytes_=(rows + reach) * width * 12,
    )


def backward_branch(own, branch, slope, pieces, group, shards, block=256):
    rows, width = branch.shape
    ff = slope.shape[1]
    half = COLS
    count = len(pieces)
    plan = assembly(group, shards)

    def kernel(own_ref, g_ref, slope_ref, *rest):
        piece_refs, rest = rest[:count], rest[count:]
        pre_ref, att_ref, presum_ref, gsum_ref, d_ref, o_ref, sems = rest
        i = pl.program_id(0)

        @pl.when(i == 0)
        def _():
            copies = assemble_copies(
                group, shards, own_ref[0], piece_refs, {"d": d_ref, "o": o_ref}, sems
            )
            for c in copies:
                c.start()
            presum_ref[...] = jnp.zeros_like(presum_ref)
            gsum_ref[...] = jnp.zeros_like(gsum_ref)
            for c in copies:
                c.wait()

        parts = [g_ref[:, j * COLS : (j + 1) * COLS] for j in range(2)]
        att_ref[...] = (nt(parts[0], o_ref[0]) + nt(parts[1], o_ref[1])).astype(bf16)
        for j in range(ff // COLS):
            at = slice(j * COLS, (j + 1) * COLS)
            got = nt(parts[0], d_ref[0, at, :]) + nt(parts[1], d_ref[1, at, :])
            pre = (got * slope_ref[:, at].astype(f32)).astype(bf16)
            pre_ref[:, at] = pre
            presum_ref[:, at] += jnp.sum(pre.astype(f32), axis=0, keepdims=True)

        core = own_ref[1]
        mine = (i * block // (rows // 2)) == core

        @pl.when(mine)
        def _():
            gsum_ref[...] += jnp.sum(g_ref[...].astype(f32), axis=0, keepdims=True)

    S = jax.ShapeDtypeStruct
    return call(
        kernel, own,
        [(branch, row_blocks(block, width)), (slope, row_blocks(block, ff))] + [(p, ANY) for p in pieces],
        [
            (S((rows, ff), bf16), row_blocks(block, ff)),
            (S((rows, half), bf16), row_blocks(block, half)),
            (S((1, ff), f32), whole((1, ff))),
            (S((1, width), f32), whole((1, width))),
        ],
        (rows // block,),
        [
            pltpu.VMEM((2, ff, COLS), bf16),
            pltpu.VMEM((2, half, COLS), bf16),
            pltpu.SemaphoreType.DMA((len(plan),)),
        ],
        flops=2 * rows * width * (ff + half), bytes_=(2 * rows + width) * (ff + half) * 2 + rows * width * 2,
    )


def backward_normed(own, dq, dkv, halo, pre_grad, unit, tables, a_pieces, u_pieces, a_group, u_group, shards, block=256):
    rows, half = dq.shape
    width, ff = unit.shape[1], pre_grad.shape[1]
    reach = halo.shape[0]
    steps, late = rows // block, (rows - reach) // block
    na, nu = len(a_pieces), len(u_pieces)
    plan_a, plan_u = assembly(a_group, shards), assembly(u_group, shards)

    def kernel(own_ref, dq_ref, dkv_ref, halo_ref, pre_ref, unit_ref, c_ref, s1_ref, s2_ref, *rest):
        a_refs, rest = rest[:na], rest[na:]
        u_refs, rest = rest[:nu], rest[nu:]
        packed_ref, part_ref, bsum_ref, gain_ref, shift_ref, a_ref, u_ref, sem_a, sem_u = rest
        i = pl.program_id(0)

        def copies():
            return assemble_copies(a_group, shards, own_ref[0], a_refs, {"a": a_ref}, sem_a) + assemble_copies(
                u_group, shards, own_ref[0], u_refs, {"u": u_ref}, sem_u
            )

        @pl.when(i == 0)
        def _():
            for c in copies():
                c.start()
            for ref in (bsum_ref, gain_ref, shift_ref):
                ref[...] = jnp.zeros_like(ref)

        dkv_now = dkv_ref[...].astype(f32) + jnp.where(i >= late, halo_ref[...].astype(f32), 0.0)
        packed_ref[:, :half] = dq_ref[...]
        for j, part in enumerate(spin(dkv_now[:, :half], c_ref[...], -s1_ref[...], -s2_ref[...])):
            packed_ref[:, half + j * 128 : half + (j + 1) * 128] = part.astype(bf16)
        packed_ref[:, 2 * half :] = dkv_now[:, half:].astype(bf16)

        @pl.when(i == 0)
        def _():
            for c in copies():
                c.wait()

        bsum_ref[...] += jnp.sum(packed_ref[...].astype(f32), axis=0, keepdims=True)
        for n in range(width // COLS):
            at = slice(n * COLS, (n + 1) * COLS)
            total = None
            for j in range(3):
                got = nt(packed_ref[:, j * COLS : (j + 1) * COLS], a_ref[j, at, :])
                total = got if total is None else total + got
            for j in range(ff // COLS):
                total += nt(pre_ref[:, j * COLS : (j + 1) * COLS], u_ref[j, at, :])
            part_ref[:, at] = total.astype(bf16)
            gain_ref[:, at] += jnp.sum(total * unit_ref[:, at].astype(f32), axis=0, keepdims=True)
            shift_ref[:, at] += jnp.sum(total, axis=0, keepdims=True)

    S = jax.ShapeDtypeStruct
    return call(
        kernel, own,
        [
            (dq, row_blocks(block, half)),
            (dkv, row_blocks(block, 2 * half)),
            (halo, pl.BlockSpec((block, 2 * half), lambda i, *_: (jnp.maximum(i - late, 0), 0))),
            (pre_grad, row_blocks(block, ff)),
            (unit, row_blocks(block, width)),
        ]
        + [(t, row_blocks(block, 128)) for t in tables]
        + [(p, ANY) for p in (*a_pieces, *u_pieces)],
        [
            (S((rows, 3 * half), bf16), row_blocks(block, 3 * half)),
            (S((rows, width), bf16), row_blocks(block, width)),
            (S((1, 3 * half), f32), whole((1, 3 * half))),
            (S((1, width), f32), whole((1, width))),
            (S((1, width), f32), whole((1, width))),
        ],
        (steps,),
        [
            pltpu.VMEM((3, width, COLS), bf16),
            pltpu.VMEM((ff // COLS, width, COLS), bf16),
            pltpu.SemaphoreType.DMA((len(plan_a),)),
            pltpu.SemaphoreType.DMA((len(plan_u),)),
        ],
        flops=2 * rows * width * (ff + 3 * half), bytes_=(rows + width) * (ff + 3 * half) * 2 + rows * width * 4,
    )


def norm_backward(own, layer, grad, parts, unit, inv, gain, block=256):
    rows, width = unit.shape

    def kernel(own_ref, g_ref, p0_ref, p1_ref, unit_ref, inv_ref, gain_ref, new_ref, low_ref):
        u = (p0_ref[...].astype(f32) + p1_ref[...].astype(f32)) * gain_ref[layer : layer + 1, :]
        unit = unit_ref[...].astype(f32)
        new = g_ref[...].astype(f32) + inv_ref[:, :1] * (
            u - jnp.mean(u, axis=1, keepdims=True) - unit * jnp.mean(u * unit, axis=1, keepdims=True)
        )
        new_ref[...] = new
        low_ref[...] = new.astype(bf16)

    S = jax.ShapeDtypeStruct
    wide = row_blocks(block, width)
    return call(
        kernel, own,
        [(grad, wide), (parts[0], wide), (parts[1], wide), (unit, wide), (inv, row_blocks(block, 128)),
         (gain, whole(gain.shape))],
        [(S((rows, width), f32), wide), (S((rows, width), bf16), wide)],
        (rows // block,), flops=2 * rows * width * width,
    )


def weight_grads(own, lefts, rights, extra, group, shards):
    rows = rights.shape[0]
    blocks = rights.shape[1] // COLS
    ks = [l.shape[1] // shards for l in lefts]
    height = sum(ks)
    n_left = len(lefts)
    extra_rows = 0 if extra is None else extra.shape[0] // shards
    rounds, _ = sum_rounds(shards)
    size = [hi - lo for lo, hi in (group.cut(0), group.cut(1))]
    parts = {}
    shapes = [(group.rows, COLS)]
    parts[0] = [(0, 0, 0, group.rows)]
    for i, keys in enumerate(rounds.values()):
        at = 0
        for r, h in keys:
            parts.setdefault(r, []).append((i + 1, at) + group.cut(h))
            at += size[h]
        shapes.append((at, COLS))

    def kernel(own_ref, *refs):
        left_refs, rest = refs[:n_left], refs[n_left:]
        right_ref, rest = rest[0], rest[1:]
        extra_ref, rest = (None, rest) if extra is None else (rest[0], rest[1:])
        out_refs, flipped = rest[: len(shapes)], rest[len(shapes) :]
        for l, t in zip(left_refs, flipped):
            t[...] = jnp.transpose(l[...])

        def store(r, start, value):
            for i, at, lo, hi in parts[r]:
                first, last = max(lo, start), min(hi, start + value.shape[0])
                if first < last:
                    out_refs[i][at + first - lo : at + last - lo, :] = value[first - start : last - start]

        for r in range(shards):
            s = lax.bitwise_xor(own_ref[0], r)
            for j in range(blocks):
                start = j * height
                right = right_ref[:, j * COLS : (j + 1) * COLS]
                for t, k in zip(flipped, ks):
                    left = t[pl.ds(pl.multiple_of(s * k, k), k), :]
                    store(r, start, nn(left, right).astype(bf16))
                    start += k
            if extra is not None:
                store(r, height * blocks, extra_ref[pl.ds(pl.multiple_of(s * extra_rows, extra_rows), extra_rows), :].astype(bf16))

    S = jax.ShapeDtypeStruct
    extras = [] if extra is None else [extra]
    inputs = [(a, whole(a.shape)) for a in (*lefts, rights, *extras)]
    return call(
        kernel, own, inputs, [(S(s, bf16), whole(s)) for s in shapes], (1,),
        [pltpu.VMEM((l.shape[1], rows), bf16) for l in lefts],
        flops=2 * rows * sum(l.shape[1] for l in lefts) * rights.shape[1],
    )


def combine(own, arrays, outs):
    n = len(arrays)

    def kernel(own_ref, *refs):
        for ref, (_, segments) in zip(refs[n:], outs):
            for start, rows, terms in segments:
                total = None
                for a, first in terms:
                    part = refs[a][first : first + rows, :]
                    if len(terms) > 1:
                        part = part.astype(f32)
                    total = part if total is None else total + part
                ref[start : start + rows, :] = total.astype(bf16)

    shapes = [(rows, arrays[0].shape[1]) for rows, _ in outs]
    return call(
        kernel, own, [(a, whole(a.shape)) for a in arrays],
        [(jax.ShapeDtypeStruct(s, bf16), whole(s)) for s in shapes], (1,),
    )


def choose(own, first, second):
    def kernel(own_ref, a_ref, b_ref, out_ref):
        out_ref[...] = jnp.where(own_ref[2] == 1, b_ref[...], a_ref[...])

    return call(
        kernel, own, [(a, whole(a.shape)) for a in (first, second)],
        [(jax.ShapeDtypeStruct(first.shape, bf16), whole(first.shape))], (1,),
    )[0]


def extra_rows(own, gain_sum, shift_sum, branch_sum, up_sum, qkv_sum, shards):
    piece, ffp = gain_sum.shape[1] // shards, up_sum.shape[1] // shards
    w = qkv_sum.shape[1] // (3 * shards)
    shape = (16 * shards, COLS)

    def kernel(own_ref, gain_ref, shift_ref, branch_ref, up_ref, qkv_ref, out_ref):
        core = own_ref[1]
        out_ref[...] = jnp.zeros_like(out_ref)
        for s in range(shards):
            row = 16 * s
            at = slice(s * piece, (s + 1) * piece)
            out_ref[row : row + 1, :piece] = gain_ref[:, at]
            out_ref[row : row + 1, COLS // 2 : COLS // 2 + piece] = shift_ref[:, at]
            out_ref[row + 1 : row + 2, :piece] = branch_ref[:, at]
            out_ref[row + 2 : row + 3, :ffp] = up_ref[:, s * ffp : (s + 1) * ffp]
            for t in range(3 * piece // w):
                b = s * (3 * piece // w) + t
                value = qkv_ref[:, (b // 2) * w : (b // 2 + 1) * w]
                r, c = divmod(t * w, COLS)
                out_ref[row + 3 + r : row + 4 + r, c : c + w] = jnp.where(core == b % 2, value, 0.0)

    return call(
        kernel, own, [(a, whole(a.shape)) for a in (gain_sum, shift_sum, branch_sum, up_sum, qkv_sum)],
        [(jax.ShapeDtypeStruct(shape, f32), whole(shape))], (1,),
    )[0]


def pick(core, first, second):
    return jnp.where(core == 0, first, second)


def vector_places(widths):
    places, row, column = {}, 0, 0
    for name, (layers, width) in widths.items():
        places[name] = []
        for _ in range(layers):
            parts, done = [], 0
            while done < width:
                take = min(COLS - column, width - done)
                parts.append((row, column, take, done))
                done += take
                column += take
                if column == COLS:
                    row, column = row + 1, 0
            places[name].append(parts)
    return places


def pack_qkv(own, weight, layer, group, shards, vectors=None):
    _, rows, columns = weight.shape
    w = columns // (6 * shards)
    halves = [(0, group.rows)]
    names = [] if vectors is None else list(vectors)
    places = vector_places({n: vectors[n].shape for n in names})

    def kernel(own_ref, w_ref, *rest):
        vec_refs, rest = rest[: len(names)], rest[len(names) :]
        out_refs = rest[:1]
        core = own_ref[1]
        if names:
            tmp = rest[1]
            tmp[...] = jnp.zeros_like(tmp)
            for n, ref in zip(names, vec_refs):
                for l, parts in enumerate(places[n]):
                    for row, column, take, first in parts:
                        tmp[row : row + 1, column : column + take] = ref[l : l + 1, first : first + take].astype(f32)
            store_rows(out_refs, halves, 3 * rows, tmp[...].astype(bf16))
        for g in range(3):
            parts = []
            for s in range(shards):
                at = (g * shards + s) * 2 * w
                parts.append(pick(core, w_ref[0, :, at : at + w], w_ref[0, :, at + w : at + 2 * w]))
            store_rows(out_refs, halves, g * rows, jnp.concatenate(parts, axis=1))

    return call(
        kernel, own,
        [(weight, pl.BlockSpec((1, rows, columns), lambda i, *_: (layer, 0, 0)))]
        + [(vectors[n], whole(vectors[n].shape)) for n in names],
        piece_output(group), (1,),
        [pltpu.VMEM((16, COLS), f32)] if names else [], bytes_=rows * columns * 3,
    )


def whole_vectors(own, pieces, group, first, widths, shards, kinds):
    ranges = piece_ranges(group, shards)
    takes = [(a, r, first - lo) for a, (r, lo, hi) in enumerate(ranges) if lo <= first and first + 16 <= hi]
    names = list(widths)
    places = vector_places(widths)

    def kernel(own_ref, *refs):
        piece_refs, rest = refs[: len(takes)], refs[len(takes) :]
        out_refs, (all_ref, sems) = rest[: len(names)], rest[len(names) :]
        core = own_ref[1]
        copies = []
        for i, ((_, r, at), ref) in enumerate(zip(takes, piece_refs)):
            copies.append(
                pltpu.make_async_copy(
                    ref.at[pl.ds(at, 16), :], all_ref.at[lax.bitwise_xor(own_ref[0], r)], sems.at[i]
                )
            )
        for c in copies:
            c.start()
        for c in copies:
            c.wait()
        rows = [all_ref[s].astype(f32) for s in range(shards)]

        def piece_of(name, l, lo, hi):
            width = widths[name][1]
            s = lo // width
            lo, hi = lo - s * width, hi - s * width
            got = []
            for row, column, take, start in places[name][l]:
                a, b = max(lo, start), min(hi, start + take)
                if a < b:
                    got.append(rows[s][row : row + 1, column + a - start : column + b - start])
            return got[0] if len(got) == 1 else jnp.concatenate(got, axis=1)

        for name, ref in zip(names, out_refs):
            layers, width = widths[name]
            for l in range(layers):
                if not kinds[name]:
                    for s in range(shards):
                        ref[l : l + 1, s * width : (s + 1) * width] = piece_of(name, l, s * width, (s + 1) * width)
                    continue
                blocks = kinds[name] * shards
                w = width * shards // (2 * blocks)
                for b in range(blocks):
                    ref[l : l + 1, b * w : (b + 1) * w] = pick(
                        core, piece_of(name, l, 2 * b * w, (2 * b + 1) * w),
                        piece_of(name, l, (2 * b + 1) * w, (2 * b + 2) * w),
                    )

    outs = []
    for n in names:
        shape = (8, widths[n][1] * shards // (2 if kinds[n] else 1))
        outs.append((jax.ShapeDtypeStruct(shape, f32), whole(shape)))
    return call(
        kernel, own, [(pieces[a], ANY) for a, _, _ in takes], outs, (1,),
        [pltpu.VMEM((shards, 16, COLS), bf16), pltpu.SemaphoreType.DMA((len(takes),))], bytes_=shards * 16 * COLS * 2,
    )


def piece_output(group):
    shape = (group.rows, COLS)
    return [(jax.ShapeDtypeStruct(shape, bf16), whole(shape))]


def pack_up(own, weight, layer, group, shards):
    _, rows, columns = weight.shape
    w = columns // (2 * shards)
    halves = [(0, group.rows)]

    def kernel(own_ref, w_ref, *out_refs):
        core = own_ref[1]
        for j in range(columns // 2 // COLS):
            parts = []
            for s in range(j * COLS // w, (j + 1) * COLS // w):
                at = s * 2 * w
                parts.append(pick(core, w_ref[0, :, at : at + w], w_ref[0, :, at + w : at + 2 * w]))
            value = parts[0] if len(parts) == 1 else jnp.concatenate(parts, axis=1)
            store_rows(out_refs, halves, j * rows, value)

    return call(
        kernel, own,
        [(weight, pl.BlockSpec((1, rows, columns), lambda i, *_: (layer, 0, 0)))],
        piece_output(group), (1,), bytes_=rows * columns * 3,
    )


def pack_out(own, down, out, layer, group):
    halves = [(0, group.rows)]
    dr, orows = down.shape[1] // 2, out.shape[1] // 2
    width = down.shape[2]
    blocks = width // COLS

    def kernel(own_ref, d_ref, o_ref, *out_refs):
        for j in range(blocks):
            at = slice(j * COLS, (j + 1) * COLS)
            base = j * (dr + orows)
            store_rows(out_refs, halves, base, d_ref[0, :, at])
            store_rows(out_refs, halves, base + dr, o_ref[0, :, at])

    spec = lambda r: pl.BlockSpec((1, r, width), lambda i, own_ref: (layer, own_ref[1], 0))
    return call(
        kernel, own, [(down, spec(dr)), (out, spec(orows))],
        piece_output(group), (1,), bytes_=(dr + orows) * width * 4,
    )


def read_rows(refs, lo, hi):
    got, start = [], 0
    for ref in refs:
        first, last = max(lo, start), min(hi, start + ref.shape[0])
        if first < last:
            got.append(ref[first - start : last - start, :])
        start += ref.shape[0]
    return got[0] if len(got) == 1 else jnp.concatenate(got)


def unpack_columns(own, mine, theirs, before, layer, layers, rows, kinds, w, shards):
    columns = kinds * shards * 2 * w

    n = len(mine)

    def kernel(own_ref, *refs):
        a_refs, b_refs, out_ref = refs[:n], refs[n : 2 * n], refs[-1]
        core = own_ref[1]
        for j in range(kinds * shards * w // COLS):
            a_block = read_rows(a_refs, j * rows, (j + 1) * rows)
            b_block = read_rows(b_refs, j * rows, (j + 1) * rows)
            for c in range(j * COLS, (j + 1) * COLS, w):
                off = c % COLS
                a = a_block[:, off : off + w].astype(f32)
                b = b_block[:, off : off + w].astype(f32)
                out_ref[0, :, 2 * c : 2 * c + w] = pick(core, a, b)
                out_ref[0, :, 2 * c + w : 2 * c + 2 * w] = pick(core, b, a)

    extra = [] if before is None else [(before, ANY)]
    return call(
        kernel, own, [(v, whole(v.shape)) for v in (*mine, *theirs)] + extra,
        [(jax.ShapeDtypeStruct((layers, rows, columns), f32),
          pl.BlockSpec((1, rows, columns), lambda i, *_: (layer, 0, 0)))],
        (1,), aliases={} if before is None else {1 + 2 * n: 0}, bytes_=rows * columns * 6,
    )[0]


def unpack_rows(own, mine, theirs, befores, layer, layers, heights, width):
    blocks = width // COLS
    total = sum(heights)

    n = len(mine)

    def kernel(own_ref, *refs):
        a_refs, b_refs, out_refs = refs[:n], refs[n : 2 * n], refs[-len(heights) :]
        core = own_ref[1]
        for j in range(blocks):
            start = j * total
            for h, ref in zip(heights, out_refs):
                a = read_rows(a_refs, start, start + h).astype(f32)
                b = read_rows(b_refs, start, start + h).astype(f32)
                ref[0, :h, j * COLS : (j + 1) * COLS] = pick(core, a, b)
                ref[0, h:, j * COLS : (j + 1) * COLS] = pick(core, b, a)
                start += h

    extra = [] if befores is None else [(b, ANY) for b in befores]
    return call(
        kernel, own, [(v, whole(v.shape)) for v in (*mine, *theirs)] + extra,
        [(jax.ShapeDtypeStruct((layers, 2 * h, width), f32),
          pl.BlockSpec((1, 2 * h, width), lambda i, *_: (layer, 0, 0))) for h in heights],
        (1,), aliases={} if befores is None else {1 + 2 * n + i: i for i in range(len(heights))},
        bytes_=total * width * 12,
    )


class Net:
    def __init__(self, shards, reps):
        self.shards, self.reps = shards, reps
        self.bits = [1 << b for b in range(shards.bit_length() - 1)]
        self.chips = reps // 2
        self.shard = lax.axis_index("shard")
        self.rep = lax.axis_index("rep")
        self.core = self.rep % 2
        self.chip = self.rep // 2

    def send(self, value, where):
        pairs = []
        for s in range(self.shards):
            for r in range(self.reps):
                to = where(s, r)
                if to is not None:
                    pairs.append((s * self.reps + r, to[0] * self.reps + to[1]))
        return lax.ppermute(value, AXES, pairs)

    def other_core(self, value):
        return self.send(value, lambda s, r: (s, r ^ 1))

    def flip(self, value, bit):
        return self.send(value, lambda s, r: (s ^ bit, r))

    def next_chip(self, value):
        return self.send(value, lambda s, r: (s, (r + 2) % self.reps))

    def last_chip(self, value):
        return self.send(value, lambda s, r: (s, (r - 2) % self.reps))

    def chip_steps(self):
        chips = self.chips
        line = 4 if chips % 4 == 0 else 1
        steps = []
        if line == 4:
            at = self.chip % 4

            def inward(s, r):
                z = (r // 2) % 4
                return (s, r + 2) if z == 0 else (s, r - 2) if z == 3 else None

            def across(s, r):
                z = (r // 2) % 4
                return (s, r + 2) if z == 1 else (s, r - 2) if z == 2 else None

            def outward(s, r):
                z = (r // 2) % 4
                return (s, r - 2) if z == 1 else (s, r + 2) if z == 2 else None

            steps += [(inward, None), (across, None), (outward, (at == 0) | (at == 3))]
        step = line
        while step < chips:
            steps.append((lambda s, r, step=step: (s, r ^ (2 * step)), None))
            step *= 2
        return steps


class Clock:
    def __init__(self):
        self.last = None

    def tie(self, value):
        if self.last is None:
            return value
        return lax.optimization_barrier((value, self.last))[0]

    def mark(self, value):
        self.last = value


class Gather:
    def __init__(self, net, group, own):
        self.net, self.group, self.own = net, group, own[0]

    def near(self, clock):
        own = clock.tie(self.own)
        clock.mark(own)
        self.pieces = {0: [own]}
        for bit in self.net.bits:
            self.pieces[bit] = [self.net.flip(own, bit)]

    def far(self, clock):
        net, bits = self.net, self.net.bits
        for bit, came in zip(bits, clock.tie(tuple(self.pieces[bit][0] for bit in bits))):
            self.pieces[bit] = [came]
        cuts, sources, outs = [], [], []
        for r, lo, hi in piece_ranges(self.group, net.shards):
            if bin(r).count("1") == 2:
                bit = last_bit(net.shards, r, 0 if lo == 0 else 1)
                sources.append(self.pieces[r ^ bit][0])
                outs.append((hi - lo, [(0, hi - lo, [(len(sources) - 1, lo)])]))
        cuts = list(combine(net.own, sources, outs))
        parts, got = list(cuts), []
        for r, lo, hi in piece_ranges(self.group, net.shards):
            count = bin(r).count("1")
            if count <= 1:
                got.append(self.pieces[r][0])
                continue
            half = 0 if lo == 0 else 1
            bit = last_bit(net.shards, r, half)
            part = cuts.pop(0) if count == 2 else self.pieces[r ^ bit][half]
            self.pieces.setdefault(r, []).append(net.flip(part, bit))
            got.append(self.pieces[r][-1])
        clock.mark(tuple(parts))
        self.arrays = got

    def arrived(self, clock):
        self.arrays = list(clock.tie(tuple(self.arrays)))
        clock.mark(tuple(self.arrays[-2:]))


class Reduce:
    def __init__(self, net, clock, group, arrays, apart):
        self.at = None
        self.steps = self.run(net, clock, group, arrays, apart)

    def step(self, name):
        while self.at != name:
            self.at = next(self.steps)

    def run(self, net, clock, group, arrays, apart):
        rounds, goes = sum_rounds(net.shards)
        last = max(d for d, _ in rounds)
        cuts = [group.cut(h) for h in range(2)]
        size = [hi - lo for lo, hi in cuts]
        own = arrays[0]
        held = dict(zip(rounds, arrays[1:]))
        came = {}
        for now in range(last + 1):
            current = [key for key in rounds if key[0] == now]
            if now:
                given, outs = [held[key] for key in current], []
                for i, key in enumerate(current):
                    segments, at = [], 0
                    for r, h in rounds[key]:
                        terms = [(i, at)]
                        for a, first in came.pop((r, h), []):
                            terms.append((len(given), first))
                            given.append(a)
                        segments.append((at, size[h], terms))
                        at += size[h]
                    outs.append((at, segments))
                values = combine(net.own, given, outs)
                clock.mark(tuple(values))
                held.update(zip(current, values))
            sent = {key: net.flip(held[key], key[1]) for key in current}
            yield "r0" if now == 0 else "r1" if now == last else None
            for key, value in clock.tie(sent).items():
                at = 0
                for r, h in rounds[key]:
                    came.setdefault(goes[r, h], []).append((value, at))
                    at += size[h]
        given, segments = [own], []
        for h, (lo, hi) in enumerate(cuts):
            terms = [(0, lo)]
            for a, first in came[0, h]:
                terms.append((len(given), first))
                given.append(a)
            segments.append((lo, hi - lo, terms))
        if apart:
            outs = [(rows, [(0, rows, terms)]) for _, rows, terms in segments]
        else:
            outs = [(group.rows, segments)]
        values = combine(net.own, given, outs)
        clock.mark(tuple(values))
        self.chains = {n: ChipSum(net, clock, v) for n, v in zip("ab" if apart else [""], values)}
        yield "r2"


def add(own, a, b):
    rows = a.shape[0]
    return combine(own, [a, b], [(rows, [(0, rows, [(0, 0), (1, 0)])])])[0]


class ChipSum:
    def __init__(self, net, clock, value):
        self.steps = self.run(net, clock, value)
        self.at = next(self.steps)

    def step(self, name):
        while self.at != name:
            self.at = next(self.steps)

    def run(self, net, clock, value):
        for i, (where, replaced) in enumerate(net.chip_steps()):
            came = net.send(value, where)
            yield f"r{2 + i}" if i < 3 else None
            came = clock.tie(came)
            value = add(net.own, value, came) if replaced is None else choose(net.own, value, came)
            clock.mark(value)
        theirs = net.other_core(value)
        yield "r5"
        self.mine, self.theirs = value, clock.tie(theirs)
        clock.mark(self.theirs)
        yield "r6"


ORDER = (
    "g0a0", "docs", "g1a0", "g2a0", "g0u0", "f10", "g1u0", "h0", "g2u0", "g0o0", "f20", "f30", "g1o0", "g2o0",
    "g0a1", "f40", "g1a1", "g2a1", "g0u1", "f11", "g1u1", "h1", "g2u1", "g0o1", "f21", "f31", "g1o1", "wo1",
    "f41", "g2o1", "r0o1", "bb1", "ab1", "p1", "r1o1", "out", "wu1", "r0u1", "r2o1", "bn1", "wa1", "r1u1",
    "nb1", "r0a1", "r3o1", "r2u1", "wo0", "r1a1", "bb0", "r3u1", "r4o1", "r2a1", "r0o0", "ab0", "r4u1", "r3a1",
    "r5o1", "r1o0", "r6o1", "p0", "wu0", "r5u1", "r2o0", "r6u1", "r0u0", "r4a1", "bn0", "r1u0", "r3o0", "nb0",
    "r2u0", "wa0", "r0a0", "r4o0", "r3u0", "r1a0", "r5a1", "r2a0", "r4u0", "r3a0a", "r3a0b", "r4a0a", "r5o0", "r6a1",
    "r4a0b", "r5a0a", "r5u0", "r6o0", "r5a0b", "r6u0", "r6a0",
)


def body(
    tokens,
    token_order,
    lengths,
    cotangent,
    norm_gain,
    norm_shift,
    qkv_weight,
    qkv_bias,
    out_weight,
    out_bias,
    up_weight,
    up_bias,
    down_weight,
    down_bias,
):
    net = Net(lax.axis_size("shard"), lax.axis_size("rep"))
    shards, core = net.shards, net.core
    layers = norm_gain.shape[0]
    row_count, width = tokens.shape
    rows = 2 * row_count
    reach = row_count
    block = 256
    piece = width // shards
    ff = up_weight.shape[2] // 2
    group_first = net.shard * row_count * net.reps
    chip_first = net.chip * rows
    edge = (net.chip % 4 == 0) | (net.chip % 4 == 3)
    own = jnp.stack([net.shard, core, edge.astype(jnp.int32)]).astype(jnp.int32)
    net.own = own
    clock = Clock()

    ff_piece, head_piece = ff // shards, width // 2 // shards
    a_blocks = [(piece, "a", j) for j in range(3)]
    group_a0 = Group(a_blocks, 3 * piece // 2, 16)
    group_a = Group(a_blocks, 3 * piece // 2)
    group_u = Group([(piece, "u", j) for j in range(ff // COLS)], piece * (ff // COLS) // 2)
    group_o = Group(
        [b for j in range(2) for b in ((ff_piece, "d", j), (head_piece, "o", j))], ff_piece + head_piece
    )
    grads_a = Group([(3 * piece + 16, "", 0)], 3 * piece // 2)

    def pair_rows(x):
        other = net.other_core(x)
        return jnp.concatenate([pick(core, x, other), pick(core, other, x)])

    def own_rows(x):
        return lax.dynamic_slice_in_dim(x, core * row_count, row_count)

    small = {
        "gain": norm_gain, "shift": norm_shift, "qkv": qkv_bias, "out": out_bias, "up": up_bias, "down": down_bias
    }
    gathers = []
    for l in range(layers):
        gathers += [
            Gather(net, group_a0 if l == 0 else group_a, pack_qkv(own, qkv_weight, l, group_a if l else group_a0, shards, None if l else small)),
            Gather(net, group_u, pack_up(own, up_weight, l, group_u, shards)),
            Gather(net, group_o, pack_out(own, down_weight, out_weight, l, group_o)),
        ]
    slots = lengths.shape[0]
    before = jnp.arange(slots)[None, :] < jnp.arange(slots)[:, None]
    dealt_start = jnp.sum(jnp.where(before, lengths[None, :], 0), axis=1)
    hit = dealt_start[:, None] == jnp.arange(row_count)[None, :]
    home = jnp.sum(jnp.where(hit, token_order[None, :], 0), axis=1) - group_first
    docs = lax.all_gather(jnp.stack([home, lengths]), "rep", axis=0)
    home, length = docs[:, 0].reshape(-1), docs[:, 1].reshape(-1)
    place = chip_first + jnp.arange(rows, dtype=jnp.int32)
    inside = (home[None, :] <= place[:, None]) & (place[:, None] < (home + length)[None, :])
    doc_start = jnp.sum(jnp.where(inside, home[None, :], 0), axis=1) - chip_first
    earliest = jnp.min(doc_start.reshape(rows // block, block), axis=1)
    meta = jnp.clip((earliest + reach) // block - jnp.arange(rows // block), 0, reach // block)
    meta = meta.astype(jnp.int32)
    start_column, start_row = doc_start[:, None], doc_start[None, :]

    lane = jnp.arange(128) % HEAD
    positions = (jnp.arange(rows, dtype=jnp.int32) - doc_start).astype(f32)
    inverse_freq = jnp.exp((lane % (ROT // 2)).astype(f32) * (-2.0 * math.log(10000.0) / ROT))
    angles = positions[:, None] * inverse_freq[None, :]
    sine = jnp.sin(angles)
    tables = (
        jnp.where(lane < ROT, jnp.cos(angles), 1.0),
        jnp.where(lane < ROT // 2, -sine, 0.0),
        jnp.where((lane >= ROT // 2) & (lane < ROT), sine, 0.0),
    )

    stream0 = pair_rows(tokens)
    branch_top = pair_rows(cotangent)
    top = layers - 1
    at = [dict() for _ in range(layers)]
    sums = {}
    common = {}

    def forward_first(l):
        a = gathers[3 * l]
        if l == 0:
            common["vectors"] = whole_vectors(
                own, a.arrays, group_a0, 3 * piece, {n: v.shape for n, v in small.items()}, shards,
                {"gain": 0, "shift": 0, "qkv": 3, "out": 0, "up": 1, "down": 0},
            )
            before, adds, biases = stream0, [], []
        else:
            before, adds = at[l - 1]["stream"], at[l - 1]["adds"]
            biases = [common["vectors"][3], common["vectors"][5]]
        gains, shifts, qkv_b, _, _, _ = common["vectors"]
        stream, unit, inv, normed, q, kv, tail = forward_qkv(
            own, l, clock.tie(before), adds, biases, gains, shifts, qkv_b, tables, a.arrays, a.group, shards,
            reach,
        )
        clock.mark(q)
        at[l].update(stream=stream, unit=unit, inv=inv, normed=normed, q=q, kv=kv, tail=tail)

    def send_halo(l):
        at[l]["halo"] = net.next_chip(clock.tie(at[l]["tail"]))

    def forward_second(l):
        at[l]["activated"], at[l]["slope"] = forward_up(
            own, l, clock.tie(at[l]["normed"]), common["vectors"][4], gathers[3 * l + 1].arrays, group_u, shards
        )
        clock.mark(at[l]["slope"])

    def forward_third(l):
        at[l]["attended"], at[l]["lse"] = attend(
            meta, clock.tie(at[l]["q"]), at[l]["kv"], at[l]["halo"], start_column
        )
        clock.mark(at[l]["lse"])

    def forward_fourth(l):
        partial = forward_out(
            own, clock.tie(at[l]["attended"]), at[l]["activated"], gathers[3 * l + 2].arrays, group_o, shards
        )
        clock.mark(partial)
        at[l]["adds"] = [partial, net.other_core(partial)]

    def branch_of(l):
        return branch_top if l == top else at[l + 1]["branch"]

    def output():
        adds = at[top]["adds"]
        value = own_rows(clock.tie(at[top]["stream"])) + own_rows(adds[0]).astype(f32) + own_rows(adds[1]).astype(f32)
        out_b, down_b = common["vectors"][3], common["vectors"][5]
        common["output"] = (value + out_b[top : top + 1] + down_b[top : top + 1]).astype(bf16)
        clock.mark(common["output"])

    def reduce(name, l, group, lefts, rights, extra=None):
        got = weight_grads(own, [clock.tie(lefts[0])] + lefts[1:], rights, extra, group, shards)
        clock.mark(got[0])
        sums[name, l] = Reduce(net, clock, group, got, name == "a" and l == 0)

    def grads_out(l):
        reduce("o", l, group_o, [at[l]["activated"], at[l]["attended"]], branch_of(l))

    def grads_up(l):
        reduce("u", l, group_u, [at[l]["normed"]], at[l]["pre_grad"])

    def grads_qkv(l):
        d = at[l]
        extra = extra_rows(
            own, d["gain_sum"], d["shift_sum"], d["branch_sum"], d["up_sum"], d["qkv_sum"], shards
        )
        reduce("a", l, grads_a, [at[l]["normed"]], at[l]["packed_grad"], extra)

    def backward_first(l):
        pre_grad, attended_grad, up_sum, branch_sum = backward_branch(
            own, clock.tie(branch_of(l)), at[l]["slope"], gathers[3 * l + 2].arrays, group_o, shards
        )
        clock.mark(attended_grad)
        at[l].update(pre_grad=pre_grad, attended_grad=attended_grad, up_sum=up_sum, branch_sum=branch_sum)

    def backward_attention(l):
        d = at[l]
        d["dq"], d["dkv"], d["far"] = attend_back(
            meta, clock.tie(d["q"]), d["kv"], d["halo"], start_row, d["attended_grad"], d["attended"], d["lse"], tables
        )
        clock.mark(d["dq"])

    def send_halo_back(l):
        at[l]["halo_grad"] = net.last_chip(clock.tie(at[l]["far"]))

    def backward_norm_in(l):
        d = at[l]
        a = gathers[3 * l]
        d["packed_grad"], part, d["qkv_sum"], d["gain_sum"], d["shift_sum"] = backward_normed(
            own, clock.tie(d["dq"]), d["dkv"], d["halo_grad"], d["pre_grad"], d["unit"], tables,
            a.arrays, gathers[3 * l + 1].arrays, a.group, group_u, shards,
        )
        clock.mark(part)
        d["parts"] = [part, net.other_core(part)]

    def backward_norm(l):
        d = at[l]
        grad = branch_top if l == top else at[l + 1]["grad"]
        d["grad"], d["branch"] = norm_backward(
            own, l, clock.tie(grad), d["parts"], d["unit"], d["inv"], common["vectors"][0]
        )
        clock.mark(d["branch"])

    def finish(name, l):
        chains = [c for _, c in sorted(sums[name, l].chains.items())]
        for c in chains:
            c.step("r6")
        mine, theirs = [c.mine for c in chains], [c.theirs for c in chains]
        if name == "o":
            got = unpack_rows(own, mine, theirs, common.get(name), l, layers, (ff_piece, head_piece), width)
        else:
            kinds, w = (3, head_piece) if name == "a" else (1, ff_piece)
            got = unpack_columns(own, mine, theirs, common.get(name), l, layers, piece, kinds, w, shards)
        common[name] = got
        clock.mark(got)
        if name == "a":
            common["small", l] = mine[-1][-16:], theirs[-1][-16:]

    kernels = {
        "f1": forward_first, "f2": forward_second, "f3": forward_third, "f4": forward_fourth, "h": send_halo,
        "wo": grads_out, "wu": grads_up, "wa": grads_qkv, "bb": backward_first, "ab": backward_attention,
        "p": send_halo_back, "bn": backward_norm_in, "nb": backward_norm,
    }
    others = {"docs": lambda: clock.mark(docs), "out": output}
    for token in ORDER:
        if token in others:
            others[token]()
        elif token[:-1] in kernels:
            kernels[token[:-1]](int(token[-1]))
        else:
            stage, name, l = token[:2], token[2], int(token[3])
            weights = gathers[3 * l + "auo".index(name)]
            if stage == "g0":
                weights.near(clock)
            elif stage == "g1":
                weights.far(clock)
            elif stage == "g2":
                weights.arrived(clock)
            elif stage == "r6":
                finish(name, l)
            elif stage in ("r0", "r1", "r2"):
                sums[name, l].step(stage)
            else:
                sums[name, l].chains[token[4:]].step(stage)
    block_output, input_grad = common["output"], own_rows(at[0]["branch"])
    (down_g, out_g), up_g, qkv_g = common["o"], common["u"], common["a"]
    mine, theirs = (
        jnp.stack([common["small", l][i] for l in range(layers)]).astype(f32) for i in range(2)
    )
    low, high = pick(core, mine, theirs), pick(core, theirs, mine)
    both = low + high
    branch_g = both[:, 1, :piece]
    return (
        block_output,
        input_grad,
        both[:, 0, :piece],
        both[:, 0, COLS // 2 : COLS // 2 + piece],
        qkv_g,
        both[:, 3:5].reshape(layers, -1)[:, : 3 * piece],
        out_g,
        branch_g,
        up_g,
        jnp.concatenate([low[:, 2, :ff_piece], high[:, 2, :ff_piece]], axis=1),
        down_g,
        branch_g,
    )


def solution(mesh):
    rows = P(("shard", "rep"), None)
    vector, matrix = P(None, "shard"), P(None, "shard", None)
    line = P(("shard", "rep"))
    return jax.shard_map(
        body,
        mesh=mesh,
        in_specs=(
            rows, line, line, rows, vector, vector, matrix, vector, matrix, vector,
            matrix, vector, matrix, vector,
        ),
        out_specs=(
            rows, rows, vector, vector, matrix, vector, matrix, vector, matrix, vector,
            matrix, vector,
        ),
        check_vma=False,
    )
```

```python
import math
from types import SimpleNamespace

import jax
import jax.numpy as jnp
from jax import lax
from jax.experimental import pallas as pl
from jax.experimental.pallas import tpu as pltpu
from jax.sharding import PartitionSpec as P

HEADS = 16
HEAD = 64
ROT = 16
EPSILON = 1e-05
NEG_FILL = -1e30
AXES = ("shard", "rep")
bf16 = jnp.bfloat16
f32 = jnp.float32
VMEM_BYTES = 48 * 1024 * 1024
COLS = 512


def nn(a, b):
    return jnp.dot(a, b, preferred_element_type=f32)


def nt(a, b):
    return lax.dot_general(a, b, (((1,), (1,)), ((), ())), preferred_element_type=f32)


def whole(shape):
    return pl.BlockSpec(shape, lambda *_: (0,) * len(shape))


def row_blocks(rows, width):
    return pl.BlockSpec((rows, width), lambda i, *_: (i, 0))


ANY = pl.BlockSpec(memory_space=pl.ANY)


HINT = {"flops": 1}


def call(kernel, scalars, inputs, outputs, grid, scratch=(), aliases={}, flops=0, bytes_=0):
    return pl.pallas_call(
        kernel,
        grid_spec=pltpu.PrefetchScalarGridSpec(
            num_scalar_prefetch=1,
            grid=grid,
            in_specs=[s for _, s in inputs],
            out_specs=[s for _, s in outputs],
            scratch_shapes=list(scratch),
        ),
        out_shape=[o for o, _ in outputs],
        input_output_aliases=aliases,
        compiler_params=pltpu.CompilerParams(vmem_limit_bytes=VMEM_BYTES),
        cost_estimate=pl.CostEstimate(flops=HINT["flops"], bytes_accessed=1, transcendentals=0),
    )(scalars, *[a for a, _ in inputs])


class Group:
    def __init__(self, blocks, first_half, extra=0):
        self.blocks = blocks
        self.rows = sum(b[0] for b in blocks) + extra
        self.first_half = first_half

    def cut(self, half):
        return (0, self.first_half) if half == 0 else (self.first_half, self.rows)


def piece_ranges(group, shards):
    ranges = []
    for r in range(shards):
        if bin(r).count("1") > 1:
            ranges += [(r,) + group.cut(0), (r,) + group.cut(1)]
        else:
            ranges.append((r, 0, group.rows))
    return ranges


def hop_bits(shards, half):
    bits = [1 << b for b in range(shards.bit_length() - 1)]
    return bits if half == 0 else bits[::-1]


def last_bit(shards, relative, half):
    return [b for b in hop_bits(shards, half) if relative & b][-1]


def sum_rounds(shards):
    keys = [(r, h) for r in range(1, shards) for h in range(2)]
    goes = {(r, h): (r ^ last_bit(shards, r, h), h) for r, h in keys}
    depth = {}
    for key in sorted(keys, key=lambda k: -bin(k[0]).count("1")):
        before = [depth[k] for k, to in goes.items() if to == key]
        depth[key] = 1 + max(before) if before else 0
    rounds = {}
    for key in sorted(keys, key=lambda k: (depth[k], -bin(k[0]).count("1"), k)):
        rounds.setdefault((depth[key], last_bit(shards, *key)), []).append(key)
    return rounds, goes


def store_rows(refs, halves, start, value):
    for (lo, hi), ref in zip(halves, refs):
        first, last = max(lo, start), min(hi, start + value.shape[0])
        if first < last:
            ref[first - lo : last - lo, :] = value[first - start : last - start]


def assembly(group, shards):
    plan = []
    for a, (r, lo, hi) in enumerate(piece_ranges(group, shards)):
        start = 0
        for rows, key, index in group.blocks:
            first, last = max(lo, start), min(hi, start + rows)
            if first < last:
                plan.append((a, first - lo, last - first, key, index, r, rows, first - start))
            start += rows
    return plan


def assemble_copies(group, shards, own, refs, targets, sems):
    copies = []
    for i, (a, src, rows, key, index, r, per, off) in enumerate(assembly(group, shards)):
        at = pl.multiple_of(lax.bitwise_xor(own, r) * per + off, 16)
        copies.append(
            pltpu.make_async_copy(
                refs[a].at[pl.ds(src, rows), :],
                targets[key].at[index, pl.ds(at, rows), :],
                sems.at[i],
            )
        )
    return copies


def spin(x, c, s1, s2):
    parts = []
    for j in range(x.shape[1] // 128):
        part = x[:, j * 128 : (j + 1) * 128]
        up = pltpu.roll(part, 128 - ROT // 2, 1)
        down = pltpu.roll(part, ROT // 2, 1)
        parts.append(part * c + up * s1 + down * s2)
    return parts


def forward_qkv(own, layer, prev, adds, biases, gain, shift, qkv_b, tables, pieces, group, shards, tail, block=256):
    rows, width = prev.shape
    late = (rows - tail) // block
    count = len(pieces)
    n_add = len(adds)
    plan = assembly(group, shards)
    half = COLS

    def kernel(own_ref, *refs):
        prev_ref, *rest = refs
        add_refs, rest = rest[:n_add], rest[n_add:]
        bias_refs, rest = rest[: len(biases)], rest[len(biases) :]
        gain_ref, shift_ref, qkvb_ref, c_ref, s1_ref, s2_ref, *rest = rest
        now = slice(layer, layer + 1)
        piece_refs, rest = rest[:count], rest[count:]
        stream_ref, unit_ref, inv_ref, normed_ref, q_ref, kv_ref, tail_ref, w_ref, sems = rest

        @pl.when(pl.program_id(0) == 0)
        def _():
            for c in assemble_copies(group, shards, own_ref[0], piece_refs, {"a": w_ref}, sems):
                c.start()

        x = prev_ref[...].astype(f32)
        if n_add:
            for a in add_refs:
                x = x + a[...].astype(f32)
            for b in bias_refs:
                x = x + b[layer - 1 : layer, :]
        stream_ref[...] = x
        mean = jnp.mean(x, axis=1, keepdims=True)
        centered = x - mean
        inv = lax.rsqrt(jnp.mean(centered * centered, axis=1, keepdims=True) + EPSILON)
        unit = centered * inv
        unit_ref[...] = unit.astype(bf16)
        inv_ref[...] = jnp.broadcast_to(inv, inv_ref.shape)
        normed = (unit * gain_ref[now, :] + shift_ref[now, :]).astype(bf16)
        normed_ref[...] = normed

        @pl.when(pl.program_id(0) == 0)
        def _():
            for c in assemble_copies(group, shards, own_ref[0], piece_refs, {"a": w_ref}, sems):
                c.wait()

        c, s1, s2 = c_ref[...], s1_ref[...], s2_ref[...]
        q = nn(normed, w_ref[0]) + qkvb_ref[now, :half]
        for j, part in enumerate(spin(q, c, s1, s2)):
            q_ref[:, j * 128 : (j + 1) * 128] = (part * HEAD ** (-0.5)).astype(bf16)
        k = nn(normed, w_ref[1]) + qkvb_ref[now, half : 2 * half]
        for j, part in enumerate(spin(k, c, s1, s2)):
            kv_ref[:, j * 128 : (j + 1) * 128] = part.astype(bf16)
        v = nn(normed, w_ref[2]) + qkvb_ref[now, 2 * half :]
        kv_ref[:, half:] = v.astype(bf16)

        @pl.when(pl.program_id(0) >= late)
        def _():
            tail_ref[...] = kv_ref[...]

    wide = row_blocks(block, width)
    inputs = (
        [(prev, wide)]
        + [(a, wide) for a in adds]
        + [(v, whole(v.shape)) for v in (*biases, gain, shift, qkv_b)]
        + [(t, row_blocks(block, 128)) for t in tables]
        + [(p, ANY) for p in pieces]
    )
    S = jax.ShapeDtypeStruct
    outputs = [
        (S((rows, width), f32), wide),
        (S((rows, width), bf16), wide),
        (S((rows, 128), f32), row_blocks(block, 128)),
        (S((rows, width), bf16), wide),
        (S((rows, half), bf16), row_blocks(block, half)),
        (S((rows, 2 * half), bf16), row_blocks(block, 2 * half)),
        (S((tail, 2 * half), bf16), pl.BlockSpec((block, 2 * half), lambda i, *_: (jnp.maximum(i - late, 0), 0))),
    ]
    return call(
        kernel, own, inputs, outputs, (rows // block,),
        [pltpu.VMEM((3, width, half), bf16), pltpu.SemaphoreType.DMA((len(plan),))],
        flops=2 * rows * width * 3 * half, bytes_=rows * width * 12 + 3 * width * half * 2,
    )


def gelu_parts(x):
    z = jnp.abs(x) * math.sqrt(0.5)
    t = 1.0 / (1.0 + 0.3275911 * z)
    poly = t * (
        0.254829592 + t * (-0.284496736 + t * (1.421413741 + t * (-1.453152027 + t * 1.061405429)))
    )
    e = jnp.exp(-0.5 * x * x)
    tail = 0.5 * poly * e
    big = jnp.where(x >= 0, 1.0 - tail, tail)
    return x * big, big + x * e * (1.0 / math.sqrt(2.0 * math.pi))


def forward_up(own, layer, normed, up_b, pieces, group, shards, block=256):
    rows, width = normed.shape
    count = len(pieces)
    plan = assembly(group, shards)
    chunks = len(group.blocks)

    def kernel(own_ref, x_ref, b_ref, *rest):
        piece_refs, rest = rest[:count], rest[count:]
        act_ref, slope_ref, w_ref, sems = rest

        @pl.when(pl.program_id(0) == 0)
        def _():
            copies = assemble_copies(group, shards, own_ref[0], piece_refs, {"u": w_ref}, sems)
            for c in copies:
                c.start()
            for c in copies:
                c.wait()

        for j in range(chunks):
            at = slice(j * COLS, (j + 1) * COLS)
            pre = nn(x_ref[...], w_ref[j]) + b_ref[layer : layer + 1, at]
            act, slope = gelu_parts(pre)
            act_ref[:, at] = act.astype(bf16)
            slope_ref[:, at] = slope.astype(bf16)

    S = jax.ShapeDtypeStruct
    ff = chunks * COLS
    out = (S((rows, ff), bf16), row_blocks(block, ff))
    return call(
        kernel, own,
        [(normed, row_blocks(block, width)), (up_b, whole(up_b.shape))] + [(p, ANY) for p in pieces],
        [out, out], (rows // block,),
        [pltpu.VMEM((chunks, width, COLS), bf16), pltpu.SemaphoreType.DMA((len(plan),))],
        flops=4 * rows * width * ff, bytes_=rows * ff * 4 + width * ff * 2 + rows * width * 2,
    )


def forward_out(own, attended, activated, pieces, group, shards, block=256):
    rows, ff = activated.shape
    half = attended.shape[1]
    count = len(pieces)
    plan = assembly(group, shards)
    width = 2 * COLS

    def kernel(own_ref, att_ref, act_ref, *rest):
        piece_refs, rest = rest[:count], rest[count:]
        out_ref, d_ref, o_ref, sems = rest

        @pl.when(pl.program_id(0) == 0)
        def _():
            copies = assemble_copies(
                group, shards, own_ref[0], piece_refs, {"d": d_ref, "o": o_ref}, sems
            )
            for c in copies:
                c.start()
            for c in copies:
                c.wait()

        for j in range(2):
            got = nn(att_ref[...], o_ref[j]) + nn(act_ref[...], d_ref[j])
            out_ref[:, j * COLS : (j + 1) * COLS] = got.astype(bf16)

    S = jax.ShapeDtypeStruct
    return call(
        kernel, own,
        [(attended, row_blocks(block, half)), (activated, row_blocks(block, ff))]
        + [(p, ANY) for p in pieces],
        [(S((rows, width), bf16), row_blocks(block, width))], (rows // block,),
        [
            pltpu.VMEM((2, ff, COLS), bf16),
            pltpu.VMEM((2, half, COLS), bf16),
            pltpu.SemaphoreType.DMA((len(plan),)),
        ],
        flops=2 * rows * width * (ff + half), bytes_=(rows + width) * (ff + half) * 2 + rows * width * 2,
    )[0]


def attend(meta, q, kv, halo, doc_start, block=256):
    rows, width = q.shape
    reach = halo.shape[0]
    heads = width // HEAD

    def kernel(meta_ref, q_ref, kv_ref, halo_ref, ds_ref, out_ref, lse_ref, ext_ref, bias_ref, sems):
        b = pl.program_id(0)

        @pl.when(b == 0)
        def _():
            one = pltpu.make_async_copy(halo_ref, ext_ref.at[pl.ds(0, reach), :], sems.at[0])
            two = pltpu.make_async_copy(kv_ref, ext_ref.at[pl.ds(reach, rows), :], sems.at[1])
            one.start()
            two.start()
            one.wait()
            two.wait()

        def variant(skip):
            count = (reach // block + 1 - skip) * block
            first = pl.multiple_of((b + skip) * block, block)
            key = first - reach + lax.broadcasted_iota(jnp.int32, (block, count), 1)
            query = b * block + lax.broadcasted_iota(jnp.int32, (block, count), 0)
            allowed = (key <= query) & (key >= ds_ref[...])
            bias_ref[:, :count] = jnp.where(allowed, 0.0, NEG_FILL)
            lane = lax.broadcasted_iota(jnp.int32, (block, 128), 1)
            lse = jnp.zeros((block, 128), f32)
            for p in range(width // 128):
                q2 = q_ref[:, p * 128 : (p + 1) * 128]
                k2 = ext_ref[pl.ds(first, count), p * 128 : (p + 1) * 128]
                v2 = ext_ref[pl.ds(first, count), width + p * 128 : width + (p + 1) * 128]
                outs = []
                for side in range(2):
                    mine = (lane < HEAD) if side == 0 else (lane >= HEAD)
                    s = nt(jnp.where(mine, q2, jnp.zeros_like(q2)), k2) + bias_ref[:, :count]
                    top = jnp.max(s, axis=1, keepdims=True)
                    e = jnp.exp(s - top)
                    total = jnp.sum(e, axis=1, keepdims=True)
                    outs.append(nn(e.astype(bf16), v2) / total)
                    lse = jnp.where(lane == 2 * p + side, top + jnp.log(total), lse)
                out_ref[:, p * 128 : (p + 1) * 128] = jnp.where(lane < HEAD, outs[0], outs[1]).astype(bf16)
            lse_ref[...] = jnp.transpose(lse)[:heads]

        for skip in range(reach // block + 1):
            pl.when(meta_ref[b] == skip)(lambda skip=skip: variant(skip))

    S = jax.ShapeDtypeStruct
    return call(
        kernel, meta,
        [
            (q, row_blocks(block, width)), (kv, ANY), (halo, ANY), (doc_start, row_blocks(block, 1)),
        ],
        [
            (S((rows, width), bf16), row_blocks(block, width)),
            (S((heads, rows), f32), pl.BlockSpec((heads, block), lambda i, *_: (0, i))),
        ],
        (rows // block,),
        [
            pltpu.VMEM((rows + reach, 2 * width), bf16),
            pltpu.VMEM((block, reach + block), f32),
            pltpu.SemaphoreType.DMA((2,)),
        ],
        flops=8 * rows * 2 * reach * width, bytes_=(rows + reach) * width * 8,
    )


def attend_back(meta, q, kv, halo, doc_start_row, grad, attended, lse, tables, block=256):
    rows, width = q.shape
    reach = halo.shape[0]
    heads = width // HEAD
    steps = rows // block

    def kernel(meta_ref, q_ref, kv_ref, halo_ref, ds_ref, g_ref, o_ref, lse_ref, c_ref, s1_ref, s2_ref,
               dq_ref, dkv_ref, far_ref, ext_ref, acc_ref, bias_ref, sems):
        b = pl.program_id(0)

        @pl.when(b == 0)
        def _():
            one = pltpu.make_async_copy(halo_ref, ext_ref.at[pl.ds(0, reach), :], sems.at[0])
            two = pltpu.make_async_copy(kv_ref, ext_ref.at[pl.ds(reach, rows), :], sems.at[1])
            one.start()
            two.start()
            acc_ref[...] = jnp.zeros_like(acc_ref)
            one.wait()
            two.wait()

        def variant(skip):
            count = (reach // block + 1 - skip) * block
            first = pl.multiple_of((b + skip) * block, block)
            key = first - reach + lax.broadcasted_iota(jnp.int32, (count, block), 0)
            query = b * block + lax.broadcasted_iota(jnp.int32, (count, block), 1)
            allowed = (key <= query) & (key >= ds_ref[...])
            bias_ref[:count, :] = jnp.where(allowed, 0.0, NEG_FILL)
            lane = lax.broadcasted_iota(jnp.int32, (block, 128), 1)
            wide_lane = lax.broadcasted_iota(jnp.int32, (count, 128), 1)
            for p in range(width // 128):
                at = slice(p * 128, (p + 1) * 128)
                q2, g2 = q_ref[:, at], g_ref[:, at]
                k2 = ext_ref[pl.ds(first, count), at]
                v2 = ext_ref[pl.ds(first, count), width + p * 128 : width + (p + 1) * 128]
                prod = jnp.transpose(g2.astype(f32) * o_ref[:, at].astype(f32))
                dk = dv = dq = None
                for side in range(2):
                    mine = (lane < HEAD) if side == 0 else (lane >= HEAD)
                    qm = jnp.where(mine, q2, jnp.zeros_like(q2))
                    gm = jnp.where(mine, g2, jnp.zeros_like(g2))
                    km = jnp.where((wide_lane < HEAD) if side == 0 else (wide_lane >= HEAD), k2, jnp.zeros_like(k2))
                    h = 2 * p + side
                    delta = jnp.sum(prod[side * HEAD : (side + 1) * HEAD], axis=0, keepdims=True)
                    prob = jnp.exp(nt(k2, qm) + bias_ref[:count, :] - lse_ref[h : h + 1, :])
                    ds = (prob * (nt(v2, gm) - delta)).astype(bf16)
                    one_dv = nn(prob.astype(bf16), gm)
                    one_dk = nn(ds, qm)
                    one_dq = lax.dot_general(ds, km, (((0,), (0,)), ((), ())), preferred_element_type=f32)
                    dv = one_dv if dv is None else dv + one_dv
                    dk = one_dk if dk is None else dk + one_dk
                    dq = one_dq if dq is None else dq + one_dq
                acc_ref[pl.ds(first, count), at] += dk
                acc_ref[pl.ds(first, count), width + p * 128 : width + (p + 1) * 128] += dv
                turned = spin(dq * HEAD ** (-0.5), c_ref[...], -s1_ref[...], -s2_ref[...])
                dq_ref[:, at] = turned[0].astype(bf16)

        for skip in range(reach // block + 1):
            pl.when(meta_ref[b] == skip)(lambda skip=skip: variant(skip))

        @pl.when(b == steps - 1)
        def _():
            far_ref[...] = acc_ref[:reach, :].astype(bf16)
            dkv_ref[...] = acc_ref[reach:, :].astype(bf16)

    S = jax.ShapeDtypeStruct
    narrow = row_blocks(block, width)
    return call(
        kernel, meta,
        [
            (q, narrow), (kv, ANY), (halo, ANY),
            (doc_start_row, pl.BlockSpec((1, block), lambda i, *_: (0, i))),
            (grad, narrow), (attended, narrow),
            (lse, pl.BlockSpec((heads, block), lambda i, *_: (0, i))),
        ]
        + [(t, row_blocks(block, 128)) for t in tables],
        [
            (S((rows, width), bf16), narrow),
            (S((rows, 2 * width), bf16), whole((rows, 2 * width))),
            (S((reach, 2 * width), bf16), whole((reach, 2 * width))),
        ],
        (steps,),
        [
            pltpu.VMEM((rows + reach, 2 * width), bf16),
            pltpu.VMEM((rows + reach, 2 * width), f32),
            pltpu.VMEM((reach + block, block), f32),
            pltpu.SemaphoreType.DMA((2,)),
        ],
        flops=20 * rows * 2 * reach * width, bytes_=(rows + reach) * width * 12,
    )


def backward_branch(own, branch, slope, pieces, group, shards, block=256):
    rows, width = branch.shape
    ff = slope.shape[1]
    half = COLS
    count = len(pieces)
    plan = assembly(group, shards)

    def kernel(own_ref, g_ref, slope_ref, *rest):
        piece_refs, rest = rest[:count], rest[count:]
        pre_ref, att_ref, presum_ref, gsum_ref, d_ref, o_ref, sems = rest
        i = pl.program_id(0)

        @pl.when(i == 0)
        def _():
            copies = assemble_copies(
                group, shards, own_ref[0], piece_refs, {"d": d_ref, "o": o_ref}, sems
            )
            for c in copies:
                c.start()
            presum_ref[...] = jnp.zeros_like(presum_ref)
            gsum_ref[...] = jnp.zeros_like(gsum_ref)
            for c in copies:
                c.wait()

        parts = [g_ref[:, j * COLS : (j + 1) * COLS] for j in range(2)]
        att_ref[...] = (nt(parts[0], o_ref[0]) + nt(parts[1], o_ref[1])).astype(bf16)
        for j in range(ff // COLS):
            at = slice(j * COLS, (j + 1) * COLS)
            got = nt(parts[0], d_ref[0, at, :]) + nt(parts[1], d_ref[1, at, :])
            pre = (got * slope_ref[:, at].astype(f32)).astype(bf16)
            pre_ref[:, at] = pre
            presum_ref[:, at] += jnp.sum(pre.astype(f32), axis=0, keepdims=True)

        core = own_ref[1]
        mine = (i * block // (rows // 2)) == core

        @pl.when(mine)
        def _():
            gsum_ref[...] += jnp.sum(g_ref[...].astype(f32), axis=0, keepdims=True)

    S = jax.ShapeDtypeStruct
    return call(
        kernel, own,
        [(branch, row_blocks(block, width)), (slope, row_blocks(block, ff))] + [(p, ANY) for p in pieces],
        [
            (S((rows, ff), bf16), row_blocks(block, ff)),
            (S((rows, half), bf16), row_blocks(block, half)),
            (S((1, ff), f32), whole((1, ff))),
            (S((1, width), f32), whole((1, width))),
        ],
        (rows // block,),
        [
            pltpu.VMEM((2, ff, COLS), bf16),
            pltpu.VMEM((2, half, COLS), bf16),
            pltpu.SemaphoreType.DMA((len(plan),)),
        ],
        flops=2 * rows * width * (ff + half), bytes_=(2 * rows + width) * (ff + half) * 2 + rows * width * 2,
    )


def backward_normed(own, dq, dkv, halo, pre_grad, unit, tables, a_pieces, u_pieces, a_group, u_group, shards, block=256):
    rows, half = dq.shape
    width, ff = unit.shape[1], pre_grad.shape[1]
    reach = halo.shape[0]
    steps, late = rows // block, (rows - reach) // block
    na, nu = len(a_pieces), len(u_pieces)
    plan_a, plan_u = assembly(a_group, shards), assembly(u_group, shards)

    def kernel(own_ref, dq_ref, dkv_ref, halo_ref, pre_ref, unit_ref, c_ref, s1_ref, s2_ref, *rest):
        a_refs, rest = rest[:na], rest[na:]
        u_refs, rest = rest[:nu], rest[nu:]
        packed_ref, part_ref, bsum_ref, gain_ref, shift_ref, a_ref, u_ref, sem_a, sem_u = rest
        i = pl.program_id(0)

        def copies():
            return assemble_copies(a_group, shards, own_ref[0], a_refs, {"a": a_ref}, sem_a) + assemble_copies(
                u_group, shards, own_ref[0], u_refs, {"u": u_ref}, sem_u
            )

        @pl.when(i == 0)
        def _():
            for c in copies():
                c.start()
            for ref in (bsum_ref, gain_ref, shift_ref):
                ref[...] = jnp.zeros_like(ref)

        dkv_now = dkv_ref[...].astype(f32) + jnp.where(i >= late, halo_ref[...].astype(f32), 0.0)
        packed_ref[:, :half] = dq_ref[...]
        for j, part in enumerate(spin(dkv_now[:, :half], c_ref[...], -s1_ref[...], -s2_ref[...])):
            packed_ref[:, half + j * 128 : half + (j + 1) * 128] = part.astype(bf16)
        packed_ref[:, 2 * half :] = dkv_now[:, half:].astype(bf16)

        @pl.when(i == 0)
        def _():
            for c in copies():
                c.wait()

        bsum_ref[...] += jnp.sum(packed_ref[...].astype(f32), axis=0, keepdims=True)
        for n in range(width // COLS):
            at = slice(n * COLS, (n + 1) * COLS)
            total = None
            for j in range(3):
                got = nt(packed_ref[:, j * COLS : (j + 1) * COLS], a_ref[j, at, :])
                total = got if total is None else total + got
            for j in range(ff // COLS):
                total += nt(pre_ref[:, j * COLS : (j + 1) * COLS], u_ref[j, at, :])
            part_ref[:, at] = total.astype(bf16)
            gain_ref[:, at] += jnp.sum(total * unit_ref[:, at].astype(f32), axis=0, keepdims=True)
            shift_ref[:, at] += jnp.sum(total, axis=0, keepdims=True)

    S = jax.ShapeDtypeStruct
    return call(
        kernel, own,
        [
            (dq, row_blocks(block, half)),
            (dkv, row_blocks(block, 2 * half)),
            (halo, pl.BlockSpec((block, 2 * half), lambda i, *_: (jnp.maximum(i - late, 0), 0))),
            (pre_grad, row_blocks(block, ff)),
            (unit, row_blocks(block, width)),
        ]
        + [(t, row_blocks(block, 128)) for t in tables]
        + [(p, ANY) for p in (*a_pieces, *u_pieces)],
        [
            (S((rows, 3 * half), bf16), row_blocks(block, 3 * half)),
            (S((rows, width), bf16), row_blocks(block, width)),
            (S((1, 3 * half), f32), whole((1, 3 * half))),
            (S((1, width), f32), whole((1, width))),
            (S((1, width), f32), whole((1, width))),
        ],
        (steps,),
        [
            pltpu.VMEM((3, width, COLS), bf16),
            pltpu.VMEM((ff // COLS, width, COLS), bf16),
            pltpu.SemaphoreType.DMA((len(plan_a),)),
            pltpu.SemaphoreType.DMA((len(plan_u),)),
        ],
        flops=2 * rows * width * (ff + 3 * half), bytes_=(rows + width) * (ff + 3 * half) * 2 + rows * width * 4,
    )


def norm_backward(own, layer, grad, parts, unit, inv, gain, block=256):
    rows, width = unit.shape

    def kernel(own_ref, g_ref, p0_ref, p1_ref, unit_ref, inv_ref, gain_ref, new_ref, low_ref):
        u = (p0_ref[...].astype(f32) + p1_ref[...].astype(f32)) * gain_ref[layer : layer + 1, :]
        unit = unit_ref[...].astype(f32)
        new = g_ref[...].astype(f32) + inv_ref[:, :1] * (
            u - jnp.mean(u, axis=1, keepdims=True) - unit * jnp.mean(u * unit, axis=1, keepdims=True)
        )
        new_ref[...] = new
        low_ref[...] = new.astype(bf16)

    S = jax.ShapeDtypeStruct
    wide = row_blocks(block, width)
    return call(
        kernel, own,
        [(grad, wide), (parts[0], wide), (parts[1], wide), (unit, wide), (inv, row_blocks(block, 128)),
         (gain, whole(gain.shape))],
        [(S((rows, width), f32), wide), (S((rows, width), bf16), wide)],
        (rows // block,), flops=2 * rows * width * width,
    )


def weight_grads(own, lefts, rights, extra, group, shards):
    rows = rights.shape[0]
    blocks = rights.shape[1] // COLS
    ks = [l.shape[1] // shards for l in lefts]
    height = sum(ks)
    n_left = len(lefts)
    extra_rows = 0 if extra is None else extra.shape[0] // shards
    rounds, _ = sum_rounds(shards)
    size = [hi - lo for lo, hi in (group.cut(0), group.cut(1))]
    parts = {}
    shapes = [(group.rows, COLS)]
    parts[0] = [(0, 0, 0, group.rows)]
    for i, keys in enumerate(rounds.values()):
        at = 0
        for r, h in keys:
            parts.setdefault(r, []).append((i + 1, at) + group.cut(h))
            at += size[h]
        shapes.append((at, COLS))

    def kernel(own_ref, *refs):
        left_refs, rest = refs[:n_left], refs[n_left:]
        right_ref, rest = rest[0], rest[1:]
        extra_ref, rest = (None, rest) if extra is None else (rest[0], rest[1:])
        out_refs, flipped = rest[: len(shapes)], rest[len(shapes) :]
        for l, t in zip(left_refs, flipped):
            t[...] = jnp.transpose(l[...])

        def store(r, start, value):
            for i, at, lo, hi in parts[r]:
                first, last = max(lo, start), min(hi, start + value.shape[0])
                if first < last:
                    out_refs[i][at + first - lo : at + last - lo, :] = value[first - start : last - start]

        for r in range(shards):
            s = lax.bitwise_xor(own_ref[0], r)
            for j in range(blocks):
                start = j * height
                right = right_ref[:, j * COLS : (j + 1) * COLS]
                for t, k in zip(flipped, ks):
                    left = t[pl.ds(pl.multiple_of(s * k, k), k), :]
                    store(r, start, nn(left, right).astype(bf16))
                    start += k
            if extra is not None:
                store(r, height * blocks, extra_ref[pl.ds(pl.multiple_of(s * extra_rows, extra_rows), extra_rows), :].astype(bf16))

    S = jax.ShapeDtypeStruct
    extras = [] if extra is None else [extra]
    inputs = [(a, whole(a.shape)) for a in (*lefts, rights, *extras)]
    return call(
        kernel, own, inputs, [(S(s, bf16), whole(s)) for s in shapes], (1,),
        [pltpu.VMEM((l.shape[1], rows), bf16) for l in lefts],
        flops=2 * rows * sum(l.shape[1] for l in lefts) * rights.shape[1],
    )


def combine(own, arrays, outs):
    n = len(arrays)

    def kernel(own_ref, *refs):
        for ref, (_, segments) in zip(refs[n:], outs):
            for start, rows, terms in segments:
                total = None
                for a, first in terms:
                    part = refs[a][first : first + rows, :]
                    if len(terms) > 1:
                        part = part.astype(f32)
                    total = part if total is None else total + part
                ref[start : start + rows, :] = total.astype(bf16)

    shapes = [(rows, arrays[0].shape[1]) for rows, _ in outs]
    return call(
        kernel, own, [(a, whole(a.shape)) for a in arrays],
        [(jax.ShapeDtypeStruct(s, bf16), whole(s)) for s in shapes], (1,),
    )


def choose(own, first, second):
    def kernel(own_ref, a_ref, b_ref, out_ref):
        out_ref[...] = jnp.where(own_ref[2] == 1, b_ref[...], a_ref[...])

    return call(
        kernel, own, [(a, whole(a.shape)) for a in (first, second)],
        [(jax.ShapeDtypeStruct(first.shape, bf16), whole(first.shape))], (1,),
    )[0]


def extra_rows(own, gain_sum, shift_sum, branch_sum, up_sum, qkv_sum, shards):
    piece, ffp = gain_sum.shape[1] // shards, up_sum.shape[1] // shards
    w = qkv_sum.shape[1] // (3 * shards)
    shape = (16 * shards, COLS)

    def kernel(own_ref, gain_ref, shift_ref, branch_ref, up_ref, qkv_ref, out_ref):
        core = own_ref[1]
        out_ref[...] = jnp.zeros_like(out_ref)
        for s in range(shards):
            row = 16 * s
            at = slice(s * piece, (s + 1) * piece)
            out_ref[row : row + 1, :piece] = gain_ref[:, at]
            out_ref[row : row + 1, COLS // 2 : COLS // 2 + piece] = shift_ref[:, at]
            out_ref[row + 1 : row + 2, :piece] = branch_ref[:, at]
            out_ref[row + 2 : row + 3, :ffp] = up_ref[:, s * ffp : (s + 1) * ffp]
            for t in range(3 * piece // w):
                b = s * (3 * piece // w) + t
                value = qkv_ref[:, (b // 2) * w : (b // 2 + 1) * w]
                r, c = divmod(t * w, COLS)
                out_ref[row + 3 + r : row + 4 + r, c : c + w] = jnp.where(core == b % 2, value, 0.0)

    return call(
        kernel, own, [(a, whole(a.shape)) for a in (gain_sum, shift_sum, branch_sum, up_sum, qkv_sum)],
        [(jax.ShapeDtypeStruct(shape, f32), whole(shape))], (1,),
    )[0]


def pick(core, first, second):
    return jnp.where(core == 0, first, second)


def vector_places(widths):
    places, row, column = {}, 0, 0
    for name, (layers, width) in widths.items():
        places[name] = []
        for _ in range(layers):
            parts, done = [], 0
            while done < width:
                take = min(COLS - column, width - done)
                parts.append((row, column, take, done))
                done += take
                column += take
                if column == COLS:
                    row, column = row + 1, 0
            places[name].append(parts)
    return places


def pack_qkv(own, weight, layer, group, shards, vectors=None):
    _, rows, columns = weight.shape
    w = columns // (6 * shards)
    halves = [(0, group.rows)]
    names = [] if vectors is None else list(vectors)
    places = vector_places({n: vectors[n].shape for n in names})

    def kernel(own_ref, w_ref, *rest):
        vec_refs, rest = rest[: len(names)], rest[len(names) :]
        out_refs = rest[:1]
        core = own_ref[1]
        if names:
            tmp = rest[1]
            tmp[...] = jnp.zeros_like(tmp)
            for n, ref in zip(names, vec_refs):
                for l, parts in enumerate(places[n]):
                    for row, column, take, first in parts:
                        tmp[row : row + 1, column : column + take] = ref[l : l + 1, first : first + take].astype(f32)
            store_rows(out_refs, halves, 3 * rows, tmp[...].astype(bf16))
        for g in range(3):
            parts = []
            for s in range(shards):
                at = (g * shards + s) * 2 * w
                parts.append(pick(core, w_ref[0, :, at : at + w], w_ref[0, :, at + w : at + 2 * w]))
            store_rows(out_refs, halves, g * rows, jnp.concatenate(parts, axis=1))

    return call(
        kernel, own,
        [(weight, pl.BlockSpec((1, rows, columns), lambda i, *_: (layer, 0, 0)))]
        + [(vectors[n], whole(vectors[n].shape)) for n in names],
        piece_output(group), (1,),
        [pltpu.VMEM((16, COLS), f32)] if names else [], bytes_=rows * columns * 3,
    )


def whole_vectors(own, pieces, group, first, widths, shards, kinds):
    ranges = piece_ranges(group, shards)
    takes = [(a, r, first - lo) for a, (r, lo, hi) in enumerate(ranges) if lo <= first and first + 16 <= hi]
    names = list(widths)
    places = vector_places(widths)

    def kernel(own_ref, *refs):
        piece_refs, rest = refs[: len(takes)], refs[len(takes) :]
        out_refs, (all_ref, sems) = rest[: len(names)], rest[len(names) :]
        core = own_ref[1]
        copies = []
        for i, ((_, r, at), ref) in enumerate(zip(takes, piece_refs)):
            copies.append(
                pltpu.make_async_copy(
                    ref.at[pl.ds(at, 16), :], all_ref.at[lax.bitwise_xor(own_ref[0], r)], sems.at[i]
                )
            )
        for c in copies:
            c.start()
        for c in copies:
            c.wait()
        rows = [all_ref[s].astype(f32) for s in range(shards)]

        def piece_of(name, l, lo, hi):
            width = widths[name][1]
            s = lo // width
            lo, hi = lo - s * width, hi - s * width
            got = []
            for row, column, take, start in places[name][l]:
                a, b = max(lo, start), min(hi, start + take)
                if a < b:
                    got.append(rows[s][row : row + 1, column + a - start : column + b - start])
            return got[0] if len(got) == 1 else jnp.concatenate(got, axis=1)

        for name, ref in zip(names, out_refs):
            layers, width = widths[name]
            for l in range(layers):
                if not kinds[name]:
                    for s in range(shards):
                        ref[l : l + 1, s * width : (s + 1) * width] = piece_of(name, l, s * width, (s + 1) * width)
                    continue
                blocks = kinds[name] * shards
                w = width * shards // (2 * blocks)
                for b in range(blocks):
                    ref[l : l + 1, b * w : (b + 1) * w] = pick(
                        core, piece_of(name, l, 2 * b * w, (2 * b + 1) * w),
                        piece_of(name, l, (2 * b + 1) * w, (2 * b + 2) * w),
                    )

    outs = []
    for n in names:
        shape = (8, widths[n][1] * shards // (2 if kinds[n] else 1))
        outs.append((jax.ShapeDtypeStruct(shape, f32), whole(shape)))
    return call(
        kernel, own, [(pieces[a], ANY) for a, _, _ in takes], outs, (1,),
        [pltpu.VMEM((shards, 16, COLS), bf16), pltpu.SemaphoreType.DMA((len(takes),))], bytes_=shards * 16 * COLS * 2,
    )


def piece_output(group):
    shape = (group.rows, COLS)
    return [(jax.ShapeDtypeStruct(shape, bf16), whole(shape))]


def pack_up(own, weight, layer, group, shards):
    _, rows, columns = weight.shape
    w = columns // (2 * shards)
    halves = [(0, group.rows)]

    def kernel(own_ref, w_ref, *out_refs):
        core = own_ref[1]
        for j in range(columns // 2 // COLS):
            parts = []
            for s in range(j * COLS // w, (j + 1) * COLS // w):
                at = s * 2 * w
                parts.append(pick(core, w_ref[0, :, at : at + w], w_ref[0, :, at + w : at + 2 * w]))
            value = parts[0] if len(parts) == 1 else jnp.concatenate(parts, axis=1)
            store_rows(out_refs, halves, j * rows, value)

    return call(
        kernel, own,
        [(weight, pl.BlockSpec((1, rows, columns), lambda i, *_: (layer, 0, 0)))],
        piece_output(group), (1,), bytes_=rows * columns * 3,
    )


def pack_out(own, down, out, layer, group):
    halves = [(0, group.rows)]
    dr, orows = down.shape[1] // 2, out.shape[1] // 2
    width = down.shape[2]
    blocks = width // COLS

    def kernel(own_ref, d_ref, o_ref, *out_refs):
        for j in range(blocks):
            at = slice(j * COLS, (j + 1) * COLS)
            base = j * (dr + orows)
            store_rows(out_refs, halves, base, d_ref[0, :, at])
            store_rows(out_refs, halves, base + dr, o_ref[0, :, at])

    spec = lambda r: pl.BlockSpec((1, r, width), lambda i, own_ref: (layer, own_ref[1], 0))
    return call(
        kernel, own, [(down, spec(dr)), (out, spec(orows))],
        piece_output(group), (1,), bytes_=(dr + orows) * width * 4,
    )


def read_rows(refs, lo, hi):
    got, start = [], 0
    for ref in refs:
        first, last = max(lo, start), min(hi, start + ref.shape[0])
        if first < last:
            got.append(ref[first - start : last - start, :])
        start += ref.shape[0]
    return got[0] if len(got) == 1 else jnp.concatenate(got)


def unpack_columns(own, mine, theirs, before, layer, layers, rows, kinds, w, shards):
    columns = kinds * shards * 2 * w

    n = len(mine)

    def kernel(own_ref, *refs):
        a_refs, b_refs, out_ref = refs[:n], refs[n : 2 * n], refs[-1]
        core = own_ref[1]
        for j in range(kinds * shards * w // COLS):
            a_block = read_rows(a_refs, j * rows, (j + 1) * rows)
            b_block = read_rows(b_refs, j * rows, (j + 1) * rows)
            for c in range(j * COLS, (j + 1) * COLS, w):
                off = c % COLS
                a = a_block[:, off : off + w].astype(f32)
                b = b_block[:, off : off + w].astype(f32)
                out_ref[0, :, 2 * c : 2 * c + w] = pick(core, a, b)
                out_ref[0, :, 2 * c + w : 2 * c + 2 * w] = pick(core, b, a)

    extra = [] if before is None else [(before, ANY)]
    return call(
        kernel, own, [(v, whole(v.shape)) for v in (*mine, *theirs)] + extra,
        [(jax.ShapeDtypeStruct((layers, rows, columns), f32),
          pl.BlockSpec((1, rows, columns), lambda i, *_: (layer, 0, 0)))],
        (1,), aliases={} if before is None else {1 + 2 * n: 0}, bytes_=rows * columns * 6,
    )[0]


def unpack_rows(own, mine, theirs, befores, layer, layers, heights, width):
    blocks = width // COLS
    total = sum(heights)

    n = len(mine)

    def kernel(own_ref, *refs):
        a_refs, b_refs, out_refs = refs[:n], refs[n : 2 * n], refs[-len(heights) :]
        core = own_ref[1]
        for j in range(blocks):
            start = j * total
            for h, ref in zip(heights, out_refs):
                a = read_rows(a_refs, start, start + h).astype(f32)
                b = read_rows(b_refs, start, start + h).astype(f32)
                ref[0, :h, j * COLS : (j + 1) * COLS] = pick(core, a, b)
                ref[0, h:, j * COLS : (j + 1) * COLS] = pick(core, b, a)
                start += h

    extra = [] if befores is None else [(b, ANY) for b in befores]
    return call(
        kernel, own, [(v, whole(v.shape)) for v in (*mine, *theirs)] + extra,
        [(jax.ShapeDtypeStruct((layers, 2 * h, width), f32),
          pl.BlockSpec((1, 2 * h, width), lambda i, *_: (layer, 0, 0))) for h in heights],
        (1,), aliases={} if befores is None else {1 + 2 * n + i: i for i in range(len(heights))},
        bytes_=total * width * 12,
    )


class Net:
    def __init__(self, shards, reps):
        self.shards, self.reps = shards, reps
        self.bits = [1 << b for b in range(shards.bit_length() - 1)]
        self.chips = reps // 2
        self.shard = lax.axis_index("shard")
        self.rep = lax.axis_index("rep")
        self.core = self.rep % 2
        self.chip = self.rep // 2

    def send(self, value, where):
        pairs = []
        for s in range(self.shards):
            for r in range(self.reps):
                to = where(s, r)
                if to is not None:
                    pairs.append((s * self.reps + r, to[0] * self.reps + to[1]))
        return lax.ppermute(value, AXES, pairs)

    def other_core(self, value):
        return self.send(value, lambda s, r: (s, r ^ 1))

    def flip(self, value, bit):
        return self.send(value, lambda s, r: (s ^ bit, r))

    def next_chip(self, value):
        return self.send(value, lambda s, r: (s, (r + 2) % self.reps))

    def last_chip(self, value):
        return self.send(value, lambda s, r: (s, (r - 2) % self.reps))

    def chip_steps(self):
        chips = self.chips
        line = 4 if chips % 4 == 0 else 1
        steps = []
        if line == 4:
            at = self.chip % 4

            def inward(s, r):
                z = (r // 2) % 4
                return (s, r + 2) if z == 0 else (s, r - 2) if z == 3 else None

            def across(s, r):
                z = (r // 2) % 4
                return (s, r + 2) if z == 1 else (s, r - 2) if z == 2 else None

            def outward(s, r):
                z = (r // 2) % 4
                return (s, r - 2) if z == 1 else (s, r + 2) if z == 2 else None

            steps += [(inward, None), (across, None), (outward, (at == 0) | (at == 3))]
        step = line
        while step < chips:
            steps.append((lambda s, r, step=step: (s, r ^ (2 * step)), None))
            step *= 2
        return steps


class Clock:
    def __init__(self):
        self.last = None

    def tie(self, value):
        if self.last is None:
            return value
        return lax.optimization_barrier((value, self.last))[0]

    def mark(self, value):
        self.last = value


class Gather:
    def __init__(self, net, group, own):
        self.net, self.group, self.own = net, group, own[0]

    def near(self, clock):
        own = clock.tie(self.own)
        clock.mark(own)
        self.pieces = {0: [own]}
        for bit in self.net.bits:
            self.pieces[bit] = [self.net.flip(own, bit)]

    def far(self, clock):
        net, bits = self.net, self.net.bits
        for bit, came in zip(bits, clock.tie(tuple(self.pieces[bit][0] for bit in bits))):
            self.pieces[bit] = [came]
        cuts, sources, outs = [], [], []
        for r, lo, hi in piece_ranges(self.group, net.shards):
            if bin(r).count("1") == 2:
                bit = last_bit(net.shards, r, 0 if lo == 0 else 1)
                sources.append(self.pieces[r ^ bit][0])
                outs.append((hi - lo, [(0, hi - lo, [(len(sources) - 1, lo)])]))
        cuts = list(combine(net.own, sources, outs))
        parts, got = list(cuts), []
        for r, lo, hi in piece_ranges(self.group, net.shards):
            count = bin(r).count("1")
            if count <= 1:
                got.append(self.pieces[r][0])
                continue
            half = 0 if lo == 0 else 1
            bit = last_bit(net.shards, r, half)
            part = cuts.pop(0) if count == 2 else self.pieces[r ^ bit][half]
            self.pieces.setdefault(r, []).append(net.flip(part, bit))
            got.append(self.pieces[r][-1])
        clock.mark(tuple(parts))
        self.arrays = got

    def arrived(self, clock):
        self.arrays = list(clock.tie(tuple(self.arrays)))
        clock.mark(tuple(self.arrays[-2:]))


class Reduce:
    def __init__(self, net, clock, group, arrays, apart):
        self.at = None
        self.steps = self.run(net, clock, group, arrays, apart)

    def step(self, name):
        while self.at != name:
            self.at = next(self.steps)

    def run(self, net, clock, group, arrays, apart):
        rounds, goes = sum_rounds(net.shards)
        last = max(d for d, _ in rounds)
        cuts = [group.cut(h) for h in range(2)]
        size = [hi - lo for lo, hi in cuts]
        own = arrays[0]
        held = dict(zip(rounds, arrays[1:]))
        came = {}
        for now in range(last + 1):
            current = [key for key in rounds if key[0] == now]
            if now:
                given, outs = [held[key] for key in current], []
                for i, key in enumerate(current):
                    segments, at = [], 0
                    for r, h in rounds[key]:
                        terms = [(i, at)]
                        for a, first in came.pop((r, h), []):
                            terms.append((len(given), first))
                            given.append(a)
                        segments.append((at, size[h], terms))
                        at += size[h]
                    outs.append((at, segments))
                values = combine(net.own, given, outs)
                clock.mark(tuple(values))
                held.update(zip(current, values))
            sent = {key: net.flip(held[key], key[1]) for key in current}
            yield "r0" if now == 0 else "r1" if now == last else None
            for key, value in clock.tie(sent).items():
                at = 0
                for r, h in rounds[key]:
                    came.setdefault(goes[r, h], []).append((value, at))
                    at += size[h]
        given, segments = [own], []
        for h, (lo, hi) in enumerate(cuts):
            terms = [(0, lo)]
            for a, first in came[0, h]:
                terms.append((len(given), first))
                given.append(a)
            segments.append((lo, hi - lo, terms))
        if apart:
            outs = [(rows, [(0, rows, terms)]) for _, rows, terms in segments]
        else:
            outs = [(group.rows, segments)]
        values = combine(net.own, given, outs)
        clock.mark(tuple(values))
        self.chains = {n: ChipSum(net, clock, v) for n, v in zip("ab" if apart else [""], values)}
        yield "r2"


def add(own, a, b):
    rows = a.shape[0]
    return combine(own, [a, b], [(rows, [(0, rows, [(0, 0), (1, 0)])])])[0]


class ChipSum:
    def __init__(self, net, clock, value):
        self.steps = self.run(net, clock, value)
        self.at = next(self.steps)

    def step(self, name):
        while self.at != name:
            self.at = next(self.steps)

    def run(self, net, clock, value):
        for i, (where, replaced) in enumerate(net.chip_steps()):
            came = net.send(value, where)
            yield f"r{2 + i}" if i < 3 else None
            came = clock.tie(came)
            value = add(net.own, value, came) if replaced is None else choose(net.own, value, came)
            clock.mark(value)
        theirs = net.other_core(value)
        yield "r5"
        self.mine, self.theirs = value, clock.tie(theirs)
        clock.mark(self.theirs)
        yield "r6"


COSTS = {"ab1": 200 * 10**8, "bb1": 400 * 10**8, "f21": 100 * 10**8, "f30": 200 * 10**8, "f31": 60 * 10**8, "wa1": 10 * 10**8}
ORDER = (
    "g0a0", "docs", "g1a0", "g2a0", "g0u0", "f10", "g1u0", "h0", "g2u0", "g0o0", "f20", "f30", "g1o0", "g2o0",
    "g0a1", "f40", "g1a1", "g2a1", "g0u1", "f11", "g1u1", "h1", "g2u1", "g0o1", "f21", "f31", "g1o1", "wo1",
    "f41", "g2o1", "r0o1", "bb1", "ab1", "p1", "r1o1", "out", "wu1", "r0u1", "r2o1", "q1", "bn1", "wa1",
    "r1u1", "nb1", "r0a1", "r3o1", "r2u1", "wo0", "r1a1", "bb0", "r2a1", "r3u1", "r4o1", "r0o0", "ab0", "r4u1",
    "p0", "r3a1", "r5o1", "r1o0", "wu0", "r5u1", "r2o0", "q0", "bn0", "r0u0", "r1u0", "r6o1", "r2u0", "wa0",
    "r0a0", "r3o0", "r4a1", "nb0", "r4o0", "r3u0", "r1a0", "r5a1", "r2a0", "r4u0", "r3a0a", "r3a0b", "r4a0a", "r5o0",
    "r6u1", "r6a1", "r4a0b", "r5a0a", "r5u0", "r6o0", "r5a0b", "r6u0", "r6a0",
)


def body(
    tokens,
    token_order,
    lengths,
    cotangent,
    norm_gain,
    norm_shift,
    qkv_weight,
    qkv_bias,
    out_weight,
    out_bias,
    up_weight,
    up_bias,
    down_weight,
    down_bias,
):
    net = Net(lax.axis_size("shard"), lax.axis_size("rep"))
    shards, core = net.shards, net.core
    layers = norm_gain.shape[0]
    row_count, width = tokens.shape
    rows = 2 * row_count
    reach = row_count
    block = 256
    piece = width // shards
    ff = up_weight.shape[2] // 2
    group_first = net.shard * row_count * net.reps
    chip_first = net.chip * rows
    edge = (net.chip % 4 == 0) | (net.chip % 4 == 3)
    own = jnp.stack([net.shard, core, edge.astype(jnp.int32)]).astype(jnp.int32)
    net.own = own
    clock = Clock()

    ff_piece, head_piece = ff // shards, width // 2 // shards
    a_blocks = [(piece, "a", j) for j in range(3)]
    group_a0 = Group(a_blocks, 3 * piece // 2, 16)
    group_a = Group(a_blocks, 3 * piece // 2)
    group_u = Group([(piece, "u", j) for j in range(ff // COLS)], piece * (ff // COLS) // 2)
    group_o = Group(
        [b for j in range(2) for b in ((ff_piece, "d", j), (head_piece, "o", j))], ff_piece + head_piece
    )
    grads_a = Group([(3 * piece + 16, "", 0)], 3 * piece // 2)

    def pair_rows(x):
        other = net.other_core(x)
        return jnp.concatenate([pick(core, x, other), pick(core, other, x)])

    def own_rows(x):
        return lax.dynamic_slice_in_dim(x, core * row_count, row_count)

    small = {
        "gain": norm_gain, "shift": norm_shift, "qkv": qkv_bias, "out": out_bias, "up": up_bias, "down": down_bias
    }
    gathers = []
    for l in range(layers):
        gathers += [
            Gather(net, group_a0 if l == 0 else group_a, pack_qkv(own, qkv_weight, l, group_a if l else group_a0, shards, None if l else small)),
            Gather(net, group_u, pack_up(own, up_weight, l, group_u, shards)),
            Gather(net, group_o, pack_out(own, down_weight, out_weight, l, group_o)),
        ]
    slots = lengths.shape[0]
    before = jnp.arange(slots)[None, :] < jnp.arange(slots)[:, None]
    dealt_start = jnp.sum(jnp.where(before, lengths[None, :], 0), axis=1)
    hit = dealt_start[:, None] == jnp.arange(row_count)[None, :]
    home = jnp.sum(jnp.where(hit, token_order[None, :], 0), axis=1) - group_first
    docs = lax.all_gather(jnp.stack([home, lengths]), "rep", axis=0)
    home, length = docs[:, 0].reshape(-1), docs[:, 1].reshape(-1)
    place = chip_first + jnp.arange(rows, dtype=jnp.int32)
    inside = (home[None, :] <= place[:, None]) & (place[:, None] < (home + length)[None, :])
    doc_start = jnp.sum(jnp.where(inside, home[None, :], 0), axis=1) - chip_first
    earliest = jnp.min(doc_start.reshape(rows // block, block), axis=1)
    meta = jnp.clip((earliest + reach) // block - jnp.arange(rows // block), 0, reach // block)
    meta = meta.astype(jnp.int32)
    start_column, start_row = doc_start[:, None], doc_start[None, :]

    lane = jnp.arange(128) % HEAD
    positions = (jnp.arange(rows, dtype=jnp.int32) - doc_start).astype(f32)
    inverse_freq = jnp.exp((lane % (ROT // 2)).astype(f32) * (-2.0 * math.log(10000.0) / ROT))
    angles = positions[:, None] * inverse_freq[None, :]
    sine = jnp.sin(angles)
    tables = (
        jnp.where(lane < ROT, jnp.cos(angles), 1.0),
        jnp.where(lane < ROT // 2, -sine, 0.0),
        jnp.where((lane >= ROT // 2) & (lane < ROT), sine, 0.0),
    )

    stream0 = pair_rows(tokens)
    branch_top = pair_rows(cotangent)
    top = layers - 1
    at = [SimpleNamespace() for _ in range(layers)]
    sums = {}
    common = SimpleNamespace(smalls={}, made={})

    def forward_first(l):
        a = gathers[3 * l]
        if l == 0:
            common.vectors = whole_vectors(
                own, a.arrays, group_a0, 3 * piece, {n: v.shape for n, v in small.items()}, shards,
                {"gain": 0, "shift": 0, "qkv": 3, "out": 0, "up": 1, "down": 0},
            )
            before, adds, biases = stream0, [], []
        else:
            before, adds = at[l - 1].stream, at[l - 1].adds
            biases = [common.vectors[3], common.vectors[5]]
        gains, shifts, qkv_b, _, _, _ = common.vectors
        stream, unit, inv, normed, q, kv, tail = forward_qkv(
            own, l, clock.tie(before), adds, biases, gains, shifts, qkv_b, tables, a.arrays, a.group, shards,
            reach,
        )
        clock.mark(q)
        s = at[l]
        s.stream, s.unit, s.inv, s.normed, s.q, s.kv, s.tail = stream, unit, inv, normed, q, kv, tail

    def send_halo(l):
        at[l].halo = net.next_chip(clock.tie(at[l].tail))

    def forward_second(l):
        at[l].activated, at[l].slope = forward_up(
            own, l, clock.tie(at[l].normed), common.vectors[4], gathers[3 * l + 1].arrays, group_u, shards
        )
        clock.mark(at[l].slope)

    def forward_third(l):
        at[l].attended, at[l].lse = attend(
            meta, clock.tie(at[l].q), at[l].kv, at[l].halo, start_column
        )
        clock.mark(at[l].lse)

    def forward_fourth(l):
        partial = forward_out(
            own, clock.tie(at[l].attended), at[l].activated, gathers[3 * l + 2].arrays, group_o, shards
        )
        clock.mark(partial)
        at[l].adds = [partial, net.other_core(partial)]

    def branch_of(l):
        return branch_top if l == top else at[l + 1].branch

    def output():
        adds = at[top].adds
        value = own_rows(clock.tie(at[top].stream)) + own_rows(adds[0]).astype(f32) + own_rows(adds[1]).astype(f32)
        out_b, down_b = common.vectors[3], common.vectors[5]
        common.output = (value + out_b[top : top + 1] + down_b[top : top + 1]).astype(bf16)
        clock.mark(common.output)

    def reduce(name, l, group, lefts, rights, extra=None):
        got = weight_grads(own, [clock.tie(lefts[0])] + lefts[1:], rights, extra, group, shards)
        clock.mark(got[0])
        sums[name, l] = Reduce(net, clock, group, got, name == "a" and l == 0)

    def grads_out(l):
        reduce("o", l, group_o, [at[l].activated, at[l].attended], branch_of(l))

    def grads_up(l):
        reduce("u", l, group_u, [at[l].normed], at[l].pre_grad)

    def grads_qkv(l):
        d = at[l]
        extra = extra_rows(
            own, d.gain_sum, d.shift_sum, d.branch_sum, d.up_sum, d.qkv_sum, shards
        )
        reduce("a", l, grads_a, [at[l].normed], at[l].packed_grad, extra)

    def backward_first(l):
        pre_grad, attended_grad, up_sum, branch_sum = backward_branch(
            own, clock.tie(branch_of(l)), at[l].slope, gathers[3 * l + 2].arrays, group_o, shards
        )
        clock.mark(attended_grad)
        s = at[l]
        s.pre_grad, s.attended_grad, s.up_sum, s.branch_sum = pre_grad, attended_grad, up_sum, branch_sum

    def backward_attention(l):
        d = at[l]
        d.dq, d.dkv, d.far = attend_back(
            meta, clock.tie(d.q), d.kv, d.halo, start_row, d.attended_grad, d.attended, d.lse, tables
        )
        clock.mark(d.dq)

    def send_halo_back(l):
        at[l].halo_grad = net.last_chip(clock.tie(at[l].far))

    def halo_back_came(l):
        at[l].halo_grad = clock.tie(at[l].halo_grad)
        clock.mark(at[l].halo_grad)

    def backward_norm_in(l):
        d = at[l]
        a = gathers[3 * l]
        d.packed_grad, part, d.qkv_sum, d.gain_sum, d.shift_sum = backward_normed(
            own, clock.tie(d.dq), d.dkv, d.halo_grad, d.pre_grad, d.unit, tables,
            a.arrays, gathers[3 * l + 1].arrays, a.group, group_u, shards,
        )
        clock.mark(part)
        d.parts = [part, net.other_core(part)]

    def backward_norm(l):
        d = at[l]
        grad = branch_top if l == top else at[l + 1].grad
        d.grad, d.branch = norm_backward(
            own, l, clock.tie(grad), d.parts, d.unit, d.inv, common.vectors[0]
        )
        clock.mark(d.branch)

    def finish(name, l):
        chains = [c for _, c in sorted(sums[name, l].chains.items())]
        for c in chains:
            c.step("r6")
        mine, theirs = [c.mine for c in chains], [c.theirs for c in chains]
        if name == "o":
            got = unpack_rows(own, mine, theirs, common.made.get(name), l, layers, (ff_piece, head_piece), width)
        else:
            kinds, w = (3, head_piece) if name == "a" else (1, ff_piece)
            got = unpack_columns(own, mine, theirs, common.made.get(name), l, layers, piece, kinds, w, shards)
        common.made[name] = got
        clock.mark(got)
        if name == "a":
            common.smalls[l] = mine[-1][-16:], theirs[-1][-16:]

    kernels = {
        "f1": forward_first, "f2": forward_second, "f3": forward_third, "f4": forward_fourth, "h": send_halo,
        "wo": grads_out, "wu": grads_up, "wa": grads_qkv, "bb": backward_first, "ab": backward_attention,
        "p": send_halo_back, "q": halo_back_came, "bn": backward_norm_in, "nb": backward_norm,
    }
    others = {"docs": lambda: clock.mark(docs), "out": output}
    for token in ORDER:
        HINT["flops"] = COSTS.get(token, 1)
        if token in others:
            others[token]()
        elif token[:-1] in kernels:
            kernels[token[:-1]](int(token[-1]))
        else:
            stage, name, l = token[:2], token[2], int(token[3])
            weights = gathers[3 * l + "auo".index(name)]
            if stage == "g0":
                weights.near(clock)
            elif stage == "g1":
                weights.far(clock)
            elif stage == "g2":
                weights.arrived(clock)
            elif stage == "r6":
                finish(name, l)
            elif stage in ("r0", "r1", "r2"):
                sums[name, l].step(stage)
            else:
                sums[name, l].chains[token[4:]].step(stage)
    block_output, input_grad = common.output, own_rows(at[0].branch)
    (down_g, out_g), up_g, qkv_g = (common.made[n] for n in "oua")
    mine, theirs = (
        jnp.stack([common.smalls[l][i] for l in range(layers)]).astype(f32) for i in range(2)
    )
    low, high = pick(core, mine, theirs), pick(core, theirs, mine)
    both = low + high
    branch_g = both[:, 1, :piece]
    return (
        block_output,
        input_grad,
        both[:, 0, :piece],
        both[:, 0, COLS // 2 : COLS // 2 + piece],
        qkv_g,
        both[:, 3:5].reshape(layers, -1)[:, : 3 * piece],
        out_g,
        branch_g,
        up_g,
        jnp.concatenate([low[:, 2, :ff_piece], high[:, 2, :ff_piece]], axis=1),
        down_g,
        branch_g,
    )


def solution(mesh):
    rows = P(("shard", "rep"), None)
    vector, matrix = P(None, "shard"), P(None, "shard", None)
    line = P(("shard", "rep"))
    return jax.shard_map(
        body,
        mesh=mesh,
        in_specs=(
            rows, line, line, rows, vector, vector, matrix, vector, matrix, vector,
            matrix, vector, matrix, vector,
        ),
        out_specs=(
            rows, rows, vector, vector, matrix, vector, matrix, vector, matrix, vector,
            matrix, vector,
        ),
        check_vma=False,
    )
```
